32 devices in a mesh: px: 4 (over z), py: 4 (over y, core), lev: 2 (over x).
Axes of the slice: x: 2, y: 2, z: 4, core: 2. Of those that a mesh axis runs over, the one named last changes fastest.
Arguments:
- pressure: float32 [8, 512, 512], P('lev', 'px', 'py'), may hold values from -6 to 6
- wind_east: float32 [8, 512, 512], P('lev', 'px', 'py'), may hold values from -6 to 6
- wind_north: float32 [8, 512, 512], P('lev', 'px', 'py'), may hold values from -6 to 6
- wind_up: float32 [8, 512, 512], P('lev', 'px', 'py'), may hold values from -6 to 6
- stiffness: float32 [8, 512, 512], P('lev', 'px', 'py'), may hold values from 0.3 to 1
- edge_table: int32 [4, 4, 4], replicated, may hold values from 0 to 7
- remap_source: int32 [65536], P(('px', 'py')), may hold values from 0 to 16383
- remap_weight: float32 [65536], P(('px', 'py')), may hold values from 0.25 to 1
- remap_owner: int32 [65536, 1], P(('px', 'py')), may hold values from 0 to 3; in each aligned block of 4096 rows (0 to 4095, 4096 to 8191, ...) at most 2048 rows name the same one
- latlon_cell: int32 [131072], P(('px', 'py')), may hold values from 0 to 2047
Outputs:
- final_pressure: float32 [8, 512, 512], P('lev', 'px', 'py')
- latlon_fields: float32 [4, 8, 32768], P(None, 'lev', ('px', 'py'))
The draws below stay inside these ranges and needn't reach their ends.
Inputs may be any that keep to these rules, and one draw needn't show every extreme that they name: `remap_owner`: among the 4096 entries of one tile no owner is named more than 2048 times, and in every draw some tile names some owner exactly 2048 times.
All inputs are finite; a program needn't handle non-finite values.
Results may differ from the reference program's by a relative error of at most 0.0003.
Values sent between devices are 32-bit elements; how exact they have to be, the bound alone decides.
A program may use at most 64 MiB of HBM per device.

```python
import math
import jax
import jax.numpy as jnp
import numpy as np
from jax import lax

TILE = 128
SUBSTEPS = 4
LV = 8
NX = 512
NY = 512
TILES = 16
ENTRIES = 4096
CELLS = 2048
SLOTS = 2048
N_PX = 4
N_PY = 4


def place_ends(drawn, stream_key, low, top_value):
    place = [jax.random.randint(jax.random.fold_in(stream_key, axis), (), 0, length) for axis, length in enumerate(drawn.shape)]
    main_axis = drawn.shape.index(max(drawn.shape))
    beside = place[:main_axis] + [(place[main_axis] + 1) % drawn.shape[main_axis]] + place[main_axis + 1:]
    return drawn.at[tuple(place)].set(low).at[tuple(beside)].set(top_value)


def steps_of(own_key, shape, pieces, low, largest):
    level, own = 1.0, jax.random.fold_in(own_key, 6)
    for axis_at, shards_of in pieces:
        heights = jnp.exp(jax.random.uniform(jax.random.fold_in(own, axis_at), (shards_of,), jnp.float32, low / len(pieces), largest / len(pieces)))
        level = level * jnp.repeat(heights, shape[axis_at] // shards_of).reshape([-1 if axis == axis_at else 1 for axis in range(len(shape))])
    return level


def shared_out(rng, own, number, rows, count, top, reach, slope):
    order = jax.random.permutation(rng, count)
    heavy_load, usual = shares(count, rows * top, reach, slope, True), shares(count, rows * top, reach, slope, False)
    places = jnp.arange(count)

    def named(sizes, offset_by):
        used = int((sizes > 0).sum())
        fixed = max(1, used // 4)
        shifted = fixed + (places - fixed + offset_by * (used - fixed)) % max(1, count - fixed)
        return jnp.zeros((count,), jnp.int32).at[order[jnp.where(places < fixed, places, shifted)]].set(jnp.asarray(sizes, jnp.int32))

    sizes = jnp.where(number % 4 == 0, named(heavy_load, number // 4), named(usual, number - number // 4 - 1))
    mixed = jax.random.permutation(jax.random.fold_in(own, 3), count)
    donor, taker = mixed[0:count // 2 * 2:2], mixed[1:count // 2 * 2:2]
    room = jnp.minimum(sizes[donor] - 1, reach - sizes[taker]) // 2
    room = jnp.where((donor == order[0]) | (taker == order[0]) | (sizes[taker] == 0), 0, jnp.maximum(room, 0))
    shifted = jax.random.randint(jax.random.fold_in(own, 4), (count // 2,), 0, 1 << 20) % (room + 1)
    sizes = sizes.at[donor].add(-shifted).at[taker].add(shifted)
    labels = jnp.searchsorted(jnp.cumsum(sizes), jnp.arange(rows * top), side="right").astype(jnp.int32)
    grid = labels.reshape(top, rows).T
    grid = grid[jax.random.permutation(jax.random.fold_in(own, 1), rows)]
    offset_by = jax.random.randint(jax.random.fold_in(own, 2), (rows, 1), 0, top)
    return jnp.take_along_axis(grid, (jnp.arange(top)[None, :] + offset_by) % top, axis=1)


def shares(count, total, limit, skew, full):
    weights = [(1 << 20) // math.isqrt(standing ** skew) + 1 for standing in range(1, count + 1)]
    largest = limit if full else min(limit, max(-(-total // count), total * weights[0] // sum(weights)))
    least = 1 if total - largest >= count - 1 else 0
    given, surplus = [largest] + [least] * (count - 1), total - largest - least * (count - 1)
    while surplus > 0:
        candidates = [i for i in range(1, count) if given[i] < largest] or [i for i in range(1, count) if given[i] < limit]
        pool, left = sum([weights[i] for i in candidates]), surplus
        for i in candidates:
            addition = min(limit - given[i], max(1, left * weights[i] // pool), surplus)
            given[i] = given[i] + addition
            surplus = surplus - addition
    return np.array(given)


def gaussian(key, shape, spread, bound, pieces=(), kind=jnp.bfloat16):
    drawn = jax.random.normal(key, shape, jnp.float32) * spread
    if len(pieces) > 0:
        drawn = steps_of(key, shape, pieces, -0.22, 0.18) * drawn
    return jnp.clip(drawn, min=-bound, max=bound).astype(kind)


def setup_inputs(seed: int = 0) -> dict:
    key_list = jax.random.split(jax.random.key(seed), 11)
    pressure = gaussian(key_list[0], (LV, NX, NY), 1.0, 6.0, ((0, 2), (1, 4), (2, 4)), jnp.float32)
    wind_east = gaussian(key_list[1], (LV, NX, NY), 1.0, 6.0, ((0, 2), (1, 4), (2, 4)), jnp.float32)
    wind_north = gaussian(key_list[2], (LV, NX, NY), 1.0, 6.0, ((0, 2), (1, 4), (2, 4)), jnp.float32)
    wind_up = gaussian(key_list[3], (LV, NX, NY), 1.0, 6.0, ((0, 2), (1, 4), (2, 4)), jnp.float32)
    stiffness = jnp.clip(jnp.exp(math.log(1.0) - 1.2039728 * jax.random.uniform(key_list[4], (LV, NX, NY), jnp.float32) ** steps_of(key_list[4], (LV, NX, NY), ((0, 2), (1, 4), (2, 4)), -0.2, 0.2)), 0.3, 1.0)
    edge_table = place_ends(jax.random.randint(key_list[5], (NX // TILE, NY // TILE, 4), 0, 8), jax.random.fold_in(key_list[5], 1), 0, 7).astype(jnp.int32)
    remap_source = place_ends(jax.random.randint(key_list[6], (TILES * ENTRIES,), 0, TILE * TILE), jax.random.fold_in(key_list[6], 1), 0, (TILE * TILE) - 1).astype(jnp.int32)
    remap_weight = jnp.clip(0.25 + 0.75 * jax.random.uniform(key_list[7], (TILES * ENTRIES,), jnp.float32) ** steps_of(key_list[7], (TILES * ENTRIES,), ((0, 16),), -0.2, 0.2), 0.25, 1.0)
    remap_owner_keys = jax.random.split(jax.random.fold_in(key_list[8], 1), (TILES * ENTRIES) // ENTRIES)
    remap_owner_turns = jax.random.permutation(jax.random.fold_in(key_list[8], 3), (TILES * ENTRIES) // ENTRIES)
    remap_owner = jax.vmap(lambda own, number: shared_out(jax.random.fold_in(key_list[8], 2), own, number, ENTRIES, N_PX, 1, SLOTS, 2))(remap_owner_keys, remap_owner_turns).reshape((TILES * ENTRIES, 1))
    latlon_cell = place_ends(jax.random.randint(key_list[9], (TILES * N_PX * SLOTS,), 0, CELLS), jax.random.fold_in(key_list[9], 1), 0, CELLS - 1).astype(jnp.int32)
    return dict(pressure=pressure, wind_east=wind_east, wind_north=wind_north, wind_up=wind_up, stiffness=stiffness, edge_table=edge_table, remap_source=remap_source, remap_weight=remap_weight, remap_owner=remap_owner, latlon_cell=latlon_cell)


horiz_coef = 0.45
vert_coef = 0.3
roll_plan = ((1, 2), (1, 3), (-1, 2), (-1, 3))


def rim_stack(field):
    blocks = field.reshape(LV, N_PX, TILE, N_PY, TILE)
    west_rim = blocks[:, :, 0, :, :]
    east_rim = blocks[:, :, -1, :, :]
    south_rim = jnp.transpose(blocks[:, :, :, :, 0], (0, 1, 3, 2))
    north_rim = jnp.transpose(blocks[:, :, :, :, -1], (0, 1, 3, 2))
    return jnp.stack([west_rim, south_rim, east_rim, north_rim])


def turn_pair(first, second, quarter_turns):
    new_first = jnp.where(quarter_turns == 0, first, jnp.where(quarter_turns == 1, -second, jnp.where(quarter_turns == 2, -first, second)))
    new_second = jnp.where(quarter_turns == 0, second, jnp.where(quarter_turns == 1, first, jnp.where(quarter_turns == 2, -second, -first)))
    return new_first, new_second


def ghost_sets(fields, edge_table, vector):
    stacks = [rim_stack(field) for field in fields]
    result = []
    for facing in range(4):
        amount, axis_num = roll_plan[facing]
        edge_code = edge_table[:, :, facing]
        quarter_turns = edge_code % 4
        flipped = edge_code // 4
        wanted = (facing + 2 + quarter_turns) % 4
        picked = []
        for stacked in stacks:
            rolled = jnp.roll(stacked, amount, axis=axis_num)
            chosen = rolled[0]
            for option in range(1, 4):
                chosen = jnp.where(wanted[None, :, :, None] == option, rolled[option], chosen)
            chosen = jnp.where(flipped[None, :, :, None] == 1, chosen[..., ::-1], chosen)
            picked.append(chosen)
        if vector:
            picked = list(turn_pair(picked[0], picked[1], quarter_turns[None, :, :, None]))
        result.append(picked)
    return result


def spreads(field, ghosts):
    west_ghost, south_ghost, east_ghost, north_ghost = ghosts
    blocks = field.reshape(LV, N_PX, TILE, N_PY, TILE)
    east_val = jnp.concatenate([blocks[:, :, 1:], east_ghost[:, :, None]], axis=2)
    west_val = jnp.concatenate([west_ghost[:, :, None], blocks[:, :, :-1]], axis=2)
    north_val = jnp.concatenate([blocks[..., 1:], jnp.transpose(north_ghost, (0, 1, 3, 2))[..., None]], axis=4)
    south_val = jnp.concatenate([jnp.transpose(south_ghost, (0, 1, 3, 2))[..., None], blocks[..., :-1]], axis=4)
    return (east_val - west_val).reshape(LV, NX, NY), (north_val - south_val).reshape(LV, NX, NY)


def ranking(owner_row):
    onehot = (owner_row[:, None] == jnp.arange(N_PX, dtype=jnp.int32)[None, :]).astype(jnp.int32)
    counts = jnp.cumsum(onehot, axis=0)
    return jnp.sum(counts * onehot, axis=1) - 1


def pick_columns(column_block, sources):
    return column_block[:, :, sources]


def reference(pressure, wind_east, wind_north, wind_up, stiffness, edge_table, remap_source, remap_weight, remap_owner, latlon_cell):
    level_pos = lax.broadcasted_iota(jnp.int32, pressure.shape, 0)
    summit_mask = level_pos == LV - 1
    zero_layer = jnp.zeros((1, NX, NY), jnp.float32)
    for substep in range(SUBSTEPS):
        press_ghosts = ghost_sets([pressure], edge_table, False)
        east_diff, north_diff = spreads(pressure, [ghost[0] for ghost in press_ghosts])
        wind_east = wind_east - horiz_coef * east_diff
        wind_north = wind_north - horiz_coef * north_diff
        press_up = jnp.concatenate([pressure[1:], zero_layer], axis=0)
        wind_up = jnp.where(summit_mask, 0.0, wind_up - vert_coef * (press_up - pressure))
        wind_low = jnp.concatenate([zero_layer, wind_up[:-1]], axis=0)
        wind_ghosts = ghost_sets([wind_east, wind_north], edge_table, True)
        east_flow = spreads(wind_east, [ghost[0] for ghost in wind_ghosts])[0]
        north_flow = spreads(wind_north, [ghost[1] for ghost in wind_ghosts])[1]
        pressure = pressure - stiffness * (horiz_coef * (east_flow + north_flow) + vert_coef * (wind_up - wind_low))
    fields = jnp.stack([pressure, wind_east, wind_north, wind_up])
    columns = fields.reshape(4, LV, N_PX, TILE, N_PY, TILE).transpose(2, 4, 0, 1, 3, 5).reshape(TILES, 4, LV, TILE * TILE)
    sources = remap_source.reshape(TILES, ENTRIES)
    weights = remap_weight.reshape(TILES, ENTRIES)
    owners = remap_owner[:, 0].reshape(TILES, ENTRIES)
    payload = jax.vmap(pick_columns)(columns, sources) * weights[:, None, None, :]
    slot_rank = lax.map(ranking, owners)
    tile_index = jnp.arange(TILES, dtype=jnp.int32)[:, None]
    tile_first = tile_index // N_PY
    tile_second = tile_index % N_PY
    cell_table = latlon_cell.reshape(N_PX, N_PY, N_PX, SLOTS)
    target_cell = cell_table[owners, tile_second, tile_first, slot_rank]
    destination = (owners * N_PY + tile_second) * CELLS + target_cell
    flat_values = payload.transpose(1, 2, 0, 3).reshape(4, LV, TILES * ENTRIES)
    latlon_fields = jnp.zeros((4, LV, TILES * CELLS), jnp.float32).at[:, :, destination.reshape(-1)].add(flat_values)
    return pressure, latlon_fields
```

```python
import functools

import jax
import jax.numpy as jnp
from jax import lax
from jax.experimental import pallas as pl
from jax.experimental.pallas import tpu as pltpu
from jax.sharding import PartitionSpec as P

SUBSTEPS = 4
A = 0.45
B = 0.3
LANES = 128
BLOCK = 256
MESH = pl.DeviceIdType.MESH


def iota(shape, dim):
    return lax.broadcasted_iota(jnp.int32, shape, dim)


def parts2(x):
    high = x.astype(jnp.bfloat16)
    return high, (x - high.astype(jnp.float32)).astype(jnp.bfloat16)


def dot_nt(a, b):
    return lax.dot_general(a, b, (((1,), (1,)), ((), ())), preferred_element_type=jnp.float32)


def opposite(s):
    return (s + 2) & 3


SHIFT = ((-1, 0), (0, -1), (1, 0), (0, 1))
DIAGONAL = ((0, 1), (0, 3), (2, 1), (2, 3))


def whole_kernel(
    sizes,
    edges,
    p_in,
    we_in,
    wn_in,
    wu_in,
    st_in,
    owner_in,
    source_in,
    weight_in,
    cell_in,
    p,
    latlon,
    we,
    wn,
    wu,
    st,
    owner,
    source,
    weight,
    cell,
    table,
    near_send,
    near_recv,
    diag_send,
    diag_recv,
    far_send,
    far_recv,
    own_relay,
    level_send,
    level_recv,
    plane_send,
    plane_recv,
    wu_below,
    flipped_cols,
    ghost_rows,
    p_strips,
    w_strips,
    st_strips,
    slot_source,
    slot_weight,
    split,
    payload,
    arrived,
    total,
    in_sems,
    near_sems,
    diag_sems,
    far_sems,
    level_sems,
    plane_sems,
    wub_sems,
    give_sem,
    take_sem,
):
    n_px, n_py, n_lev = sizes
    levels, tile, _ = p.shape
    last = tile - 1
    loads = [
        pltpu.make_async_copy(src, dst, in_sems.at[k])
        for k, (src, dst) in enumerate(
            (
                (p_in, p),
                (we_in, we),
                (wn_in, wn),
                (st_in, st),
                (wu_in, wu),
                (owner_in, owner),
                (source_in, source),
                (weight_in, weight),
                (cell_in, cell),
            )
        )
    ]
    for load in loads:
        load.start()
    ix, iy, iz = lax.axis_index("px"), lax.axis_index("py"), lax.axis_index("lev")
    has_above, has_below = iz < n_lev - 1, iz > 0

    def place(dx, dy):
        return lax.rem(ix + dx + 2 * n_px, n_px), lax.rem(iy + dy + 2 * n_py, n_py)

    def at(dx, dy):
        x, y = place(dx, dy)
        return {"px": x, "py": y}

    others = {(d, 0) for d in range(1, n_px)}
    for dx, dy in ((0, 1), (0, -1), (0, 2), (0, -2), (1, 1), (1, -1), (-1, 1), (-1, -1)):
        others.add((dx % n_px, dy % n_py))
    beside = sorted(o for o in others if o[1])

    barrier = pltpu.get_barrier_semaphore()
    for dx, dy in beside:
        pl.semaphore_signal(barrier, inc=1, device_id=at(dx, dy), device_id_type=MESH)

    def greet(d, carry):
        pl.semaphore_signal(barrier, inc=1, device_id={"px": lax.rem(ix + d, n_px)}, device_id_type=MESH)
        return carry

    lax.fori_loop(1, n_px, greet, 0)

    @pl.when(has_above)
    def _():
        pl.semaphore_signal(barrier, inc=1, device_id={"lev": iz + 1}, device_id_type=MESH)

    @pl.when(has_below)
    def _():
        pl.semaphore_signal(barrier, inc=1, device_id={"lev": iz - 1}, device_id_type=MESH)

    def remote(src, dst, sems, index, device):
        return pltpu.make_async_remote_copy(
            src_ref=src,
            dst_ref=dst,
            send_sem=sems.at[(0,) + index],
            recv_sem=sems.at[(1,) + index],
            device_id=device,
            device_id_type=MESH,
        )

    def near_copy(t, s):
        dx, dy = SHIFT[s]
        return remote(near_send.at[t, s], near_recv.at[t, s], near_sems, (t, s), at(-dx, -dy))

    def diag_copy(t, k):
        (ax, ay), (bx, by) = SHIFT[DIAGONAL[k][0]], SHIFT[DIAGONAL[k][1]]
        return remote(diag_send.at[t, k], diag_recv.at[t, k], diag_sems, (t, k), at(-ax - bx, -ay - by))

    def far_copy(t, s):
        dx, dy = SHIFT[s]
        return remote(far_send.at[t, s], far_recv.at[t, s], far_sems, (t, s), at(-2 * dx, -2 * dy))

    def level_copy(t, up):
        return remote(
            level_send.at[t, up],
            level_recv.at[t, up],
            level_sems,
            (t, up),
            {"lev": iz + 1 if up else iz - 1},
        )

    def plane_copy(t, up, first=False):
        src = p_in.at[levels - 1 if up else 0] if first else plane_send.at[t, up]
        return remote(src, plane_recv.at[t, up], plane_sems, (t, up), {"lev": iz + 1 if up else iz - 1})

    def wub_copy():
        return remote(wu_in.at[levels - 1], wu_below, wub_sems, (0,), {"lev": iz + 1})

    row, lane = iota((tile, tile), 0), iota((tile, tile), 1)
    strip_row, strip_lane = iota((2 * levels, tile), 0), iota((2 * levels, tile), 1)
    outer = strip_row < levels

    def d_rows(f):
        return jnp.where(row == last, 0.0, pltpu.roll(f, last, 0)) - jnp.where(
            row == 0, 0.0, pltpu.roll(f, 1, 0)
        )

    def d_lanes(f):
        return jnp.where(lane == last, 0.0, pltpu.roll(f, last, 1)) - jnp.where(
            lane == 0, 0.0, pltpu.roll(f, 1, 1)
        )

    def columns(deep, shallow):
        packed = jnp.zeros((tile, tile), jnp.float32)
        for j, f in enumerate(deep):
            packed = jnp.where((lane >> 2) == j, pltpu.roll(f, 4 * j + 2, 1), packed)
        base = 4 * len(deep)
        for j, f in enumerate(shallow):
            packed = jnp.where((lane >> 1) == base // 2 + j, pltpu.roll(f, base + 2 * j + 1, 1), packed)
        flipped_cols[...] = packed.T

    def column(k):
        return flipped_cols[pl.ds(k, levels, stride=4), :]

    def rim_column(k):
        return flipped_cols[pl.ds(4 * levels + k, levels, stride=2), :]

    def take_strips():
        columns([p[j] for j in range(levels)], [wn[j] for j in range(levels)])
        for s, (a, b) in ((0, (0, 1)), (2, (last, last - 1))):
            p_strips[s, :levels] = p[:, a, :]
            p_strips[s, levels:] = p[:, b, :]
            w_strips[s, :levels] = we[:, a, :]
        for s, (a, b, c) in ((1, (2, 3, 1)), (3, (1, 0, 0))):
            p_strips[s, :levels] = column(a)
            p_strips[s, levels:] = column(b)
            w_strips[s, :levels] = rim_column(c)

    def code(x, y, s):
        c = edges[x, y, s]
        return c & 3, c >> 2

    def wanted(s, turn):
        return (s + 2 + turn) & 3

    def sign(s, turn):
        plus = ((turn + 1) & 3) < 2 if s % 2 == 0 else turn < 2
        return jnp.where(plus, 1.0, -1.0) * (1.0 if s < 2 else -1.0)

    def rim_sign(w):
        return jnp.where(w < 2, 1.0, -1.0) if not isinstance(w, int) else (1.0 if w < 2 else -1.0)

    near_plan = []
    for s in range(4):
        dx, dy = SHIFT[s]
        turn, flip = code(*place(-dx, -dy), s)
        near_plan.append((flip * 4 + wanted(s, turn), sign(s, turn)))

    def relay_plan(s, w, ax, ay):
        turn_a, flip_a = code(*place(ax, ay), s)
        turn_b, flip_b = code(*place(ax + SHIFT[s][0], ay + SHIFT[s][1]), w)
        return (flip_a ^ flip_b) * 4 + wanted(w, turn_b), sign(s, turn_a) * rim_sign(w)

    def relay_to(s, w):
        return relay_plan(s, w, -SHIFT[s][0] - SHIFT[w][0], -SHIFT[s][1] - SHIFT[w][1])

    diag_plan = [(relay_to(a, b), relay_to(b, a)) for a, b in DIAGONAL]
    far_plan = [relay_to(s, s) for s in range(4)]
    own_plan = [relay_to(s, opposite(s)) for s in range(4)]
    mine = [wanted(s, code(ix, iy, s)[0]) for s in range(4)]

    def relayed(t, s):
        found = own_relay[s]
        for k, (a, b) in enumerate(DIAGONAL):
            if s == a:
                found = jnp.where(mine[s] == b, diag_recv[t, k, :levels], found)
            if s == b:
                found = jnp.where(mine[s] == a, diag_recv[t, k, levels:], found)
        return jnp.where(mine[s] == s, far_recv[t, s], found)

    def send_rims(t):
        strips = [p_strips[s] for s in range(4)]
        rims = []
        for s in range(4):
            turned = A * pltpu.roll(strips[s], levels, 0)
            rims.append(jnp.where(outer, w_strips[s] - rim_sign(s) * turned, turned))
        for s in range(4):
            table[s] = rims[s]
            table[4 + s] = jnp.take_along_axis(rims[s], last - strip_lane, axis=1)
        for s in range(4):
            k, sgn = near_plan[s]
            rim = table[k]
            near_send[t, s] = jnp.where(outer, sgn * rim, rim)
            near_copy(t, s).start()
        for k in range(4):
            for half in range(2):
                which, sgn = diag_plan[k][half]
                diag_send[t, k, half * levels : (half + 1) * levels] = sgn * table[which, levels:]
            diag_copy(t, k).start()
        for s in range(4):
            k, sgn = far_plan[s]
            far_send[t, s] = sgn * table[k, levels:]
            far_copy(t, s).start()
        for s in range(4):
            k, sgn = own_plan[s]
            own_relay[s] = sgn * table[k, levels:]
            for up, level in ((1, levels - 1), (0, 0)):
                level_send[t, up, 2 * s : 2 * s + 2] = p_strips[s, pl.ds(level, 2, stride=levels), :]

        @pl.when(has_above)
        def _():
            level_copy(t, 1).start()

        @pl.when(has_below)
        def _():
            level_copy(t, 0).start()

    def corners(s, low, high):
        found = jnp.zeros((2 * levels, tile), jnp.float32)
        for depth in range(2):
            start = depth if s < 2 else last - depth
            for e in range(2):
                for pair, end in ((low, e), (high, last - e)):
                    moved = pltpu.roll(pair[depth ^ e], (end - start) % tile, 1) if end != start else pair[depth ^ e]
                    here = (strip_lane == end) & (outer if depth == 0 else jnp.logical_not(outer))
                    found = jnp.where(here, moved, found)
        return found

    def next_strips(t):
        for s in range(4):
            near_copy(t, s).wait_recv()
        for k in range(4):
            diag_copy(t, k).wait_recv()
        for s in range(4):
            far_copy(t, s).wait_recv()

        @pl.when(has_above)
        def _():
            level_copy(t, 0).wait_recv()

        @pl.when(has_below)
        def _():
            level_copy(t, 1).wait_recv()

        zero = jnp.zeros((levels, tile), jnp.float32)
        ghosts = []
        for s in range(4):
            ghosts.append(near_recv[t, s] + jnp.concatenate([relayed(t, s), zero], axis=0))
        pairs = [(g, pltpu.roll(g, levels, 0)) for g in ghosts]
        for s in range(4):
            low, high = (pairs[1], pairs[3]) if s % 2 == 0 else (pairs[0], pairs[2])
            across = jnp.zeros((2 * levels, tile), jnp.float32)
            for depth in range(2):
                below, above = level_recv[t, 1], level_recv[t, 0]
                k = 2 * s + depth
                across = jnp.where(strip_row == depth * levels, below[k : k + 1], across)
                across = across + jnp.where(strip_row == (depth + 1) * levels - 1, above[k : k + 1], 0.0)
            p_strips[s] = p_strips[s] + st_strips[s] * (
                A * (ghosts[s] + corners(s, low, high)) + (B * B) * across
            )
            w_strips[s] = jnp.where(outer, w_strips[s] + rim_sign(s) * pairs[s][1], 0.0)

    def give_copy(o):
        return pltpu.make_async_remote_copy(
            src_ref=payload.at[o],
            dst_ref=arrived.at[ix],
            send_sem=give_sem.at[o],
            recv_sem=take_sem.at[ix],
            device_id={"px": o},
            device_id_type=MESH,
        )

    def got(o):
        return pltpu.make_async_remote_copy(
            src_ref=payload.at[o],
            dst_ref=arrived.at[o],
            send_sem=give_sem.at[o],
            recv_sem=take_sem.at[o],
            device_id={"px": o},
            device_id_type=MESH,
        )

    w_strips[...] = jnp.zeros(w_strips.shape, jnp.float32)
    ghost_rows[...] = jnp.zeros((tile, tile), jnp.float32)

    @pl.when(jnp.logical_not(has_below))
    def _():
        wu_below[...] = jnp.zeros((tile, tile), jnp.float32)
        level_recv[:, 1] = jnp.zeros((SUBSTEPS, 8, tile), jnp.float32)

    @pl.when(jnp.logical_not(has_above))
    def _():
        level_recv[:, 0] = jnp.zeros((SUBSTEPS, 8, tile), jnp.float32)

    for load in loads[:3]:
        load.wait()
    take_strips()
    pl.semaphore_wait(
        barrier, n_px - 1 + len(beside) + has_above.astype(jnp.int32) + has_below.astype(jnp.int32)
    )
    send_rims(0)

    @pl.when(has_above)
    def _():
        wub_copy().start()
        plane_copy(0, 1, True).start()

    @pl.when(has_below)
    def _():
        plane_copy(0, 0, True).start()

    for load in loads[3:]:
        load.wait()
    columns([st[j] for j in range(levels)], [])
    for s, (a, b) in ((0, (0, 1)), (2, (last, last - 1))):
        st_strips[s, :levels] = st[:, a, :]
        st_strips[s, levels:] = st[:, b, :]
    for s, (a, b) in ((1, (2, 3)), (3, (1, 0))):
        st_strips[s, :levels] = column(a)
        st_strips[s, levels:] = column(b)
    slot_count = payload.shape[2]
    find_slots(n_px, slot_count, owner, source, weight, slot_source, slot_weight)

    def ahead(d):
        return lax.rem(ix + d + 1, n_px)

    def substep(t, carry):
        for j in range(levels):
            we[j] = we[j] - A * d_rows(p[j])
            wn[j] = wn[j] - A * d_lanes(p[j])
        for j in range(levels - 1):
            wu[j] = wu[j] - B * (p[j + 1] - p[j])

        @pl.when(has_above)
        def _():
            wu[levels - 1] = wu[levels - 1] + B * p[levels - 1]

        @pl.when(jnp.logical_not(has_above))
        def _():
            wu[levels - 1] = jnp.zeros((tile, tile), jnp.float32)

        for j in range(1, levels):
            p[j] = p[j] - st[j] * (A * (d_rows(we[j]) + d_lanes(wn[j])) + B * (wu[j] - wu[j - 1]))

        @pl.when(has_below & (t == 0))
        def _():
            wub_copy().wait_recv()

        @pl.when(has_below)
        def _():
            wu_below[...] = wu_below[...] - B * p[0]

        p[0] = p[0] - st[0] * (A * (d_rows(we[0]) + d_lanes(wn[0])) + B * (wu[0] - wu_below[...]))
        take_strips()
        next_strips(t)

        @pl.when(t < SUBSTEPS - 1)
        def _():
            send_rims(t + 1)

        @pl.when(has_above)
        def _():
            plane_copy(t, 0).wait_recv()
            wu[levels - 1] = wu[levels - 1] - B * plane_recv[t, 0]
            p[levels - 1] = p[levels - 1] + (B * B) * (st[levels - 1] * plane_recv[t, 0])

        @pl.when(has_below)
        def _():
            plane_copy(t, 1).wait_recv()
            wu_below[...] = wu_below[...] + B * plane_recv[t, 1]
            p[0] = p[0] + (B * B) * (st[0] * plane_recv[t, 1])

        for s, (a, b) in ((0, (0, 1)), (2, (last, last - 1))):
            p[:, a, :] = p_strips[s, :levels]
            p[:, b, :] = p_strips[s, levels:]
            we[:, a, :] = w_strips[s, :levels]
        for k, (s, half) in enumerate(((3, 1), (3, 0), (1, 0), (1, 1))):
            ghost_rows[pl.ds(k, levels, stride=4), :] = p_strips[s, half * levels : (half + 1) * levels]
        for k, s in enumerate((3, 1)):
            ghost_rows[pl.ds(4 * levels + k, levels, stride=2), :] = w_strips[s, :levels]
        turned = ghost_rows[...].T
        rim = (lane == 0) | (lane == last)
        band = (lane <= 1) | (lane >= last - 1)
        for j in range(levels):
            p[j] = jnp.where(band, pltpu.roll(turned, (tile - 4 * j - 2) % tile, 1), p[j])
            wn[j] = jnp.where(rim, pltpu.roll(turned, (tile - 4 * levels - 2 * j - 1) % tile, 1), wn[j])

        @pl.when((t < SUBSTEPS - 1) & has_above)
        def _():
            plane_send[t + 1, 1] = p[levels - 1]
            plane_copy(t + 1, 1).start()

        @pl.when((t < SUBSTEPS - 1) & has_below)
        def _():
            plane_send[t + 1, 0] = p[0]
            plane_copy(t + 1, 0).start()

        return carry

    lax.fori_loop(0, SUBSTEPS, substep, 0)

    for q, field in enumerate((p, we, wn, wu)):
        split_field(split, field, q)

    def hand_out(d, carry):
        pick(split, slot_source, slot_weight, payload, ahead(d), ahead(d), 0, 4)
        give_copy(ahead(d)).start()
        return carry

    lax.fori_loop(0, n_px - 1, hand_out, 0)
    pick(split, slot_source, slot_weight, arrived, ix, ix, 0, 4)
    total[...] = jnp.zeros(total.shape, jnp.float32)
    land(arrived, cell, ix, total)

    def bring_in(d, carry):
        o = lax.rem(ix + n_px - d - 1, n_px)
        got(o).wait_recv()
        land(arrived, cell, o, total)
        return carry

    lax.fori_loop(0, n_px - 1, bring_in, 0)
    count, groups = 4 * levels, latlon.shape[2] // BLOCK
    for g in range(groups):
        both = total[g * count : (g + 1) * count] + total[(groups + g) * count : (groups + g + 1) * count]
        for q in range(4):
            latlon[q, :, g * BLOCK : (g + 1) * BLOCK] = both[q * levels : (q + 1) * levels]

    def drain(t, carry):
        for s in range(4):
            near_copy(t, s).wait_send()
            diag_copy(t, s).wait_send()
            far_copy(t, s).wait_send()

        @pl.when(has_above)
        def _():
            level_copy(t, 1).wait_send()
            plane_copy(t, 1).wait_send()

        @pl.when(has_below)
        def _():
            level_copy(t, 0).wait_send()
            plane_copy(t, 0).wait_send()

        return carry

    lax.fori_loop(0, SUBSTEPS, drain, 0)

    @pl.when(has_above)
    def _():
        wub_copy().wait_send()

    def sent(d, carry):
        give_copy(ahead(d)).wait_send()
        return carry

    lax.fori_loop(0, n_px - 1, sent, 0)


def find_slots(owner_count, slot_count, owner, source, weight, slot_source, slot_weight):
    rows = owner.shape[0]
    slot_rows = slot_source.shape[0]
    names = owner[...]
    up_to = (iota((LANES, LANES), 0) <= iota((LANES, LANES), 1)).astype(jnp.bfloat16)
    ones = jnp.ones((LANES, LANES), jnp.bfloat16)
    before = (iota((rows, rows), 0) > iota((rows, rows), 1)).astype(jnp.bfloat16)

    def count(o, rank):
        named = names == o
        hot = named.astype(jnp.float32).astype(jnp.bfloat16)
        within = jnp.dot(hot, up_to, preferred_element_type=jnp.float32)
        total = jnp.dot(hot, ones, preferred_element_type=jnp.float32).astype(jnp.bfloat16)
        earlier = jnp.dot(before, total, preferred_element_type=jnp.float32)
        return jnp.where(named, within + earlier - 1.0, rank)

    rank = lax.fori_loop(0, owner_count, count, jnp.zeros(names.shape, jnp.float32))
    slot = names * slot_count + rank.astype(jnp.int32)
    slot_high, slot_low = slot >> 7, slot & (LANES - 1)
    src = source[...]
    w = weight[...]
    w1 = w.astype(jnp.bfloat16).astype(jnp.float32)
    w2 = (w - w1).astype(jnp.bfloat16).astype(jnp.float32)
    w3 = w - w1 - w2
    pieces = [(src >> 7).astype(jnp.float32), (src & (LANES - 1)).astype(jnp.float32), w1, w2, w3]
    high_place, low_place = iota((slot_rows, LANES), 0), iota((LANES, LANES), 0)
    total = jnp.zeros((len(pieces) * slot_rows, LANES), jnp.float32)
    for r in range(rows):
        here = high_place == slot_high[r : r + 1]
        left = jnp.concatenate([jnp.where(here, piece[r : r + 1], 0.0) for piece in pieces], axis=0)
        right = jnp.where(low_place == slot_low[r : r + 1], 1.0, 0.0)
        total += dot_nt(left.astype(jnp.bfloat16), right.astype(jnp.bfloat16))
    part = [total[k * slot_rows : (k + 1) * slot_rows] for k in range(len(pieces))]
    slot_source[...] = (part[0] * LANES + part[1]).astype(jnp.int32)
    slot_weight[...] = part[2] + part[3] + part[4]


def split_field(split, field, q):
    levels, tile, _ = field.shape
    half = tile // 2
    for l in range(levels):
        h, d = parts2(field[l].T)
        at = slice((q * levels + l) * half, (q * levels + l + 1) * half)
        for k, part in enumerate((h[:half], h[half:], d[:half], d[half:])):
            split[at, k * tile : (k + 1) * tile] = part


def pick(split, slot_source, slot_weight, dst, place, o, first, end):
    rows, slot_count = dst.shape[1:]
    tile = split.shape[1] // 4
    half = tile // 2
    width = min(BLOCK, slot_count)
    pieces = width // LANES
    quarter = rows // 4
    at = slice(first * quarter * half, end * quarter * half)

    def joined(ref, b):
        row = o * (slot_count // LANES) + b * pieces
        return jnp.concatenate([ref[pl.ds(row + k, 1), :] for k in range(pieces)], axis=1)

    def step(b, carry):
        src, w = joined(slot_source, b), joined(slot_weight, b)
        x, y = src >> 7, src & (tile - 1)
        line = x + jnp.where(y >= half, tile, 0)
        hot = jnp.where(iota((2 * tile, width), 0) == line, 1.0, 0.0).astype(jnp.bfloat16)
        picked = jnp.dot(
            split[at, :], jnp.concatenate([hot, hot], axis=0), preferred_element_type=jnp.float32
        )
        mask = jnp.where(iota((half, width), 0) == (y & (half - 1)), w, 0.0)
        dst[place, first * quarter : end * quarter, pl.ds(pl.multiple_of(b * width, width), width)] = jnp.sum(
            picked.reshape((end - first) * quarter, half, width) * mask[None], axis=1
        )
        return carry

    lax.fori_loop(0, slot_count // width, step, 0)


def land(arrived, cell, o, total):
    count, slot_count = arrived.shape[1:]
    groups = total.shape[0] // (2 * count)
    width = min(4 * BLOCK, slot_count)

    def step(b, carry):
        at = pl.ds(pl.multiple_of(b * width, width), width)
        row = o * (slot_count // LANES) + b * (width // LANES)
        c = jnp.concatenate([cell[pl.ds(row + k, 1), :] for k in range(width // LANES)], axis=1)
        values = arrived[o, :, at]
        h = values.astype(jnp.bfloat16).astype(jnp.float32)
        group = c >> 8
        spread = [jnp.where(group == g, h, 0.0) for g in range(groups)]
        spread += [jnp.where(group == g, values - h, 0.0) for g in range(groups)]
        hot = jnp.where(iota((BLOCK, width), 0) == (c & (BLOCK - 1)), 1.0, 0.0)
        total[...] += dot_nt(jnp.concatenate(spread, axis=0).astype(jnp.bfloat16), hot.astype(jnp.bfloat16))
        return carry

    lax.fori_loop(0, slot_count // width, step, 0)


def per_device(
    sizes,
    pressure,
    wind_east,
    wind_north,
    wind_up,
    stiffness,
    edge_table,
    remap_source,
    remap_weight,
    remap_owner,
    latlon_cell,
):
    levels, tile, _ = pressure.shape
    owner_count = sizes[0]
    slots = latlon_cell.shape[0]
    slot_count = slots // owner_count
    cell_count = tile * tile // 8
    count = 4 * levels
    rows = remap_source.shape[0] // LANES
    f32, i32 = jnp.float32, jnp.int32
    n = SUBSTEPS
    field = pltpu.VMEM(pressure.shape, f32)
    plane = pltpu.VMEM((tile, tile), f32)
    dma = pltpu.SemaphoreType.DMA
    in_vmem = pl.BlockSpec(memory_space=pltpu.VMEM)
    return pl.pallas_call(
        functools.partial(whole_kernel, sizes),
        out_shape=[
            jax.ShapeDtypeStruct(pressure.shape, f32),
            jax.ShapeDtypeStruct((4, levels, cell_count), f32),
        ],
        in_specs=[pl.BlockSpec(memory_space=pltpu.SMEM)] + [pl.BlockSpec(memory_space=pl.ANY)] * 9,
        out_specs=[in_vmem] * 2,
        scratch_shapes=[
            field,
            field,
            field,
            field,
            pltpu.VMEM((rows, LANES), i32),
            pltpu.VMEM((rows, LANES), i32),
            pltpu.VMEM((rows, LANES), f32),
            pltpu.VMEM((slots // LANES, LANES), i32),
            pltpu.VMEM((8, 2 * levels, tile), f32),
            pltpu.VMEM((n, 4, 2 * levels, tile), f32),
            pltpu.VMEM((n, 4, 2 * levels, tile), f32),
            pltpu.VMEM((n, 4, 2 * levels, tile), f32),
            pltpu.VMEM((n, 4, 2 * levels, tile), f32),
            pltpu.VMEM((n, 4, levels, tile), f32),
            pltpu.VMEM((n, 4, levels, tile), f32),
            pltpu.VMEM((4, levels, tile), f32),
            pltpu.VMEM((n, 2, 8, tile), f32),
            pltpu.VMEM((n, 2, 8, tile), f32),
            pltpu.VMEM((n, 2, tile, tile), f32),
            pltpu.VMEM((n, 2, tile, tile), f32),
            plane,
            plane,
            plane,
            pltpu.VMEM((4, 2 * levels, tile), f32),
            pltpu.VMEM((4, 2 * levels, tile), f32),
            pltpu.VMEM((4, 2 * levels, tile), f32),
            pltpu.VMEM((slots // LANES, LANES), i32),
            pltpu.VMEM((slots // LANES, LANES), f32),
            pltpu.VMEM((count * tile // 2, 4 * tile), jnp.bfloat16),
            pltpu.VMEM((owner_count, count, slot_count), f32),
            pltpu.VMEM((owner_count, count, slot_count), f32),
            pltpu.VMEM((2 * count * (cell_count // BLOCK), BLOCK), f32),
            dma((9,)),
            dma((2, n, 4)),
            dma((2, n, 4)),
            dma((2, n, 4)),
            dma((2, n, 2)),
            dma((2, n, 2)),
            dma((2, 1)),
            dma((owner_count,)),
            dma((owner_count,)),
        ],
        compiler_params=pltpu.CompilerParams(
            collective_id=0, has_side_effects=True, vmem_limit_bytes=60 * 2**20
        ),
    )(
        edge_table,
        pressure,
        wind_east,
        wind_north,
        wind_up,
        stiffness,
        remap_owner.reshape(rows, LANES),
        remap_source.reshape(rows, LANES),
        remap_weight.reshape(rows, LANES),
        latlon_cell.reshape(slots // LANES, LANES),
    )


def solution(mesh):
    field = P("lev", "px", "py")
    entries = P(("px", "py"))
    sizes = (mesh.shape["px"], mesh.shape["py"], mesh.shape["lev"])
    return jax.shard_map(
        functools.partial(per_device, sizes),
        mesh=mesh,
        in_specs=(field,) * 5 + (P(), entries, entries, P(("px", "py"), None), entries),
        out_specs=(field, P(None, "lev", ("px", "py"))),
        check_vma=False,
    )
```

```python
import functools

import jax
import jax.numpy as jnp
from jax import lax
from jax.experimental import pallas as pl
from jax.experimental.pallas import tpu as pltpu
from jax.sharding import PartitionSpec as P

SUBSTEPS = 4
A = 0.45
B = 0.3
LANES = 128
BLOCK = 256
MESH = pl.DeviceIdType.MESH


def iota(shape, dim):
    return lax.broadcasted_iota(jnp.int32, shape, dim)


def parts2(x):
    high = x.astype(jnp.bfloat16)
    return high, (x - high.astype(jnp.float32)).astype(jnp.bfloat16)


def dot_nt(a, b):
    return lax.dot_general(a, b, (((1,), (1,)), ((), ())), preferred_element_type=jnp.float32)


def opposite(s):
    return (s + 2) & 3


SHIFT = ((-1, 0), (0, -1), (1, 0), (0, 1))
DIAGONAL = ((0, 1), (0, 3), (2, 1), (2, 3))


def whole_kernel(
    sizes,
    edges,
    p_in,
    we_in,
    wn_in,
    wu_in,
    st_in,
    owner_in,
    source_in,
    weight_in,
    cell_in,
    p,
    latlon,
    we,
    wn,
    wu,
    st,
    owner,
    source,
    weight,
    cell,
    table,
    near_send,
    near_recv,
    diag_send,
    diag_recv,
    far_send,
    far_recv,
    own_relay,
    level_send,
    level_recv,
    plane_send,
    plane_recv,
    wu_below,
    flipped_cols,
    ghost_rows,
    p_strips,
    w_strips,
    st_strips,
    slot_source,
    slot_weight,
    pick_hot,
    pick_mask,
    land_hot,
    split,
    picked_early,
    picked_first,
    picked_second,
    picked_third,
    payload_early,
    payload_first,
    payload_top,
    payload_second,
    payload_third,
    arrived_early,
    arrived_first,
    arrived_top,
    arrived_second,
    arrived_third,
    total,
    in_sems,
    near_sems,
    diag_sems,
    far_sems,
    level_sems,
    plane_sems,
    wub_sems,
    give_sem,
    take_sem,
):
    n_px, n_py, n_lev = sizes
    levels, tile, _ = p.shape
    last = tile - 1
    loads = [
        pltpu.make_async_copy(src, dst, in_sems.at[k])
        for k, (src, dst) in enumerate(
            (
                (p_in, p),
                (we_in, we),
                (wn_in, wn),
                (st_in, st),
                (wu_in, wu),
                (owner_in, owner),
                (source_in, source),
                (weight_in, weight),
                (cell_in, cell),
            )
        )
    ]
    for load in loads:
        load.start()
    ix, iy, iz = lax.axis_index("px"), lax.axis_index("py"), lax.axis_index("lev")
    has_above, has_below = iz < n_lev - 1, iz > 0
    payload = (payload_early, payload_first, payload_top, payload_second, payload_third)
    arrived = (arrived_early, arrived_first, arrived_top, arrived_second, arrived_third)

    def place(dx, dy):
        return lax.rem(ix + dx + 2 * n_px, n_px), lax.rem(iy + dy + 2 * n_py, n_py)

    def at(dx, dy):
        x, y = place(dx, dy)
        return {"px": x, "py": y}

    others = {(d, 0) for d in range(1, n_px)}
    for dx, dy in ((0, 1), (0, -1), (0, 2), (0, -2), (1, 1), (1, -1), (-1, 1), (-1, -1)):
        others.add((dx % n_px, dy % n_py))
    beside = sorted(o for o in others if o[1])

    barrier = pltpu.get_barrier_semaphore()
    for dx, dy in beside:
        pl.semaphore_signal(barrier, inc=1, device_id=at(dx, dy), device_id_type=MESH)

    def greet(d, carry):
        pl.semaphore_signal(barrier, inc=1, device_id={"px": lax.rem(ix + d, n_px)}, device_id_type=MESH)
        return carry

    lax.fori_loop(1, n_px, greet, 0)

    @pl.when(has_above)
    def _():
        pl.semaphore_signal(barrier, inc=1, device_id={"lev": iz + 1}, device_id_type=MESH)

    @pl.when(has_below)
    def _():
        pl.semaphore_signal(barrier, inc=1, device_id={"lev": iz - 1}, device_id_type=MESH)

    def remote(src, dst, sems, index, device):
        return pltpu.make_async_remote_copy(
            src_ref=src,
            dst_ref=dst,
            send_sem=sems.at[(0,) + index],
            recv_sem=sems.at[(1,) + index],
            device_id=device,
            device_id_type=MESH,
        )

    def near_copy(t, s):
        dx, dy = SHIFT[s]
        return remote(near_send.at[t, s], near_recv.at[t, s], near_sems, (t, s), at(-dx, -dy))

    def diag_copy(t, k):
        (ax, ay), (bx, by) = SHIFT[DIAGONAL[k][0]], SHIFT[DIAGONAL[k][1]]
        return remote(diag_send.at[t, k], diag_recv.at[t, k], diag_sems, (t, k), at(-ax - bx, -ay - by))

    def far_copy(t, s):
        dx, dy = SHIFT[s]
        return remote(far_send.at[t, s], far_recv.at[t, s], far_sems, (t, s), at(-2 * dx, -2 * dy))

    def level_copy(t, up):
        return remote(
            level_send.at[t, up],
            level_recv.at[t, up],
            level_sems,
            (t, up),
            {"lev": iz + 1 if up else iz - 1},
        )

    def plane_copy(t, up, first=False):
        src = p_in.at[levels - 1 if up else 0] if first else plane_send.at[t, up]
        return remote(src, plane_recv.at[t, up], plane_sems, (t, up), {"lev": iz + 1 if up else iz - 1})

    def wub_copy():
        return remote(wu_in.at[levels - 1], wu_below, wub_sems, (0,), {"lev": iz + 1})

    row, lane = iota((tile, tile), 0), iota((tile, tile), 1)
    strip_row, strip_lane = iota((2 * levels, tile), 0), iota((2 * levels, tile), 1)
    outer = strip_row < levels

    def d_rows(f):
        return jnp.where(row == last, 0.0, pltpu.roll(f, last, 0)) - jnp.where(
            row == 0, 0.0, pltpu.roll(f, 1, 0)
        )

    def d_lanes(f):
        return jnp.where(lane == last, 0.0, pltpu.roll(f, last, 1)) - jnp.where(
            lane == 0, 0.0, pltpu.roll(f, 1, 1)
        )

    def columns(deep, shallow):
        packed = jnp.zeros((tile, tile), jnp.float32)
        for j, f in enumerate(deep):
            packed = jnp.where((lane >> 2) == j, pltpu.roll(f, 4 * j + 2, 1), packed)
        base = 4 * len(deep)
        for j, f in enumerate(shallow):
            packed = jnp.where((lane >> 1) == base // 2 + j, pltpu.roll(f, base + 2 * j + 1, 1), packed)
        flipped_cols[...] = packed.T

    def column(k):
        return flipped_cols[pl.ds(k, levels, stride=4), :]

    def rim_column(k):
        return flipped_cols[pl.ds(4 * levels + k, levels, stride=2), :]

    def take_strips():
        columns([p[j] for j in range(levels)], [wn[j] for j in range(levels)])
        for s, (a, b) in ((0, (0, 1)), (2, (last, last - 1))):
            p_strips[s, :levels] = p[:, a, :]
            p_strips[s, levels:] = p[:, b, :]
            w_strips[s, :levels] = we[:, a, :]
        for s, (a, b, c) in ((1, (2, 3, 1)), (3, (1, 0, 0))):
            p_strips[s, :levels] = column(a)
            p_strips[s, levels:] = column(b)
            w_strips[s, :levels] = rim_column(c)

    def code(x, y, s):
        c = edges[x, y, s]
        return c & 3, c >> 2

    def wanted(s, turn):
        return (s + 2 + turn) & 3

    def sign(s, turn):
        plus = ((turn + 1) & 3) < 2 if s % 2 == 0 else turn < 2
        return jnp.where(plus, 1.0, -1.0) * (1.0 if s < 2 else -1.0)

    def rim_sign(w):
        return jnp.where(w < 2, 1.0, -1.0) if not isinstance(w, int) else (1.0 if w < 2 else -1.0)

    near_plan = []
    for s in range(4):
        dx, dy = SHIFT[s]
        turn, flip = code(*place(-dx, -dy), s)
        near_plan.append((flip * 4 + wanted(s, turn), sign(s, turn)))

    def relay_plan(s, w, ax, ay):
        turn_a, flip_a = code(*place(ax, ay), s)
        turn_b, flip_b = code(*place(ax + SHIFT[s][0], ay + SHIFT[s][1]), w)
        return (flip_a ^ flip_b) * 4 + wanted(w, turn_b), sign(s, turn_a) * rim_sign(w)

    def relay_to(s, w):
        return relay_plan(s, w, -SHIFT[s][0] - SHIFT[w][0], -SHIFT[s][1] - SHIFT[w][1])

    diag_plan = [(relay_to(a, b), relay_to(b, a)) for a, b in DIAGONAL]
    far_plan = [relay_to(s, s) for s in range(4)]
    own_plan = [relay_to(s, opposite(s)) for s in range(4)]
    mine = [wanted(s, code(ix, iy, s)[0]) for s in range(4)]

    def relayed(t, s):
        found = own_relay[s]
        for k, (a, b) in enumerate(DIAGONAL):
            if s == a:
                found = jnp.where(mine[s] == b, diag_recv[t, k, :levels], found)
            if s == b:
                found = jnp.where(mine[s] == a, diag_recv[t, k, levels:], found)
        return jnp.where(mine[s] == s, far_recv[t, s], found)

    def send_rims(t):
        strips = [p_strips[s] for s in range(4)]
        rims = []
        for s in range(4):
            turned = A * pltpu.roll(strips[s], levels, 0)
            rims.append(jnp.where(outer, w_strips[s] - rim_sign(s) * turned, turned))
        for s in range(4):
            table[s] = rims[s]
            table[4 + s] = jnp.take_along_axis(rims[s], last - strip_lane, axis=1)
        for s in range(4):
            k, sgn = near_plan[s]
            rim = table[k]
            near_send[t, s] = jnp.where(outer, sgn * rim, rim)
            near_copy(t, s).start()
        for k in range(4):
            for half in range(2):
                which, sgn = diag_plan[k][half]
                diag_send[t, k, half * levels : (half + 1) * levels] = sgn * table[which, levels:]
            diag_copy(t, k).start()
        for s in range(4):
            k, sgn = far_plan[s]
            far_send[t, s] = sgn * table[k, levels:]
            far_copy(t, s).start()
        for s in range(4):
            k, sgn = own_plan[s]
            own_relay[s] = sgn * table[k, levels:]
            for up, level in ((1, levels - 1), (0, 0)):
                level_send[t, up, 2 * s : 2 * s + 2] = p_strips[s, pl.ds(level, 2, stride=levels), :]

        @pl.when(has_above)
        def _():
            level_copy(t, 1).start()

        @pl.when(has_below)
        def _():
            level_copy(t, 0).start()

    def corners(s, low, high):
        found = jnp.zeros((2 * levels, tile), jnp.float32)
        for depth in range(2):
            start = depth if s < 2 else last - depth
            for e in range(2):
                for pair, end in ((low, e), (high, last - e)):
                    moved = pltpu.roll(pair[depth ^ e], (end - start) % tile, 1) if end != start else pair[depth ^ e]
                    here = (strip_lane == end) & (outer if depth == 0 else jnp.logical_not(outer))
                    found = jnp.where(here, moved, found)
        return found

    def next_strips(t):
        for s in range(4):
            near_copy(t, s).wait_recv()
        for k in range(4):
            diag_copy(t, k).wait_recv()
        for s in range(4):
            far_copy(t, s).wait_recv()

        @pl.when(has_above)
        def _():
            level_copy(t, 0).wait_recv()

        @pl.when(has_below)
        def _():
            level_copy(t, 1).wait_recv()

        zero = jnp.zeros((levels, tile), jnp.float32)
        ghosts = []
        for s in range(4):
            ghosts.append(near_recv[t, s] + jnp.concatenate([relayed(t, s), zero], axis=0))
        pairs = [(g, pltpu.roll(g, levels, 0)) for g in ghosts]
        for s in range(4):
            low, high = (pairs[1], pairs[3]) if s % 2 == 0 else (pairs[0], pairs[2])
            across = jnp.zeros((2 * levels, tile), jnp.float32)
            for depth in range(2):
                below, above = level_recv[t, 1], level_recv[t, 0]
                k = 2 * s + depth
                across = jnp.where(strip_row == depth * levels, below[k : k + 1], across)
                across = across + jnp.where(strip_row == (depth + 1) * levels - 1, above[k : k + 1], 0.0)
            p_strips[s] = p_strips[s] + st_strips[s] * (
                A * (ghosts[s] + corners(s, low, high)) + (B * B) * across
            )
            w_strips[s] = jnp.where(outer, w_strips[s] + rim_sign(s) * pairs[s][1], 0.0)

    def give_copy(c, o):
        return pltpu.make_async_remote_copy(
            src_ref=payload[c].at[o],
            dst_ref=arrived[c].at[ix],
            send_sem=give_sem.at[c, o],
            recv_sem=take_sem.at[c, ix],
            device_id={"px": o},
            device_id_type=MESH,
        )

    def got(c, o):
        return pltpu.make_async_remote_copy(
            src_ref=payload[c].at[o],
            dst_ref=arrived[c].at[o],
            send_sem=give_sem.at[c, o],
            recv_sem=take_sem.at[c, o],
            device_id={"px": o},
            device_id_type=MESH,
        )

    w_strips[...] = jnp.zeros(w_strips.shape, jnp.float32)
    ghost_rows[...] = jnp.zeros((tile, tile), jnp.float32)

    @pl.when(jnp.logical_not(has_below))
    def _():
        wu_below[...] = jnp.zeros((tile, tile), jnp.float32)
        level_recv[:, 1] = jnp.zeros((SUBSTEPS, 8, tile), jnp.float32)

    @pl.when(jnp.logical_not(has_above))
    def _():
        level_recv[:, 0] = jnp.zeros((SUBSTEPS, 8, tile), jnp.float32)

    for load in loads[:3]:
        load.wait()
    take_strips()
    pl.semaphore_wait(
        barrier, n_px - 1 + len(beside) + has_above.astype(jnp.int32) + has_below.astype(jnp.int32)
    )
    send_rims(0)

    @pl.when(has_above)
    def _():
        wub_copy().start()
        plane_copy(0, 1, True).start()

    @pl.when(has_below)
    def _():
        plane_copy(0, 0, True).start()

    for load in loads[3:]:
        load.wait()
    columns([st[j] for j in range(levels)], [])
    for s, (a, b) in ((0, (0, 1)), (2, (last, last - 1))):
        st_strips[s, :levels] = st[:, a, :]
        st_strips[s, levels:] = st[:, b, :]
    for s, (a, b) in ((1, (2, 3)), (3, (1, 0))):
        st_strips[s, :levels] = column(a)
        st_strips[s, levels:] = column(b)
    slot_count = payload_first.shape[2]
    top = levels - 1
    every = tuple(range(levels))
    stages = (
        (picked_early, ((0, 0, top),), [(wu, l) for l in every[:top]]),
        (picked_first, ((1, 0, levels), (2, levels, levels + 1)), [(we, l) for l in every] + [(wu, top)]),
        (picked_second, ((3, 0, levels),), [(wn, l) for l in every]),
        (picked_third, ((4, 0, levels),), [(p, l) for l in every]),
    )
    capacity = pick_hot.shape[1]
    packed = capacity < n_px * slot_count
    find_slots(n_px, slot_count, packed, owner, source, weight, slot_source, slot_weight)
    steps = (capacity // LANES - 1).bit_length()
    if packed:
        filled = [
            jnp.sum(jnp.sum((owner[...] == o).astype(jnp.int32), axis=0, keepdims=True), axis=1, keepdims=True)
            for o in range(n_px)
        ]

    def part_of(o, found, low, high):
        if not packed:
            return found[low:high, pl.ds(pl.multiple_of(o * slot_count, LANES), slot_count)]
        start, count = jnp.zeros((1, 1), jnp.int32), jnp.zeros((1, 1), jnp.int32)
        for k, n in enumerate(filled):
            start = start + jnp.where(k < o, (n + (LANES - 1)) >> 7, 0)
            count = count + jnp.where(k == o, n, 0)
        part = found[low:high, :]
        for k in reversed(range(steps)):
            width = slot_count + ((1 << k) - 1) * LANES
            part = jnp.where(
                ((start >> k) & 1) == 1, part[:, LANES << k : (LANES << k) + width], part[:, :width]
            )
        return jnp.where(iota(part.shape, 1) < count, part, 0.0)

    def ahead(d):
        return lax.rem(ix + d + 1, n_px)

    def hand_over(k):
        found, parts, planes = stages[k]
        first = sum(len(stage[2]) for stage in stages[:k])
        for n, (field, l) in enumerate(planes):
            split_plane(split, field[l], first + n)
        pick(first, split, pick_hot, pick_mask, found)

        def lay_out(o):
            whole = part_of(o, found, 0, len(planes))
            for c, low, high in parts:
                payload[c][o] = whole[low:high]

        def send(d, carry):
            lay_out(ahead(d))
            for c, _, _ in parts:
                give_copy(c, ahead(d)).start()
            return carry

        lax.fori_loop(0, n_px - 1, send, 0)
        lay_out(ix)

    def substep(t, carry):
        for j in range(levels):
            we[j] = we[j] - A * d_rows(p[j])
            wn[j] = wn[j] - A * d_lanes(p[j])
        for j in range(levels - 1):
            wu[j] = wu[j] - B * (p[j + 1] - p[j])

        @pl.when(has_above)
        def _():
            wu[levels - 1] = wu[levels - 1] + B * p[levels - 1]

        @pl.when(jnp.logical_not(has_above))
        def _():
            wu[levels - 1] = jnp.zeros((tile, tile), jnp.float32)

        for j in range(1, levels):
            p[j] = p[j] - st[j] * (A * (d_rows(we[j]) + d_lanes(wn[j])) + B * (wu[j] - wu[j - 1]))

        @pl.when(has_below & (t == 0))
        def _():
            wub_copy().wait_recv()

        @pl.when(has_below)
        def _():
            wu_below[...] = wu_below[...] - B * p[0]

        p[0] = p[0] - st[0] * (A * (d_rows(we[0]) + d_lanes(wn[0])) + B * (wu[0] - wu_below[...]))
        take_strips()

        @pl.when(t == 1)
        def _():
            pick_tables(slot_source, slot_weight, pick_hot, pick_mask)
            if packed:
                for found, _, planes in stages:
                    found[:, capacity:] = jnp.zeros((len(planes), found.shape[1] - capacity), jnp.float32)

        @pl.when(t == 2)
        def _():
            land_tables(cell, land_hot)
            total[...] = jnp.zeros(total.shape, jnp.float32)

        @pl.when(t == SUBSTEPS - 1)
        def _():
            hand_over(0)

        next_strips(t)

        @pl.when(t < SUBSTEPS - 1)
        def _():
            send_rims(t + 1)

        @pl.when(has_above)
        def _():
            plane_copy(t, 0).wait_recv()
            wu[levels - 1] = wu[levels - 1] - B * plane_recv[t, 0]
            p[levels - 1] = p[levels - 1] + (B * B) * (st[levels - 1] * plane_recv[t, 0])

        @pl.when(has_below)
        def _():
            plane_copy(t, 1).wait_recv()
            wu_below[...] = wu_below[...] + B * plane_recv[t, 1]
            p[0] = p[0] + (B * B) * (st[0] * plane_recv[t, 1])

        for s, (a, b) in ((0, (0, 1)), (2, (last, last - 1))):
            p[:, a, :] = p_strips[s, :levels]
            p[:, b, :] = p_strips[s, levels:]
            we[:, a, :] = w_strips[s, :levels]
        for k, (s, half) in enumerate(((3, 1), (3, 0), (1, 0), (1, 1))):
            ghost_rows[pl.ds(k, levels, stride=4), :] = p_strips[s, half * levels : (half + 1) * levels]
        for k, s in enumerate((3, 1)):
            ghost_rows[pl.ds(4 * levels + k, levels, stride=2), :] = w_strips[s, :levels]
        turned = ghost_rows[...].T
        rim = (lane == 0) | (lane == last)
        band = (lane <= 1) | (lane >= last - 1)
        for j in range(levels):
            p[j] = jnp.where(band, pltpu.roll(turned, (tile - 4 * j - 2) % tile, 1), p[j])
            wn[j] = jnp.where(rim, pltpu.roll(turned, (tile - 4 * levels - 2 * j - 1) % tile, 1), wn[j])

        @pl.when((t < SUBSTEPS - 1) & has_above)
        def _():
            plane_send[t + 1, 1] = p[levels - 1]
            plane_copy(t + 1, 1).start()

        @pl.when((t < SUBSTEPS - 1) & has_below)
        def _():
            plane_send[t + 1, 0] = p[0]
            plane_copy(t + 1, 0).start()

        return carry

    lax.fori_loop(0, SUBSTEPS, substep, 0)

    for k in range(1, len(stages)):
        hand_over(k)

    groups = latlon.shape[2] // BLOCK
    sums = ((3, (0, 2)), (1, (1,)), (2, (3,)), (0, (4,)))

    for q, parts in sums:
        land(q, [payload[c][ix] for c in parts], cell, land_hot, ix, total)

    for q, parts in sums:

        def bring_in(d, carry):
            o = lax.rem(ix + n_px - d - 1, n_px)
            for c in parts:
                got(c, o).wait_recv()
            land(q, [arrived[c][o] for c in parts], cell, land_hot, o, total)
            return carry

        lax.fori_loop(0, n_px - 1, bring_in, 0)
        for g in range(groups):
            high, low = g * levels, (groups + g) * levels
            latlon[q, :, g * BLOCK : (g + 1) * BLOCK] = total[q, high : high + levels] + total[q, low : low + levels]

    def drain(t, carry):
        for s in range(4):
            near_copy(t, s).wait_send()
            diag_copy(t, s).wait_send()
            far_copy(t, s).wait_send()

        @pl.when(has_above)
        def _():
            level_copy(t, 1).wait_send()
            plane_copy(t, 1).wait_send()

        @pl.when(has_below)
        def _():
            level_copy(t, 0).wait_send()
            plane_copy(t, 0).wait_send()

        return carry

    lax.fori_loop(0, SUBSTEPS, drain, 0)

    @pl.when(has_above)
    def _():
        wub_copy().wait_send()

    def sent(d, carry):
        for c in range(len(payload)):
            give_copy(c, ahead(d)).wait_send()
        return carry

    lax.fori_loop(0, n_px - 1, sent, 0)


def find_slots(owner_count, slot_count, packed, owner, source, weight, slot_source, slot_weight):
    rows = owner.shape[0]
    slot_rows = slot_source.shape[0]
    names = owner[...]
    up_to = (iota((LANES, LANES), 0) <= iota((LANES, LANES), 1)).astype(jnp.bfloat16)
    ones = jnp.ones((LANES, LANES), jnp.bfloat16)
    before = (iota((rows, rows), 0) > iota((rows, rows), 1)).astype(jnp.bfloat16)

    def count(o, carry):
        place, start = carry
        named = names == o
        hot = named.astype(jnp.float32).astype(jnp.bfloat16)
        within = jnp.dot(hot, up_to, preferred_element_type=jnp.float32)
        total = jnp.dot(hot, ones, preferred_element_type=jnp.float32)
        earlier = jnp.dot(before, total.astype(jnp.bfloat16), preferred_element_type=jnp.float32)
        place = jnp.where(named, within + earlier - 1.0 + start, place)
        if packed:
            filled = jnp.sum(total, axis=0, keepdims=True)
            start = start + jnp.floor((filled + (LANES - 1.0)) / LANES) * LANES
        else:
            start = start + float(slot_count)
        return place, start

    zero = jnp.zeros(names.shape, jnp.float32)
    place, _ = lax.fori_loop(0, owner_count, count, (zero, jnp.zeros((1, LANES), jnp.float32)))
    slot = place.astype(jnp.int32)
    slot_high, slot_low = slot >> 7, slot & (LANES - 1)
    src = source[...]
    w = weight[...]
    w1 = w.astype(jnp.bfloat16).astype(jnp.float32)
    w2 = (w - w1).astype(jnp.bfloat16).astype(jnp.float32)
    w3 = w - w1 - w2
    pieces = [(src >> 7).astype(jnp.float32), (src & (LANES - 1)).astype(jnp.float32), w1, w2, w3]
    high_place, low_place = iota((slot_rows, LANES), 0), iota((LANES, LANES), 0)
    total = jnp.zeros((len(pieces) * slot_rows, LANES), jnp.float32)
    for r in range(rows):
        here = high_place == slot_high[r : r + 1]
        left = jnp.concatenate([jnp.where(here, piece[r : r + 1], 0.0) for piece in pieces], axis=0)
        right = jnp.where(low_place == slot_low[r : r + 1], 1.0, 0.0)
        total += dot_nt(left.astype(jnp.bfloat16), right.astype(jnp.bfloat16))
    part = [total[k * slot_rows : (k + 1) * slot_rows] for k in range(len(pieces))]
    slot_source[...] = (part[0] * LANES + part[1]).astype(jnp.int32)
    slot_weight[...] = part[2] + part[3] + part[4]


def split_plane(split, plane, r):
    tile = plane.shape[0]
    half = tile // 2
    h, d = parts2(plane.T)
    for k, part in enumerate((h[:half], h[half:], d[:half], d[half:])):
        split[r * half : (r + 1) * half, k * tile : (k + 1) * tile] = part


def joined(ref, row, pieces):
    return jnp.concatenate([ref[pl.ds(row + k, 1), :] for k in range(pieces)], axis=1)


def pick_tables(slot_source, slot_weight, pick_hot, pick_mask):
    lines, capacity = pick_hot.shape
    tile, half = lines // 2, pick_mask.shape[0]
    pieces = BLOCK // LANES

    def step(b, carry):
        at = pl.ds(pl.multiple_of(b * BLOCK, BLOCK), BLOCK)
        src, w = joined(slot_source, b * pieces, pieces), joined(slot_weight, b * pieces, pieces)
        x, y = src >> 7, src & (tile - 1)
        line = x + jnp.where(y >= half, tile, 0)
        pick_hot[:, at] = jnp.where(iota((lines, BLOCK), 0) == line, 1.0, 0.0).astype(jnp.bfloat16)
        pick_mask[:, at] = jnp.where(iota((half, BLOCK), 0) == (y & (half - 1)), w, 0.0)
        return carry

    lax.fori_loop(0, capacity // BLOCK, step, 0)


def pick(first, split, pick_hot, pick_mask, found):
    rows = found.shape[0]
    half, capacity = pick_mask.shape
    lines = slice(first * half, (first + rows) * half)
    width = 2 * BLOCK if capacity % (2 * BLOCK) == 0 else BLOCK
    steps = capacity // width

    def step(b, carry):
        at = pl.ds(pl.multiple_of(b * width, width), width)
        hot = pick_hot[:, at]
        line = jnp.dot(
            split[lines, :], jnp.concatenate([hot, hot], axis=0), preferred_element_type=jnp.float32
        )
        found[:, at] = jnp.sum(line.reshape(rows, half, width) * pick_mask[:, at][None], axis=1)
        return carry

    lax.fori_loop(0, steps, step, 0, unroll=steps if steps < 12 else 4)


def land_tables(cell, land_hot):
    owner_count, _, slot_count = land_hot.shape
    pieces = slot_count // LANES

    def step(o, carry):
        c = joined(cell, o * pieces, pieces)
        hot = jnp.where(iota((BLOCK, slot_count), 0) == (c & (BLOCK - 1)), 1.0, 0.0)
        land_hot[o] = hot.astype(jnp.bfloat16)
        return carry

    lax.fori_loop(0, owner_count, step, 0)


def land(q, parts, cell, land_hot, o, total):
    values = parts[0] if len(parts) == 1 else jnp.concatenate(parts, axis=0)
    rows, slot_count = values.shape
    groups = total.shape[1] // (2 * rows)
    pieces = slot_count // LANES
    group = joined(cell, o * pieces, pieces) >> 8
    h = values.astype(jnp.bfloat16).astype(jnp.float32)
    spread = [jnp.where(group == g, h, 0.0) for g in range(groups)]
    spread += [jnp.where(group == g, values - h, 0.0) for g in range(groups)]
    total[q] += dot_nt(jnp.concatenate(spread, axis=0).astype(jnp.bfloat16), land_hot[o])


def per_device(
    sizes,
    pressure,
    wind_east,
    wind_north,
    wind_up,
    stiffness,
    edge_table,
    remap_source,
    remap_weight,
    remap_owner,
    latlon_cell,
):
    levels, tile, _ = pressure.shape
    owner_count = sizes[0]
    slots = latlon_cell.shape[0]
    slot_count = slots // owner_count
    cell_count = tile * tile // 8
    count = 4 * levels
    entries = remap_source.shape[0]
    rows = entries // LANES
    capacity = -(-(entries + (owner_count - 1) * (LANES - 1)) // BLOCK) * BLOCK
    capacity = min(capacity, slots)
    room = capacity
    if capacity < slots:
        room = slot_count + ((2 << (capacity // LANES - 1).bit_length() - 1) - 1) * LANES + LANES
        room = max(room, capacity)
    slot_rows = -(-capacity // (8 * LANES)) * 8
    part_rows = (levels - 1, levels, 1, levels, levels)
    f32, i32 = jnp.float32, jnp.int32
    n = SUBSTEPS
    field = pltpu.VMEM(pressure.shape, f32)
    plane = pltpu.VMEM((tile, tile), f32)
    dma = pltpu.SemaphoreType.DMA
    in_vmem = pl.BlockSpec(memory_space=pltpu.VMEM)
    return pl.pallas_call(
        functools.partial(whole_kernel, sizes),
        out_shape=[
            jax.ShapeDtypeStruct(pressure.shape, f32),
            jax.ShapeDtypeStruct((4, levels, cell_count), f32),
        ],
        in_specs=[pl.BlockSpec(memory_space=pltpu.SMEM)] + [pl.BlockSpec(memory_space=pl.ANY)] * 9,
        out_specs=[in_vmem] * 2,
        scratch_shapes=[
            field,
            field,
            field,
            field,
            pltpu.VMEM((rows, LANES), i32),
            pltpu.VMEM((rows, LANES), i32),
            pltpu.VMEM((rows, LANES), f32),
            pltpu.VMEM((slots // LANES, LANES), i32),
            pltpu.VMEM((8, 2 * levels, tile), f32),
            pltpu.VMEM((n, 4, 2 * levels, tile), f32),
            pltpu.VMEM((n, 4, 2 * levels, tile), f32),
            pltpu.VMEM((n, 4, 2 * levels, tile), f32),
            pltpu.VMEM((n, 4, 2 * levels, tile), f32),
            pltpu.VMEM((n, 4, levels, tile), f32),
            pltpu.VMEM((n, 4, levels, tile), f32),
            pltpu.VMEM((4, levels, tile), f32),
            pltpu.VMEM((n, 2, 8, tile), f32),
            pltpu.VMEM((n, 2, 8, tile), f32),
            pltpu.VMEM((n, 2, tile, tile), f32),
            pltpu.VMEM((n, 2, tile, tile), f32),
            plane,
            plane,
            plane,
            pltpu.VMEM((4, 2 * levels, tile), f32),
            pltpu.VMEM((4, 2 * levels, tile), f32),
            pltpu.VMEM((4, 2 * levels, tile), f32),
            pltpu.VMEM((slot_rows, LANES), i32),
            pltpu.VMEM((slot_rows, LANES), f32),
            pltpu.VMEM((2 * tile, capacity), jnp.bfloat16),
            pltpu.VMEM((tile // 2, capacity), f32),
            pltpu.VMEM((owner_count, BLOCK, slot_count), jnp.bfloat16),
            pltpu.VMEM((count * tile // 2, 4 * tile), jnp.bfloat16),
            *(pltpu.VMEM((n_rows, room), f32) for n_rows in (levels - 1, levels + 1, levels, levels)),
            *(pltpu.VMEM((owner_count, n_rows, slot_count), f32) for n_rows in part_rows),
            *(pltpu.VMEM((owner_count, n_rows, slot_count), f32) for n_rows in part_rows),
            pltpu.VMEM((4, 2 * levels * (cell_count // BLOCK), BLOCK), f32),
            dma((9,)),
            dma((2, n, 4)),
            dma((2, n, 4)),
            dma((2, n, 4)),
            dma((2, n, 2)),
            dma((2, n, 2)),
            dma((2, 1)),
            dma((len(part_rows), owner_count)),
            dma((len(part_rows), owner_count)),
        ],
        compiler_params=pltpu.CompilerParams(
            collective_id=0, has_side_effects=True, vmem_limit_bytes=60 * 2**20
        ),
    )(
        edge_table,
        pressure,
        wind_east,
        wind_north,
        wind_up,
        stiffness,
        remap_owner.reshape(rows, LANES),
        remap_source.reshape(rows, LANES),
        remap_weight.reshape(rows, LANES),
        latlon_cell.reshape(slots // LANES, LANES),
    )


def solution(mesh):
    field = P("lev", "px", "py")
    entries = P(("px", "py"))
    sizes = (mesh.shape["px"], mesh.shape["py"], mesh.shape["lev"])
    return jax.shard_map(
        functools.partial(per_device, sizes),
        mesh=mesh,
        in_specs=(field,) * 5 + (P(), entries, entries, P(("px", "py"), None), entries),
        out_specs=(field, P(None, "lev", ("px", "py"))),
        check_vma=False,
    )
```

```python
import functools

import jax
import jax.numpy as jnp
from jax import lax
from jax.experimental import pallas as pl
from jax.experimental.pallas import tpu as pltpu
from jax.sharding import PartitionSpec as P

SUBSTEPS = 4
A = 0.45
B = 0.3
LANES = 128
BLOCK = 256
MESH = pl.DeviceIdType.MESH


def iota(shape, dim):
    return lax.broadcasted_iota(jnp.int32, shape, dim)


def parts2(x):
    high = x.astype(jnp.bfloat16)
    return high, (x - high.astype(jnp.float32)).astype(jnp.bfloat16)


def dot_nt(a, b):
    return lax.dot_general(a, b, (((1,), (1,)), ((), ())), preferred_element_type=jnp.float32)


def opposite(s):
    return (s + 2) & 3


SHIFT = ((-1, 0), (0, -1), (1, 0), (0, 1))
DIAGONAL = ((0, 1), (0, 3), (2, 1), (2, 3))


def whole_kernel(
    sizes,
    edges,
    p_in,
    we_in,
    wn_in,
    wu_in,
    st_in,
    owner_in,
    source_in,
    weight_in,
    cell_in,
    p,
    latlon,
    we,
    wn,
    wu,
    st,
    owner,
    source,
    weight,
    cell,
    table,
    near_send,
    near_recv,
    diag_send,
    diag_recv,
    far_send,
    far_recv,
    own_relay,
    level_send,
    level_recv,
    plane_send,
    plane_recv,
    wu_below,
    flipped_cols,
    ghost_rows,
    p_strips,
    w_strips,
    st_strips,
    slot_source,
    slot_weight,
    pick_hot,
    pick_mask,
    land_hot,
    split,
    picked_early,
    picked_first,
    picked_second,
    picked_third,
    payload_early,
    payload_first,
    payload_top,
    payload_second,
    payload_third,
    arrived_early,
    arrived_first,
    arrived_top,
    arrived_second,
    arrived_third,
    total,
    in_sems,
    near_sems,
    diag_sems,
    far_sems,
    level_sems,
    plane_sems,
    wub_sems,
    give_sem,
    take_sem,
):
    n_px, n_py, n_lev = sizes
    levels, tile, _ = p.shape
    last = tile - 1
    loads = [
        pltpu.make_async_copy(src, dst, in_sems.at[k])
        for k, (src, dst) in enumerate(
            (
                (p_in, p),
                (we_in, we),
                (wn_in, wn),
                (st_in, st),
                (wu_in, wu),
                (owner_in, owner),
                (source_in, source),
                (weight_in, weight),
                (cell_in, cell),
            )
        )
    ]
    for load in loads:
        load.start()
    ix, iy, iz = lax.axis_index("px"), lax.axis_index("py"), lax.axis_index("lev")
    has_above, has_below = iz < n_lev - 1, iz > 0
    payload = (payload_early, payload_first, payload_top, payload_second, payload_third)
    arrived = (arrived_early, arrived_first, arrived_top, arrived_second, arrived_third)

    def place(dx, dy):
        return lax.rem(ix + dx + 2 * n_px, n_px), lax.rem(iy + dy + 2 * n_py, n_py)

    def at(dx, dy):
        x, y = place(dx, dy)
        return {"px": x, "py": y}

    others = {(d, 0) for d in range(1, n_px)}
    for dx, dy in ((0, 1), (0, -1), (0, 2), (0, -2), (1, 1), (1, -1), (-1, 1), (-1, -1)):
        others.add((dx % n_px, dy % n_py))
    beside = sorted(o for o in others if o[1])

    barrier = pltpu.get_barrier_semaphore()
    for dx, dy in beside:
        pl.semaphore_signal(barrier, inc=1, device_id=at(dx, dy), device_id_type=MESH)

    def greet(d, carry):
        pl.semaphore_signal(barrier, inc=1, device_id={"px": lax.rem(ix + d, n_px)}, device_id_type=MESH)
        return carry

    lax.fori_loop(1, n_px, greet, 0)

    @pl.when(has_above)
    def _():
        pl.semaphore_signal(barrier, inc=1, device_id={"lev": iz + 1}, device_id_type=MESH)

    @pl.when(has_below)
    def _():
        pl.semaphore_signal(barrier, inc=1, device_id={"lev": iz - 1}, device_id_type=MESH)

    def remote(src, dst, sems, index, device):
        return pltpu.make_async_remote_copy(
            src_ref=src,
            dst_ref=dst,
            send_sem=sems.at[(0,) + index],
            recv_sem=sems.at[(1,) + index],
            device_id=device,
            device_id_type=MESH,
        )

    def near_copy(t, s):
        dx, dy = SHIFT[s]
        return remote(near_send.at[t, s], near_recv.at[t, s], near_sems, (t, s), at(-dx, -dy))

    def diag_copy(t, k):
        (ax, ay), (bx, by) = SHIFT[DIAGONAL[k][0]], SHIFT[DIAGONAL[k][1]]
        return remote(diag_send.at[t, k], diag_recv.at[t, k], diag_sems, (t, k), at(-ax - bx, -ay - by))

    def far_copy(t, s):
        dx, dy = SHIFT[s]
        return remote(far_send.at[t, s], far_recv.at[t, s], far_sems, (t, s), at(-2 * dx, -2 * dy))

    def level_copy(t, up):
        return remote(
            level_send.at[t, up],
            level_recv.at[t, up],
            level_sems,
            (t, up),
            {"lev": iz + 1 if up else iz - 1},
        )

    def plane_copy(t, up, first=False):
        src = p_in.at[levels - 1 if up else 0] if first else plane_send.at[t, up]
        return remote(src, plane_recv.at[t, up], plane_sems, (t, up), {"lev": iz + 1 if up else iz - 1})

    def wub_copy():
        return remote(wu_in.at[levels - 1], wu_below, wub_sems, (0,), {"lev": iz + 1})

    row, lane = iota((tile, tile), 0), iota((tile, tile), 1)
    strip_row, strip_lane = iota((2 * levels, tile), 0), iota((2 * levels, tile), 1)
    outer = strip_row < levels

    def d_rows(f):
        return jnp.where(row == last, 0.0, pltpu.roll(f, last, 0)) - jnp.where(
            row == 0, 0.0, pltpu.roll(f, 1, 0)
        )

    def d_lanes(f):
        return jnp.where(lane == last, 0.0, pltpu.roll(f, last, 1)) - jnp.where(
            lane == 0, 0.0, pltpu.roll(f, 1, 1)
        )

    def columns(deep, shallow):
        packed = jnp.zeros((tile, tile), jnp.float32)
        for j, f in enumerate(deep):
            packed = jnp.where((lane >> 2) == j, pltpu.roll(f, 4 * j + 2, 1), packed)
        base = 4 * len(deep)
        for j, f in enumerate(shallow):
            packed = jnp.where((lane >> 1) == base // 2 + j, pltpu.roll(f, base + 2 * j + 1, 1), packed)
        flipped_cols[...] = packed.T

    def column(k):
        return flipped_cols[pl.ds(k, levels, stride=4), :]

    def rim_column(k):
        return flipped_cols[pl.ds(4 * levels + k, levels, stride=2), :]

    def take_strips():
        columns([p[j] for j in range(levels)], [wn[j] for j in range(levels)])
        for s, (a, b) in ((0, (0, 1)), (2, (last, last - 1))):
            p_strips[s, :levels] = p[:, a, :]
            p_strips[s, levels:] = p[:, b, :]
            w_strips[s, :levels] = we[:, a, :]
        for s, (a, b, c) in ((1, (2, 3, 1)), (3, (1, 0, 0))):
            p_strips[s, :levels] = column(a)
            p_strips[s, levels:] = column(b)
            w_strips[s, :levels] = rim_column(c)

    def code(x, y, s):
        c = edges[x, y, s]
        return c & 3, c >> 2

    def wanted(s, turn):
        return (s + 2 + turn) & 3

    def sign(s, turn):
        plus = ((turn + 1) & 3) < 2 if s % 2 == 0 else turn < 2
        return jnp.where(plus, 1.0, -1.0) * (1.0 if s < 2 else -1.0)

    def rim_sign(w):
        return jnp.where(w < 2, 1.0, -1.0) if not isinstance(w, int) else (1.0 if w < 2 else -1.0)

    near_plan = []
    for s in range(4):
        dx, dy = SHIFT[s]
        turn, flip = code(*place(-dx, -dy), s)
        near_plan.append((flip * 4 + wanted(s, turn), sign(s, turn)))

    def relay_plan(s, w, ax, ay):
        turn_a, flip_a = code(*place(ax, ay), s)
        turn_b, flip_b = code(*place(ax + SHIFT[s][0], ay + SHIFT[s][1]), w)
        return (flip_a ^ flip_b) * 4 + wanted(w, turn_b), sign(s, turn_a) * rim_sign(w)

    def relay_to(s, w):
        return relay_plan(s, w, -SHIFT[s][0] - SHIFT[w][0], -SHIFT[s][1] - SHIFT[w][1])

    diag_plan = [(relay_to(a, b), relay_to(b, a)) for a, b in DIAGONAL]
    far_plan = [relay_to(s, s) for s in range(4)]
    own_plan = [relay_to(s, opposite(s)) for s in range(4)]
    mine = [wanted(s, code(ix, iy, s)[0]) for s in range(4)]

    def relayed(t, s):
        found = own_relay[s]
        for k, (a, b) in enumerate(DIAGONAL):
            if s == a:
                found = jnp.where(mine[s] == b, diag_recv[t, k, :levels], found)
            if s == b:
                found = jnp.where(mine[s] == a, diag_recv[t, k, levels:], found)
        return jnp.where(mine[s] == s, far_recv[t, s], found)

    def send_rims(t):
        strips = [p_strips[s] for s in range(4)]
        rims = []
        for s in range(4):
            turned = A * pltpu.roll(strips[s], levels, 0)
            rims.append(jnp.where(outer, w_strips[s] - rim_sign(s) * turned, turned))
        for s in range(4):
            table[s] = rims[s]
            table[4 + s] = jnp.take_along_axis(rims[s], last - strip_lane, axis=1)
        for s in range(4):
            k, sgn = near_plan[s]
            rim = table[k]
            near_send[t, s] = jnp.where(outer, sgn * rim, rim)
            near_copy(t, s).start()
        for k in range(4):
            for half in range(2):
                which, sgn = diag_plan[k][half]
                diag_send[t, k, half * levels : (half + 1) * levels] = sgn * table[which, levels:]
            diag_copy(t, k).start()
        for s in range(4):
            k, sgn = far_plan[s]
            far_send[t, s] = sgn * table[k, levels:]
            far_copy(t, s).start()
        for s in range(4):
            k, sgn = own_plan[s]
            own_relay[s] = sgn * table[k, levels:]
            for up, level in ((1, levels - 1), (0, 0)):
                level_send[t, up, 2 * s : 2 * s + 2] = p_strips[s, pl.ds(level, 2, stride=levels), :]

        @pl.when(has_above)
        def _():
            level_copy(t, 1).start()

        @pl.when(has_below)
        def _():
            level_copy(t, 0).start()

    def corners(s, low, high):
        found = jnp.zeros((2 * levels, tile), jnp.float32)
        for depth in range(2):
            start = depth if s < 2 else last - depth
            for e in range(2):
                for pair, end in ((low, e), (high, last - e)):
                    moved = pltpu.roll(pair[depth ^ e], (end - start) % tile, 1) if end != start else pair[depth ^ e]
                    here = (strip_lane == end) & (outer if depth == 0 else jnp.logical_not(outer))
                    found = jnp.where(here, moved, found)
        return found

    def next_strips(t):
        for s in range(4):
            near_copy(t, s).wait_recv()
        for k in range(4):
            diag_copy(t, k).wait_recv()
        for s in range(4):
            far_copy(t, s).wait_recv()

        @pl.when(has_above)
        def _():
            level_copy(t, 0).wait_recv()

        @pl.when(has_below)
        def _():
            level_copy(t, 1).wait_recv()

        zero = jnp.zeros((levels, tile), jnp.float32)
        ghosts = []
        for s in range(4):
            ghosts.append(near_recv[t, s] + jnp.concatenate([relayed(t, s), zero], axis=0))
        pairs = [(g, pltpu.roll(g, levels, 0)) for g in ghosts]
        for s in range(4):
            low, high = (pairs[1], pairs[3]) if s % 2 == 0 else (pairs[0], pairs[2])
            across = jnp.zeros((2 * levels, tile), jnp.float32)
            for depth in range(2):
                below, above = level_recv[t, 1], level_recv[t, 0]
                k = 2 * s + depth
                across = jnp.where(strip_row == depth * levels, below[k : k + 1], across)
                across = across + jnp.where(strip_row == (depth + 1) * levels - 1, above[k : k + 1], 0.0)
            p_strips[s] = p_strips[s] + st_strips[s] * (
                A * (ghosts[s] + corners(s, low, high)) + (B * B) * across
            )
            w_strips[s] = jnp.where(outer, w_strips[s] + rim_sign(s) * pairs[s][1], 0.0)

    def give_copy(c, o):
        return pltpu.make_async_remote_copy(
            src_ref=payload[c].at[o],
            dst_ref=arrived[c].at[ix],
            send_sem=give_sem.at[c, o],
            recv_sem=take_sem.at[c, ix],
            device_id={"px": o},
            device_id_type=MESH,
        )

    def got(c, o):
        return pltpu.make_async_remote_copy(
            src_ref=payload[c].at[o],
            dst_ref=arrived[c].at[o],
            send_sem=give_sem.at[c, o],
            recv_sem=take_sem.at[c, o],
            device_id={"px": o},
            device_id_type=MESH,
        )

    w_strips[...] = jnp.zeros(w_strips.shape, jnp.float32)
    ghost_rows[...] = jnp.zeros((tile, tile), jnp.float32)

    @pl.when(jnp.logical_not(has_below))
    def _():
        wu_below[...] = jnp.zeros((tile, tile), jnp.float32)
        level_recv[:, 1] = jnp.zeros((SUBSTEPS, 8, tile), jnp.float32)

    @pl.when(jnp.logical_not(has_above))
    def _():
        level_recv[:, 0] = jnp.zeros((SUBSTEPS, 8, tile), jnp.float32)

    for load in loads[:3]:
        load.wait()
    take_strips()
    pl.semaphore_wait(
        barrier, n_px - 1 + len(beside) + has_above.astype(jnp.int32) + has_below.astype(jnp.int32)
    )
    send_rims(0)

    @pl.when(has_above)
    def _():
        wub_copy().start()
        plane_copy(0, 1, True).start()

    @pl.when(has_below)
    def _():
        plane_copy(0, 0, True).start()

    for load in loads[3:]:
        load.wait()
    columns([st[j] for j in range(levels)], [])
    for s, (a, b) in ((0, (0, 1)), (2, (last, last - 1))):
        st_strips[s, :levels] = st[:, a, :]
        st_strips[s, levels:] = st[:, b, :]
    for s, (a, b) in ((1, (2, 3)), (3, (1, 0))):
        st_strips[s, :levels] = column(a)
        st_strips[s, levels:] = column(b)
    slot_count = payload_first.shape[2]
    top = levels - 1
    every = tuple(range(levels))
    stages = (
        (picked_early, ((0, 0, top),), [(wu, l) for l in every[:top]]),
        (picked_first, ((1, 0, levels), (2, levels, levels + 1)), [(we, l) for l in every] + [(wu, top)]),
        (picked_second, ((3, 0, levels),), [(wn, l) for l in every]),
        (picked_third, ((4, 0, levels),), [(p, l) for l in every]),
    )
    capacity = pick_hot.shape[1]
    packed = capacity < n_px * slot_count
    find_slots(n_px, slot_count, packed, owner, source, weight, slot_source, slot_weight)
    steps = (capacity // LANES - 1).bit_length()
    if packed:
        filled = [
            jnp.sum(jnp.sum((owner[...] == o).astype(jnp.int32), axis=0, keepdims=True), axis=1, keepdims=True)
            for o in range(n_px)
        ]

    def part_of(o, found, low, high):
        if not packed:
            return found[low:high, pl.ds(pl.multiple_of(o * slot_count, LANES), slot_count)]
        start, count = jnp.zeros((1, 1), jnp.int32), jnp.zeros((1, 1), jnp.int32)
        for k, n in enumerate(filled):
            start = start + jnp.where(k < o, (n + (LANES - 1)) >> 7, 0)
            count = count + jnp.where(k == o, n, 0)
        part = found[low:high, :]
        for k in reversed(range(steps)):
            width = slot_count + ((1 << k) - 1) * LANES
            part = jnp.where(
                ((start >> k) & 1) == 1, part[:, LANES << k : (LANES << k) + width], part[:, :width]
            )
        return jnp.where(iota(part.shape, 1) < count, part, 0.0)

    def ahead(d):
        return lax.rem(ix + d + 1, n_px)

    def hand_over(k):
        found, parts, planes = stages[k]
        first = sum(len(stage[2]) for stage in stages[:k])
        for n, (field, l) in enumerate(planes):
            split_plane(split, field[l], first + n)
        pick(first, split, pick_hot, pick_mask, found)

        def lay_out(o):
            whole = part_of(o, found, 0, len(planes))
            for c, low, high in parts:
                payload[c][o] = whole[low:high]

        def send(d, carry):
            lay_out(ahead(d))
            for c, _, _ in parts:
                give_copy(c, ahead(d)).start()
            return carry

        lax.fori_loop(0, n_px - 1, send, 0)
        lay_out(ix)

    def substep(t, carry):
        for j in range(levels):
            we[j] = we[j] - A * d_rows(p[j])
            wn[j] = wn[j] - A * d_lanes(p[j])
        for j in range(levels - 1):
            wu[j] = wu[j] - B * (p[j + 1] - p[j])

        @pl.when(has_above)
        def _():
            wu[levels - 1] = wu[levels - 1] + B * p[levels - 1]

        @pl.when(jnp.logical_not(has_above))
        def _():
            wu[levels - 1] = jnp.zeros((tile, tile), jnp.float32)

        for j in range(1, levels):
            p[j] = p[j] - st[j] * (A * (d_rows(we[j]) + d_lanes(wn[j])) + B * (wu[j] - wu[j - 1]))

        @pl.when(has_below & (t == 0))
        def _():
            wub_copy().wait_recv()

        @pl.when(has_below)
        def _():
            wu_below[...] = wu_below[...] - B * p[0]

        p[0] = p[0] - st[0] * (A * (d_rows(we[0]) + d_lanes(wn[0])) + B * (wu[0] - wu_below[...]))
        take_strips()

        @pl.when(t == 1)
        def _():
            pick_tables(slot_source, slot_weight, pick_hot, pick_mask)
            if packed:
                for found, _, planes in stages:
                    found[:, capacity:] = jnp.zeros((len(planes), found.shape[1] - capacity), jnp.float32)

        @pl.when(t == 2)
        def _():
            land_tables(cell, land_hot)
            total[...] = jnp.zeros(total.shape, jnp.float32)

        @pl.when(t == SUBSTEPS - 1)
        def _():
            hand_over(0)

        next_strips(t)

        @pl.when(t < SUBSTEPS - 1)
        def _():
            send_rims(t + 1)

        @pl.when(has_above)
        def _():
            plane_copy(t, 0).wait_recv()
            wu[levels - 1] = wu[levels - 1] - B * plane_recv[t, 0]
            p[levels - 1] = p[levels - 1] + (B * B) * (st[levels - 1] * plane_recv[t, 0])

        @pl.when(has_below)
        def _():
            plane_copy(t, 1).wait_recv()
            wu_below[...] = wu_below[...] + B * plane_recv[t, 1]
            p[0] = p[0] + (B * B) * (st[0] * plane_recv[t, 1])

        for s, (a, b) in ((0, (0, 1)), (2, (last, last - 1))):
            p[:, a, :] = p_strips[s, :levels]
            p[:, b, :] = p_strips[s, levels:]
            we[:, a, :] = w_strips[s, :levels]
        for k, (s, half) in enumerate(((3, 1), (3, 0), (1, 0), (1, 1))):
            ghost_rows[pl.ds(k, levels, stride=4), :] = p_strips[s, half * levels : (half + 1) * levels]
        for k, s in enumerate((3, 1)):
            ghost_rows[pl.ds(4 * levels + k, levels, stride=2), :] = w_strips[s, :levels]
        turned = ghost_rows[...].T
        rim = (lane == 0) | (lane == last)
        band = (lane <= 1) | (lane >= last - 1)
        for j in range(levels):
            p[j] = jnp.where(band, pltpu.roll(turned, (tile - 4 * j - 2) % tile, 1), p[j])
            wn[j] = jnp.where(rim, pltpu.roll(turned, (tile - 4 * levels - 2 * j - 1) % tile, 1), wn[j])

        @pl.when((t < SUBSTEPS - 1) & has_above)
        def _():
            plane_send[t + 1, 1] = p[levels - 1]
            plane_copy(t + 1, 1).start()

        @pl.when((t < SUBSTEPS - 1) & has_below)
        def _():
            plane_send[t + 1, 0] = p[0]
            plane_copy(t + 1, 0).start()

        return carry

    lax.fori_loop(0, SUBSTEPS, substep, 0)

    for k in range(1, len(stages)):
        hand_over(k)

    groups = latlon.shape[2] // BLOCK
    sums = ((3, (0, 2)), (1, (1,)), (2, (3,)), (0, (4,)))

    for q, parts in sums:
        land(q, [payload[c][ix] for c in parts], cell, land_hot, ix, total)

    for q, parts in sums:

        def bring_in(d, carry):
            o = lax.rem(ix + n_px - d - 1, n_px)
            for c in parts:
                got(c, o).wait_recv()
            land(q, [arrived[c][o] for c in parts], cell, land_hot, o, total)
            return carry

        lax.fori_loop(0, n_px - 1, bring_in, 0)
        for g in range(groups):
            high, low = g * levels, (groups + g) * levels
            latlon[q, :, g * BLOCK : (g + 1) * BLOCK] = total[q, high : high + levels] + total[q, low : low + levels]

    def drain(t, carry):
        for s in range(4):
            near_copy(t, s).wait_send()
            diag_copy(t, s).wait_send()
            far_copy(t, s).wait_send()

        @pl.when(has_above)
        def _():
            level_copy(t, 1).wait_send()
            plane_copy(t, 1).wait_send()

        @pl.when(has_below)
        def _():
            level_copy(t, 0).wait_send()
            plane_copy(t, 0).wait_send()

        return carry

    lax.fori_loop(0, SUBSTEPS, drain, 0)

    @pl.when(has_above)
    def _():
        wub_copy().wait_send()

    def sent(d, carry):
        for c in range(len(payload)):
            give_copy(c, ahead(d)).wait_send()
        return carry

    lax.fori_loop(0, n_px - 1, sent, 0)


def find_slots(owner_count, slot_count, packed, owner, source, weight, slot_source, slot_weight):
    rows = owner.shape[0]
    slot_rows = slot_source.shape[0]
    names = owner[...]
    up_to = (iota((LANES, LANES), 0) <= iota((LANES, LANES), 1)).astype(jnp.bfloat16)
    ones = jnp.ones((LANES, LANES), jnp.bfloat16)
    before = (iota((rows, rows), 0) > iota((rows, rows), 1)).astype(jnp.bfloat16)

    def count(o, carry):
        place, start = carry
        named = names == o
        hot = named.astype(jnp.float32).astype(jnp.bfloat16)
        within = jnp.dot(hot, up_to, preferred_element_type=jnp.float32)
        total = jnp.dot(hot, ones, preferred_element_type=jnp.float32)
        earlier = jnp.dot(before, total.astype(jnp.bfloat16), preferred_element_type=jnp.float32)
        place = jnp.where(named, within + earlier - 1.0 + start, place)
        if packed:
            filled = jnp.sum(total, axis=0, keepdims=True)
            start = start + jnp.floor((filled + (LANES - 1.0)) / LANES) * LANES
        else:
            start = start + float(slot_count)
        return place, start

    zero = jnp.zeros(names.shape, jnp.float32)
    place, _ = lax.fori_loop(0, owner_count, count, (zero, jnp.zeros((1, LANES), jnp.float32)))
    slot = place.astype(jnp.int32)
    slot_high, slot_low = slot >> 7, slot & (LANES - 1)
    src = source[...]
    w = weight[...]
    w1 = w.astype(jnp.bfloat16).astype(jnp.float32)
    w2 = (w - w1).astype(jnp.bfloat16).astype(jnp.float32)
    w3 = w - w1 - w2
    pieces = [(src >> 7).astype(jnp.float32), (src & (LANES - 1)).astype(jnp.float32), w1, w2, w3]
    high_place, low_place = iota((slot_rows, LANES), 0), iota((LANES, LANES), 0)
    total = jnp.zeros((len(pieces) * slot_rows, LANES), jnp.float32)
    for r in range(rows):
        here = high_place == slot_high[r : r + 1]
        left = jnp.concatenate([jnp.where(here, piece[r : r + 1], 0.0) for piece in pieces], axis=0)
        right = jnp.where(low_place == slot_low[r : r + 1], 1.0, 0.0)
        total += dot_nt(left.astype(jnp.bfloat16), right.astype(jnp.bfloat16))
    part = [total[k * slot_rows : (k + 1) * slot_rows] for k in range(len(pieces))]
    slot_source[...] = (part[0] * LANES + part[1]).astype(jnp.int32)
    slot_weight[...] = part[2] + part[3] + part[4]


def split_plane(split, plane, r):
    tile = plane.shape[0]
    half = tile // 2
    h, d = parts2(plane.T)
    for k, part in enumerate((h[:half], h[half:], d[:half], d[half:])):
        split[r * half : (r + 1) * half, k * tile : (k + 1) * tile] = part


def joined(ref, row, pieces):
    return jnp.concatenate([ref[pl.ds(row + k, 1), :] for k in range(pieces)], axis=1)


def pick_tables(slot_source, slot_weight, pick_hot, pick_mask):
    lines, capacity = pick_hot.shape
    tile, half = lines // 2, pick_mask.shape[0]
    pieces = BLOCK // LANES

    def step(b, carry):
        at = pl.ds(pl.multiple_of(b * BLOCK, BLOCK), BLOCK)
        src, w = joined(slot_source, b * pieces, pieces), joined(slot_weight, b * pieces, pieces)
        x, y = src >> 7, src & (tile - 1)
        line = x + jnp.where(y >= half, tile, 0)
        pick_hot[:, at] = jnp.where(iota((lines, BLOCK), 0) == line, 1.0, 0.0).astype(jnp.bfloat16)
        pick_mask[:, at] = jnp.where(iota((half, BLOCK), 0) == (y & (half - 1)), w, 0.0)
        return carry

    lax.fori_loop(0, capacity // BLOCK, step, 0)


def pick(first, split, pick_hot, pick_mask, found):
    rows = found.shape[0]
    half, capacity = pick_mask.shape
    lines = slice(first * half, (first + rows) * half)
    width = 2 * BLOCK if capacity % (2 * BLOCK) == 0 else BLOCK
    steps = capacity // width

    def step(b, carry):
        at = pl.ds(pl.multiple_of(b * width, width), width)
        hot = pick_hot[:, at]
        line = jnp.dot(
            split[lines, :], jnp.concatenate([hot, hot], axis=0), preferred_element_type=jnp.float32
        )
        found[:, at] = jnp.sum(line.reshape(rows, half, width) * pick_mask[:, at][None], axis=1)
        return carry

    lax.fori_loop(0, steps, step, 0, unroll=steps if steps < 12 else 4)


def land_tables(cell, land_hot):
    owner_count, _, slot_count = land_hot.shape
    pieces = slot_count // LANES

    def step(o, carry):
        c = joined(cell, o * pieces, pieces)
        hot = jnp.where(iota((BLOCK, slot_count), 0) == (c & (BLOCK - 1)), 1.0, 0.0)
        land_hot[o] = hot.astype(jnp.bfloat16)
        return carry

    lax.fori_loop(0, owner_count, step, 0)


def land(q, parts, cell, land_hot, o, total):
    values = parts[0] if len(parts) == 1 else jnp.concatenate(parts, axis=0)
    rows, slot_count = values.shape
    groups = total.shape[1] // (2 * rows)
    pieces = slot_count // LANES
    group = joined(cell, o * pieces, pieces) >> 8
    h = values.astype(jnp.bfloat16).astype(jnp.float32)
    spread = [jnp.where(group == g, h, 0.0) for g in range(groups)]
    spread += [jnp.where(group == g, values - h, 0.0) for g in range(groups)]
    total[q] += dot_nt(jnp.concatenate(spread, axis=0).astype(jnp.bfloat16), land_hot[o])


def per_device(
    sizes,
    pressure,
    wind_east,
    wind_north,
    wind_up,
    stiffness,
    edge_table,
    remap_source,
    remap_weight,
    remap_owner,
    latlon_cell,
):
    levels, tile, _ = pressure.shape
    owner_count = sizes[0]
    slots = latlon_cell.shape[0]
    slot_count = slots // owner_count
    cell_count = tile * tile // 8
    count = 4 * levels
    entries = remap_source.shape[0]
    rows = entries // LANES
    capacity = -(-(entries + (owner_count - 1) * (LANES - 1)) // BLOCK) * BLOCK
    capacity = min(capacity, slots)
    room = capacity
    if capacity < slots:
        room = slot_count + ((2 << (capacity // LANES - 1).bit_length() - 1) - 1) * LANES + LANES
        room = max(room, capacity)
    slot_rows = -(-capacity // (8 * LANES)) * 8
    part_rows = (levels - 1, levels, 1, levels, levels)
    f32, i32 = jnp.float32, jnp.int32
    n = SUBSTEPS
    field = pltpu.VMEM(pressure.shape, f32)
    plane = pltpu.VMEM((tile, tile), f32)
    dma = pltpu.SemaphoreType.DMA
    in_vmem = pl.BlockSpec(memory_space=pltpu.VMEM)
    return pl.pallas_call(
        functools.partial(whole_kernel, sizes),
        out_shape=[
            pltpu.VMEM(pressure.shape, f32),
            pltpu.VMEM((4, levels, cell_count), f32),
        ],
        in_specs=[pl.BlockSpec(memory_space=pltpu.SMEM)] + [pl.BlockSpec(memory_space=pl.ANY)] * 9,
        out_specs=[in_vmem] * 2,
        scratch_shapes=[
            field,
            field,
            field,
            field,
            pltpu.VMEM((rows, LANES), i32),
            pltpu.VMEM((rows, LANES), i32),
            pltpu.VMEM((rows, LANES), f32),
            pltpu.VMEM((slots // LANES, LANES), i32),
            pltpu.VMEM((8, 2 * levels, tile), f32),
            pltpu.VMEM((n, 4, 2 * levels, tile), f32),
            pltpu.VMEM((n, 4, 2 * levels, tile), f32),
            pltpu.VMEM((n, 4, 2 * levels, tile), f32),
            pltpu.VMEM((n, 4, 2 * levels, tile), f32),
            pltpu.VMEM((n, 4, levels, tile), f32),
            pltpu.VMEM((n, 4, levels, tile), f32),
            pltpu.VMEM((4, levels, tile), f32),
            pltpu.VMEM((n, 2, 8, tile), f32),
            pltpu.VMEM((n, 2, 8, tile), f32),
            pltpu.VMEM((n, 2, tile, tile), f32),
            pltpu.VMEM((n, 2, tile, tile), f32),
            plane,
            plane,
            plane,
            pltpu.VMEM((4, 2 * levels, tile), f32),
            pltpu.VMEM((4, 2 * levels, tile), f32),
            pltpu.VMEM((4, 2 * levels, tile), f32),
            pltpu.VMEM((slot_rows, LANES), i32),
            pltpu.VMEM((slot_rows, LANES), f32),
            pltpu.VMEM((2 * tile, capacity), jnp.bfloat16),
            pltpu.VMEM((tile // 2, capacity), f32),
            pltpu.VMEM((owner_count, BLOCK, slot_count), jnp.bfloat16),
            pltpu.VMEM((count * tile // 2, 4 * tile), jnp.bfloat16),
            *(pltpu.VMEM((n_rows, room), f32) for n_rows in (levels - 1, levels + 1, levels, levels)),
            *(pltpu.VMEM((owner_count, n_rows, slot_count), f32) for n_rows in part_rows),
            *(pltpu.VMEM((owner_count, n_rows, slot_count), f32) for n_rows in part_rows),
            pltpu.VMEM((4, 2 * levels * (cell_count // BLOCK), BLOCK), f32),
            dma((9,)),
            dma((2, n, 4)),
            dma((2, n, 4)),
            dma((2, n, 4)),
            dma((2, n, 2)),
            dma((2, n, 2)),
            dma((2, 1)),
            dma((len(part_rows), owner_count)),
            dma((len(part_rows), owner_count)),
        ],
        compiler_params=pltpu.CompilerParams(
            collective_id=0, has_side_effects=True, vmem_limit_bytes=60 * 2**20
        ),
    )(
        edge_table,
        pressure,
        wind_east,
        wind_north,
        wind_up,
        stiffness,
        remap_owner.reshape(rows, LANES),
        remap_source.reshape(rows, LANES),
        remap_weight.reshape(rows, LANES),
        latlon_cell.reshape(slots // LANES, LANES),
    )


def solution(mesh):
    field = P("lev", "px", "py")
    entries = P(("px", "py"))
    sizes = (mesh.shape["px"], mesh.shape["py"], mesh.shape["lev"])
    return jax.shard_map(
        functools.partial(per_device, sizes),
        mesh=mesh,
        in_specs=(field,) * 5 + (P(), entries, entries, P(("px", "py"), None), entries),
        out_specs=(field, P(None, "lev", ("px", "py"))),
        check_vma=False,
    )
```

```python
import functools

import jax
import jax.numpy as jnp
from jax import lax
from jax.experimental import pallas as pl
from jax.experimental.pallas import tpu as pltpu
from jax.sharding import PartitionSpec as P

SUBSTEPS = 4
A = 0.45
B = 0.3
LANES = 128
BLOCK = 256
EARLY = 2
MESH = pl.DeviceIdType.MESH


def iota(shape, dim):
    return lax.broadcasted_iota(jnp.int32, shape, dim)


def parts2(x):
    high = x.astype(jnp.bfloat16)
    return high, (x - high.astype(jnp.float32)).astype(jnp.bfloat16)


def dot_nt(a, b):
    return lax.dot_general(a, b, (((1,), (1,)), ((), ())), preferred_element_type=jnp.float32)


def opposite(s):
    return (s + 2) & 3


SHIFT = ((-1, 0), (0, -1), (1, 0), (0, 1))
DIAGONAL = ((0, 1), (0, 3), (2, 1), (2, 3))


def whole_kernel(
    sizes,
    edges_in,
    p_in,
    we_in,
    wn_in,
    wu_in,
    st_in,
    owner_in,
    source_in,
    weight_in,
    cell_in,
    p,
    latlon,
    edges,
    we,
    wn,
    wu,
    st,
    owner,
    source,
    weight,
    cell,
    table,
    near_send,
    near_recv,
    diag_send,
    diag_recv,
    far_send,
    far_recv,
    own_relay,
    level_send,
    level_recv,
    plane_send,
    plane_recv,
    wu_below,
    flipped_cols,
    ghost_rows,
    p_strips,
    w_strips,
    st_strips,
    rim_change,
    slot_source,
    slot_weight,
    pick_hot,
    pick_mask,
    land_hot,
    split,
    picked_early,
    picked_first,
    picked_second,
    picked_third,
    payload_early,
    payload_first,
    payload_top,
    payload_second,
    payload_third,
    arrived_early,
    arrived_first,
    arrived_top,
    arrived_second,
    arrived_third,
    total,
    in_sems,
    near_sems,
    diag_sems,
    far_sems,
    level_sems,
    plane_sems,
    wub_sems,
    give_sem,
    take_sem,
):
    n_px, n_py, n_lev = sizes
    levels, tile, _ = p.shape
    last = tile - 1
    ix, iy, iz = lax.axis_index("px"), lax.axis_index("py"), lax.axis_index("lev")
    has_above, has_below = iz < n_lev - 1, iz > 0
    payload = (payload_early, payload_first, payload_top, payload_second, payload_third)
    arrived = (arrived_early, arrived_first, arrived_top, arrived_second, arrived_third)

    def place(dx, dy):
        return lax.rem(ix + dx + 2 * n_px, n_px), lax.rem(iy + dy + 2 * n_py, n_py)

    def at(dx, dy):
        x, y = place(dx, dy)
        return {"px": x, "py": y}

    others = {(d, 0) for d in range(1, n_px)}
    for dx, dy in ((0, 1), (0, -1), (0, 2), (0, -2), (1, 1), (1, -1), (-1, 1), (-1, -1)):
        others.add((dx % n_px, dy % n_py))
    beside = sorted(o for o in others if o[1])

    barrier = pltpu.get_barrier_semaphore()
    for dx, dy in beside:
        pl.semaphore_signal(barrier, inc=1, device_id=at(dx, dy), device_id_type=MESH)

    def greet(d, carry):
        pl.semaphore_signal(barrier, inc=1, device_id={"px": lax.rem(ix + d, n_px)}, device_id_type=MESH)
        return carry

    lax.fori_loop(1, n_px, greet, 0)

    @pl.when(has_above)
    def _():
        pl.semaphore_signal(barrier, inc=1, device_id={"lev": iz + 1}, device_id_type=MESH)

    @pl.when(has_below)
    def _():
        pl.semaphore_signal(barrier, inc=1, device_id={"lev": iz - 1}, device_id_type=MESH)

    loads = [
        pltpu.make_async_copy(src, dst, in_sems.at[k])
        for k, (src, dst) in enumerate(
            (
                (edges_in, edges),
                (p_in, p),
                (we_in, we),
                (wn_in, wn),
                (st_in, st),
                (wu_in, wu),
                (owner_in, owner),
                (source_in, source),
                (weight_in, weight),
                (cell_in, cell),
            )
        )
    ]
    for load in loads:
        load.start()
    def remote(src, dst, sems, index, device):
        return pltpu.make_async_remote_copy(
            src_ref=src,
            dst_ref=dst,
            send_sem=sems.at[(0,) + index],
            recv_sem=sems.at[(1,) + index],
            device_id=device,
            device_id_type=MESH,
        )

    def near_copy(t, s):
        dx, dy = SHIFT[s]
        return remote(near_send.at[t, s], near_recv.at[t, s], near_sems, (t, s), at(-dx, -dy))

    def diag_copy(t, k):
        (ax, ay), (bx, by) = SHIFT[DIAGONAL[k][0]], SHIFT[DIAGONAL[k][1]]
        return remote(diag_send.at[t, k], diag_recv.at[t, k], diag_sems, (t, k), at(-ax - bx, -ay - by))

    def far_copy(t, s):
        dx, dy = SHIFT[s]
        return remote(far_send.at[t, s], far_recv.at[t, s], far_sems, (t, s), at(-2 * dx, -2 * dy))

    def level_copy(t, up):
        return remote(
            level_send.at[t, up],
            level_recv.at[t, up],
            level_sems,
            (t, up),
            {"lev": iz + 1 if up else iz - 1},
        )

    def plane_copy(t, up, first=False):
        src = p_in.at[levels - 1 if up else 0] if first else plane_send.at[t, up]
        return remote(src, plane_recv.at[t, up], plane_sems, (t, up), {"lev": iz + 1 if up else iz - 1})

    def wub_copy():
        return remote(wu_in.at[levels - 1], wu_below, wub_sems, (0,), {"lev": iz + 1})

    row, lane = iota((tile, tile), 0), iota((tile, tile), 1)
    strip_row, strip_lane = iota((2 * levels, tile), 0), iota((2 * levels, tile), 1)
    outer = strip_row < levels

    def d_rows(f):
        return jnp.where(row == last, 0.0, pltpu.roll(f, last, 0)) - jnp.where(
            row == 0, 0.0, pltpu.roll(f, 1, 0)
        )

    def d_lanes(f):
        return jnp.where(lane == last, 0.0, pltpu.roll(f, last, 1)) - jnp.where(
            lane == 0, 0.0, pltpu.roll(f, 1, 1)
        )

    def columns(deep, shallow):
        packed = jnp.zeros((tile, tile), jnp.float32)
        for j, f in enumerate(deep):
            packed = jnp.where((lane >> 2) == j, pltpu.roll(f, 4 * j + 2, 1), packed)
        base = 4 * len(deep)
        for j, f in enumerate(shallow):
            packed = jnp.where((lane >> 1) == base // 2 + j, pltpu.roll(f, base + 2 * j + 1, 1), packed)
        flipped_cols[...] = packed.T

    def column(k):
        return flipped_cols[pl.ds(k, levels, stride=4), :]

    def rim_column(k):
        return flipped_cols[pl.ds(4 * levels + k, levels, stride=2), :]

    def take_strips():
        columns([p[j] for j in range(levels)], [wn[j] for j in range(levels)])
        for s, (a, b) in ((0, (0, 1)), (2, (last, last - 1))):
            p_strips[s, :levels] = p[:, a, :]
            p_strips[s, levels:] = p[:, b, :]
            w_strips[s, :levels] = we[:, a, :]
        for s, (a, b, c) in ((1, (2, 3, 1)), (3, (1, 0, 0))):
            p_strips[s, :levels] = column(a)
            p_strips[s, levels:] = column(b)
            w_strips[s, :levels] = rim_column(c)

    def code(x, y, s):
        c = edges[x, y, s]
        return c & 3, c >> 2

    def wanted(s, turn):
        return (s + 2 + turn) & 3

    def sign(s, turn):
        plus = ((turn + 1) & 3) < 2 if s % 2 == 0 else turn < 2
        return jnp.where(plus, 1.0, -1.0) * (1.0 if s < 2 else -1.0)

    def rim_sign(w):
        return jnp.where(w < 2, 1.0, -1.0) if not isinstance(w, int) else (1.0 if w < 2 else -1.0)

    loads[0].wait()
    near_plan = []
    for s in range(4):
        dx, dy = SHIFT[s]
        turn, flip = code(*place(-dx, -dy), s)
        near_plan.append((flip * 4 + wanted(s, turn), sign(s, turn)))

    def relay_plan(s, w, ax, ay):
        turn_a, flip_a = code(*place(ax, ay), s)
        turn_b, flip_b = code(*place(ax + SHIFT[s][0], ay + SHIFT[s][1]), w)
        return (flip_a ^ flip_b) * 4 + wanted(w, turn_b), sign(s, turn_a) * rim_sign(w)

    def relay_to(s, w):
        return relay_plan(s, w, -SHIFT[s][0] - SHIFT[w][0], -SHIFT[s][1] - SHIFT[w][1])

    diag_plan = [(relay_to(a, b), relay_to(b, a)) for a, b in DIAGONAL]
    far_plan = [relay_to(s, s) for s in range(4)]
    own_plan = [relay_to(s, opposite(s)) for s in range(4)]
    mine = [wanted(s, code(ix, iy, s)[0]) for s in range(4)]

    def relayed(t, s):
        found = own_relay[s]
        for k, (a, b) in enumerate(DIAGONAL):
            if s == a:
                found = jnp.where(mine[s] == b, diag_recv[t, k, :levels], found)
            if s == b:
                found = jnp.where(mine[s] == a, diag_recv[t, k, levels:], found)
        return jnp.where(mine[s] == s, far_recv[t, s], found)

    def send_rims(t):
        strips = [p_strips[s] for s in range(4)]
        rims = []
        for s in range(4):
            turned = A * pltpu.roll(strips[s], levels, 0)
            rims.append(jnp.where(outer, w_strips[s] - rim_sign(s) * turned, turned))
        for s in range(4):
            table[s] = rims[s]
            table[4 + s] = jnp.take_along_axis(rims[s], last - strip_lane, axis=1)
        for s in range(4):
            k, sgn = near_plan[s]
            rim = table[k]
            near_send[t, s] = jnp.where(outer, sgn * rim, rim)
            near_copy(t, s).start()
        for k in range(4):
            for half in range(2):
                which, sgn = diag_plan[k][half]
                diag_send[t, k, half * levels : (half + 1) * levels] = sgn * table[which, levels:]
            diag_copy(t, k).start()
        for s in range(4):
            k, sgn = far_plan[s]
            far_send[t, s] = sgn * table[k, levels:]
            far_copy(t, s).start()
        for s in range(4):
            k, sgn = own_plan[s]
            own_relay[s] = sgn * table[k, levels:]
            for up, level in ((1, levels - 1), (0, 0)):
                level_send[t, up, 2 * s : 2 * s + 2] = p_strips[s, pl.ds(level, 2, stride=levels), :]

        @pl.when(has_above)
        def _():
            level_copy(t, 1).start()

        @pl.when(has_below)
        def _():
            level_copy(t, 0).start()

    def corners(s, low, high):
        found = jnp.zeros((2 * levels, tile), jnp.float32)
        for depth in range(2):
            start = depth if s < 2 else last - depth
            for e in range(2):
                for pair, end in ((low, e), (high, last - e)):
                    moved = pltpu.roll(pair[depth ^ e], (end - start) % tile, 1) if end != start else pair[depth ^ e]
                    here = (strip_lane == end) & (outer if depth == 0 else jnp.logical_not(outer))
                    found = jnp.where(here, moved, found)
        return found

    def next_strips(t):
        for s in range(4):
            near_copy(t, s).wait_recv()
        for k in range(4):
            diag_copy(t, k).wait_recv()
        for s in range(4):
            far_copy(t, s).wait_recv()

        @pl.when(has_above)
        def _():
            level_copy(t, 0).wait_recv()

        @pl.when(has_below)
        def _():
            level_copy(t, 1).wait_recv()

        zero = jnp.zeros((levels, tile), jnp.float32)
        ghosts = []
        for s in range(4):
            ghosts.append(near_recv[t, s] + jnp.concatenate([relayed(t, s), zero], axis=0))
        pairs = [(g, pltpu.roll(g, levels, 0)) for g in ghosts]
        for s in range(2):
            rim_change[s] = jnp.where(outer, pairs[s][1], -ghosts[s + 2])
        for s in range(4):
            low, high = (pairs[1], pairs[3]) if s % 2 == 0 else (pairs[0], pairs[2])
            across = jnp.zeros((2 * levels, tile), jnp.float32)
            for depth in range(2):
                below, above = level_recv[t, 1], level_recv[t, 0]
                k = 2 * s + depth
                across = jnp.where(strip_row == depth * levels, below[k : k + 1], across)
                across = across + jnp.where(strip_row == (depth + 1) * levels - 1, above[k : k + 1], 0.0)
            p_strips[s] = p_strips[s] + st_strips[s] * (
                A * (ghosts[s] + corners(s, low, high)) + (B * B) * across
            )
            w_strips[s] = jnp.where(outer, w_strips[s] + rim_sign(s) * pairs[s][1], 0.0)

    def give_copy(c, o):
        return pltpu.make_async_remote_copy(
            src_ref=payload[c].at[o],
            dst_ref=arrived[c].at[ix],
            send_sem=give_sem.at[c, o],
            recv_sem=take_sem.at[c, ix],
            device_id={"px": o},
            device_id_type=MESH,
        )

    def got(c, o):
        return pltpu.make_async_remote_copy(
            src_ref=payload[c].at[o],
            dst_ref=arrived[c].at[o],
            send_sem=give_sem.at[c, o],
            recv_sem=take_sem.at[c, o],
            device_id={"px": o},
            device_id_type=MESH,
        )

    w_strips[...] = jnp.zeros(w_strips.shape, jnp.float32)
    ghost_rows[...] = jnp.zeros((tile, tile), jnp.float32)

    @pl.when(jnp.logical_not(has_below))
    def _():
        wu_below[...] = jnp.zeros((tile, tile), jnp.float32)
        level_recv[:, 1] = jnp.zeros((SUBSTEPS, 8, tile), jnp.float32)

    @pl.when(jnp.logical_not(has_above))
    def _():
        level_recv[:, 0] = jnp.zeros((SUBSTEPS, 8, tile), jnp.float32)

    for load in loads[1:4]:
        load.wait()
    take_strips()
    pl.semaphore_wait(
        barrier, n_px - 1 + len(beside) + has_above.astype(jnp.int32) + has_below.astype(jnp.int32)
    )
    send_rims(0)

    @pl.when(has_above)
    def _():
        wub_copy().start()
        plane_copy(0, 1, True).start()

    @pl.when(has_below)
    def _():
        plane_copy(0, 0, True).start()

    for load in loads[4:]:
        load.wait()
    columns([st[j] for j in range(levels)], [])
    for s, (a, b) in ((0, (0, 1)), (2, (last, last - 1))):
        st_strips[s, :levels] = st[:, a, :]
        st_strips[s, levels:] = st[:, b, :]
    for s, (a, b) in ((1, (2, 3)), (3, (1, 0))):
        st_strips[s, :levels] = column(a)
        st_strips[s, levels:] = column(b)
    slot_count = payload_first.shape[2]
    top = levels - 1
    every = tuple(range(levels))
    stages = (
        (picked_early, ((0, 0, top),), [(wu, l) for l in every[:top]]),
        (picked_first, ((1, 0, levels),), [(we, l) for l in every]),
        (picked_second, ((3, 0, levels), (2, levels, levels + 1)), [(wn, l) for l in every] + [(wu, top)]),
        (picked_third, ((4, 0, levels),), [(p, l) for l in every]),
    )
    capacity = pick_hot.shape[1]
    packed = capacity < n_px * slot_count
    find_slots(n_px, slot_count, packed, owner, source, weight, slot_source, slot_weight)
    steps = (capacity // LANES - 1).bit_length()
    if packed:
        filled = [
            jnp.sum(jnp.sum((owner[...] == o).astype(jnp.int32), axis=0, keepdims=True), axis=1, keepdims=True)
            for o in range(n_px)
        ]

    def part_of(o, found, low, high):
        if not packed:
            return found[low:high, pl.ds(pl.multiple_of(o * slot_count, LANES), slot_count)]
        start, count = jnp.zeros((1, 1), jnp.int32), jnp.zeros((1, 1), jnp.int32)
        for k, n in enumerate(filled):
            start = start + jnp.where(k < o, (n + (LANES - 1)) >> 7, 0)
            count = count + jnp.where(k == o, n, 0)
        part = found[low:high, :]
        for k in reversed(range(steps)):
            width = slot_count + ((1 << k) - 1) * LANES
            part = jnp.where(
                ((start >> k) & 1) == 1, part[:, LANES << k : (LANES << k) + width], part[:, :width]
            )
        return jnp.where(iota(part.shape, 1) < count, part, 0.0)

    def ahead(d):
        return lax.rem(ix + d + 1, n_px)

    def choose(k):
        found, _, planes = stages[k]
        first = sum(len(stage[2]) for stage in stages[:k])
        for n, (field, l) in enumerate(planes):
            split_plane(split, field[l], first + n)
        pick(first, split, pick_hot, pick_mask, found)

    def add_rims(k):
        found = stages[k][0]

        def step(b, carry):
            at = pl.ds(pl.multiple_of(b * LANES, LANES), LANES)
            src = jnp.broadcast_to(slot_source[pl.ds(b, 1), :], (2 * levels, LANES))
            across, along = (src >> 7, src & last) if k == 1 else (src & last, src >> 7)
            change = jnp.take_along_axis(rim_change[k - 1], along, axis=1) * slot_weight[pl.ds(b, 1), :]
            change = jnp.where(across == jnp.where(outer, 0, last), change, 0.0)
            found[:, at] = found[:, at] + (change[:levels] + change[levels:])
            return carry

        lax.fori_loop(0, capacity // LANES, step, 0, unroll=4)

    def hand_over(k):
        found, parts, planes = stages[k]

        def lay_out(o):
            whole = part_of(o, found, 0, len(planes))
            for c, low, high in parts:
                payload[c][o] = whole[low:high]

        def send(d, carry):
            lay_out(ahead(d))
            for c, _, _ in parts:
                give_copy(c, ahead(d)).start()
            return carry

        lax.fori_loop(0, n_px - 1, send, 0)
        lay_out(ix)

    def substep(t, carry):
        for j in range(levels):
            we[j] = we[j] - A * d_rows(p[j])
            wn[j] = wn[j] - A * d_lanes(p[j])
        for j in range(levels - 1):
            wu[j] = wu[j] - B * (p[j + 1] - p[j])

        @pl.when(has_above)
        def _():
            wu[levels - 1] = wu[levels - 1] + B * p[levels - 1]

        @pl.when(jnp.logical_not(has_above))
        def _():
            wu[levels - 1] = jnp.zeros((tile, tile), jnp.float32)

        for j in range(1, levels):
            p[j] = p[j] - st[j] * (A * (d_rows(we[j]) + d_lanes(wn[j])) + B * (wu[j] - wu[j - 1]))

        @pl.when(has_below & (t == 0))
        def _():
            wub_copy().wait_recv()

        @pl.when(has_below)
        def _():
            wu_below[...] = wu_below[...] - B * p[0]

        p[0] = p[0] - st[0] * (A * (d_rows(we[0]) + d_lanes(wn[0])) + B * (wu[0] - wu_below[...]))
        take_strips()

        @pl.when(t == 1)
        def _():
            pick_tables(slot_source, slot_weight, pick_hot, pick_mask)
            if packed:
                for found, _, planes in stages:
                    found[:, capacity:] = jnp.zeros((len(planes), found.shape[1] - capacity), jnp.float32)

        @pl.when(t == 2)
        def _():
            land_tables(cell, land_hot)
            total[...] = jnp.zeros(total.shape, jnp.float32)

        @pl.when(t == SUBSTEPS - 1)
        def _():
            choose(0)
            hand_over(0)
            for k in range(1, EARLY):
                choose(k)

        next_strips(t)

        @pl.when(t == SUBSTEPS - 1)
        def _():
            for k in range(1, EARLY):
                add_rims(k)
                hand_over(k)

        @pl.when(t < SUBSTEPS - 1)
        def _():
            send_rims(t + 1)

        @pl.when(has_above)
        def _():
            plane_copy(t, 0).wait_recv()
            wu[levels - 1] = wu[levels - 1] - B * plane_recv[t, 0]
            p[levels - 1] = p[levels - 1] + (B * B) * (st[levels - 1] * plane_recv[t, 0])

        @pl.when(has_below)
        def _():
            plane_copy(t, 1).wait_recv()
            wu_below[...] = wu_below[...] + B * plane_recv[t, 1]
            p[0] = p[0] + (B * B) * (st[0] * plane_recv[t, 1])

        for s, (a, b) in ((0, (0, 1)), (2, (last, last - 1))):
            p[:, a, :] = p_strips[s, :levels]
            p[:, b, :] = p_strips[s, levels:]
            we[:, a, :] = w_strips[s, :levels]
        for k, (s, half) in enumerate(((3, 1), (3, 0), (1, 0), (1, 1))):
            ghost_rows[pl.ds(k, levels, stride=4), :] = p_strips[s, half * levels : (half + 1) * levels]
        for k, s in enumerate((3, 1)):
            ghost_rows[pl.ds(4 * levels + k, levels, stride=2), :] = w_strips[s, :levels]
        turned = ghost_rows[...].T
        rim = (lane == 0) | (lane == last)
        band = (lane <= 1) | (lane >= last - 1)
        for j in range(levels):
            p[j] = jnp.where(band, pltpu.roll(turned, (tile - 4 * j - 2) % tile, 1), p[j])
            wn[j] = jnp.where(rim, pltpu.roll(turned, (tile - 4 * levels - 2 * j - 1) % tile, 1), wn[j])

        @pl.when((t < SUBSTEPS - 1) & has_above)
        def _():
            plane_send[t + 1, 1] = p[levels - 1]
            plane_copy(t + 1, 1).start()

        @pl.when((t < SUBSTEPS - 1) & has_below)
        def _():
            plane_send[t + 1, 0] = p[0]
            plane_copy(t + 1, 0).start()

        return carry

    lax.fori_loop(0, SUBSTEPS, substep, 0)

    for k in range(EARLY, len(stages)):
        choose(k)
        hand_over(k)

    groups = latlon.shape[2] // BLOCK
    sums = ((1, (1,)), (2, (3,)), (3, (0, 2)), (0, (4,)))

    for q, parts in sums:
        land(q, [payload[c][ix] for c in parts], cell, land_hot, ix, total)

    for q, parts in sums:

        def bring_in(d, carry):
            o = lax.rem(ix + n_px - d - 1, n_px)
            for c in parts:
                got(c, o).wait_recv()
            land(q, [arrived[c][o] for c in parts], cell, land_hot, o, total)
            return carry

        lax.fori_loop(0, n_px - 1, bring_in, 0)
        for g in range(groups):
            high, low = g * levels, (groups + g) * levels
            latlon[q, :, g * BLOCK : (g + 1) * BLOCK] = total[q, high : high + levels] + total[q, low : low + levels]

    def drain(t, carry):
        for s in range(4):
            near_copy(t, s).wait_send()
            diag_copy(t, s).wait_send()
            far_copy(t, s).wait_send()

        @pl.when(has_above)
        def _():
            level_copy(t, 1).wait_send()
            plane_copy(t, 1).wait_send()

        @pl.when(has_below)
        def _():
            level_copy(t, 0).wait_send()
            plane_copy(t, 0).wait_send()

        return carry

    lax.fori_loop(0, SUBSTEPS, drain, 0)

    @pl.when(has_above)
    def _():
        wub_copy().wait_send()

    def sent(d, carry):
        for c in range(len(payload)):
            give_copy(c, ahead(d)).wait_send()
        return carry

    lax.fori_loop(0, n_px - 1, sent, 0)


def find_slots(owner_count, slot_count, packed, owner, source, weight, slot_source, slot_weight):
    rows = owner.shape[0]
    slot_rows = slot_source.shape[0]
    names = owner[...]
    up_to = (iota((LANES, LANES), 0) <= iota((LANES, LANES), 1)).astype(jnp.bfloat16)
    ones = jnp.ones((LANES, LANES), jnp.bfloat16)
    before = (iota((rows, rows), 0) > iota((rows, rows), 1)).astype(jnp.bfloat16)

    def count(o, carry):
        place, start = carry
        named = names == o
        hot = named.astype(jnp.float32).astype(jnp.bfloat16)
        within = jnp.dot(hot, up_to, preferred_element_type=jnp.float32)
        total = jnp.dot(hot, ones, preferred_element_type=jnp.float32)
        earlier = jnp.dot(before, total.astype(jnp.bfloat16), preferred_element_type=jnp.float32)
        place = jnp.where(named, within + earlier - 1.0 + start, place)
        if packed:
            filled = jnp.sum(total, axis=0, keepdims=True)
            start = start + jnp.floor((filled + (LANES - 1.0)) / LANES) * LANES
        else:
            start = start + float(slot_count)
        return place, start

    zero = jnp.zeros(names.shape, jnp.float32)
    place, _ = lax.fori_loop(0, owner_count, count, (zero, jnp.zeros((1, LANES), jnp.float32)))
    slot = place.astype(jnp.int32)
    slot_high, slot_low = slot >> 7, slot & (LANES - 1)
    src = source[...]
    w = weight[...]
    w1 = w.astype(jnp.bfloat16).astype(jnp.float32)
    w2 = (w - w1).astype(jnp.bfloat16).astype(jnp.float32)
    w3 = w - w1 - w2
    pieces = [(src >> 7).astype(jnp.float32), (src & (LANES - 1)).astype(jnp.float32), w1, w2, w3]
    high_place, low_place = iota((slot_rows, LANES), 0), iota((LANES, LANES), 0)
    total = jnp.zeros((len(pieces) * slot_rows, LANES), jnp.float32)
    for r in range(rows):
        here = high_place == slot_high[r : r + 1]
        left = jnp.concatenate([jnp.where(here, piece[r : r + 1], 0.0) for piece in pieces], axis=0)
        right = jnp.where(low_place == slot_low[r : r + 1], 1.0, 0.0)
        total += dot_nt(left.astype(jnp.bfloat16), right.astype(jnp.bfloat16))
    part = [total[k * slot_rows : (k + 1) * slot_rows] for k in range(len(pieces))]
    slot_source[...] = (part[0] * LANES + part[1]).astype(jnp.int32)
    slot_weight[...] = part[2] + part[3] + part[4]


def split_plane(split, plane, r):
    tile = plane.shape[0]
    half = tile // 2
    h, d = parts2(plane.T)
    for k, part in enumerate((h[:half], h[half:], d[:half], d[half:])):
        split[r * half : (r + 1) * half, k * tile : (k + 1) * tile] = part


def joined(ref, row, pieces):
    return jnp.concatenate([ref[pl.ds(row + k, 1), :] for k in range(pieces)], axis=1)


def pick_tables(slot_source, slot_weight, pick_hot, pick_mask):
    lines, capacity = pick_hot.shape
    tile, half = lines // 2, pick_mask.shape[0]
    pieces = BLOCK // LANES

    def step(b, carry):
        at = pl.ds(pl.multiple_of(b * BLOCK, BLOCK), BLOCK)
        src, w = joined(slot_source, b * pieces, pieces), joined(slot_weight, b * pieces, pieces)
        x, y = src >> 7, src & (tile - 1)
        line = x + jnp.where(y >= half, tile, 0)
        pick_hot[:, at] = jnp.where(iota((lines, BLOCK), 0) == line, 1.0, 0.0).astype(jnp.bfloat16)
        pick_mask[:, at] = jnp.where(iota((half, BLOCK), 0) == (y & (half - 1)), w, 0.0)
        return carry

    lax.fori_loop(0, capacity // BLOCK, step, 0)


def pick(first, split, pick_hot, pick_mask, found):
    rows = found.shape[0]
    half, capacity = pick_mask.shape
    lines = slice(first * half, (first + rows) * half)
    width = 2 * BLOCK if capacity % (2 * BLOCK) == 0 else BLOCK
    steps = capacity // width

    def step(b, carry):
        at = pl.ds(pl.multiple_of(b * width, width), width)
        hot = pick_hot[:, at]
        line = jnp.dot(
            split[lines, :], jnp.concatenate([hot, hot], axis=0), preferred_element_type=jnp.float32
        )
        found[:, at] = jnp.sum(line.reshape(rows, half, width) * pick_mask[:, at][None], axis=1)
        return carry

    lax.fori_loop(0, steps, step, 0, unroll=steps if steps < 12 else 4)


def land_tables(cell, land_hot):
    owner_count, _, slot_count = land_hot.shape
    pieces = slot_count // LANES

    def step(o, carry):
        c = joined(cell, o * pieces, pieces)
        hot = jnp.where(iota((BLOCK, slot_count), 0) == (c & (BLOCK - 1)), 1.0, 0.0)
        land_hot[o] = hot.astype(jnp.bfloat16)
        return carry

    lax.fori_loop(0, owner_count, step, 0)


def land(q, parts, cell, land_hot, o, total):
    values = parts[0] if len(parts) == 1 else jnp.concatenate(parts, axis=0)
    rows, slot_count = values.shape
    groups = total.shape[1] // (2 * rows)
    pieces = slot_count // LANES
    group = joined(cell, o * pieces, pieces) >> 8
    h = values.astype(jnp.bfloat16).astype(jnp.float32)
    spread = [jnp.where(group == g, h, 0.0) for g in range(groups)]
    spread += [jnp.where(group == g, values - h, 0.0) for g in range(groups)]
    total[q] += dot_nt(jnp.concatenate(spread, axis=0).astype(jnp.bfloat16), land_hot[o])


def per_device(
    sizes,
    pressure,
    wind_east,
    wind_north,
    wind_up,
    stiffness,
    edge_table,
    remap_source,
    remap_weight,
    remap_owner,
    latlon_cell,
):
    levels, tile, _ = pressure.shape
    owner_count = sizes[0]
    slots = latlon_cell.shape[0]
    slot_count = slots // owner_count
    cell_count = tile * tile // 8
    count = 4 * levels
    entries = remap_source.shape[0]
    rows = entries // LANES
    capacity = -(-(entries + (owner_count - 1) * (LANES - 1)) // BLOCK) * BLOCK
    capacity = min(capacity, slots)
    room = capacity
    if capacity < slots:
        room = slot_count + ((2 << (capacity // LANES - 1).bit_length() - 1) - 1) * LANES + LANES
        room = max(room, capacity)
    slot_rows = -(-capacity // (8 * LANES)) * 8
    part_rows = (levels - 1, levels, 1, levels, levels)
    f32, i32 = jnp.float32, jnp.int32
    n = SUBSTEPS
    field = pltpu.VMEM(pressure.shape, f32)
    plane = pltpu.VMEM((tile, tile), f32)
    dma = pltpu.SemaphoreType.DMA
    in_vmem = pl.BlockSpec(memory_space=pltpu.VMEM)
    return pl.pallas_call(
        functools.partial(whole_kernel, sizes),
        out_shape=[
            pltpu.VMEM(pressure.shape, f32),
            pltpu.VMEM((4, levels, cell_count), f32),
        ],
        in_specs=[pl.BlockSpec(memory_space=pl.ANY)] * 10,
        out_specs=[in_vmem] * 2,
        scratch_shapes=[
            pltpu.SMEM(edge_table.shape, i32),
            field,
            field,
            field,
            field,
            pltpu.VMEM((rows, LANES), i32),
            pltpu.VMEM((rows, LANES), i32),
            pltpu.VMEM((rows, LANES), f32),
            pltpu.VMEM((slots // LANES, LANES), i32),
            pltpu.VMEM((8, 2 * levels, tile), f32),
            pltpu.VMEM((n, 4, 2 * levels, tile), f32),
            pltpu.VMEM((n, 4, 2 * levels, tile), f32),
            pltpu.VMEM((n, 4, 2 * levels, tile), f32),
            pltpu.VMEM((n, 4, 2 * levels, tile), f32),
            pltpu.VMEM((n, 4, levels, tile), f32),
            pltpu.VMEM((n, 4, levels, tile), f32),
            pltpu.VMEM((4, levels, tile), f32),
            pltpu.VMEM((n, 2, 8, tile), f32),
            pltpu.VMEM((n, 2, 8, tile), f32),
            pltpu.VMEM((n, 2, tile, tile), f32),
            pltpu.VMEM((n, 2, tile, tile), f32),
            plane,
            plane,
            plane,
            pltpu.VMEM((4, 2 * levels, tile), f32),
            pltpu.VMEM((4, 2 * levels, tile), f32),
            pltpu.VMEM((4, 2 * levels, tile), f32),
            pltpu.VMEM((2, 2 * levels, tile), f32),
            pltpu.VMEM((slot_rows, LANES), i32),
            pltpu.VMEM((slot_rows, LANES), f32),
            pltpu.VMEM((2 * tile, capacity), jnp.bfloat16),
            pltpu.VMEM((tile // 2, capacity), f32),
            pltpu.VMEM((owner_count, BLOCK, slot_count), jnp.bfloat16),
            pltpu.VMEM((count * tile // 2, 4 * tile), jnp.bfloat16),
            *(pltpu.VMEM((n_rows, room), f32) for n_rows in (levels - 1, levels, levels + 1, levels)),
            *(pltpu.VMEM((owner_count, n_rows, slot_count), f32) for n_rows in part_rows),
            *(pltpu.VMEM((owner_count, n_rows, slot_count), f32) for n_rows in part_rows),
            pltpu.VMEM((4, 2 * levels * (cell_count // BLOCK), BLOCK), f32),
            dma((10,)),
            dma((2, n, 4)),
            dma((2, n, 4)),
            dma((2, n, 4)),
            dma((2, n, 2)),
            dma((2, n, 2)),
            dma((2, 1)),
            dma((len(part_rows), owner_count)),
            dma((len(part_rows), owner_count)),
        ],
        compiler_params=pltpu.CompilerParams(
            collective_id=0, has_side_effects=True, vmem_limit_bytes=60 * 2**20
        ),
    )(
        edge_table,
        pressure,
        wind_east,
        wind_north,
        wind_up,
        stiffness,
        remap_owner.reshape(rows, LANES),
        remap_source.reshape(rows, LANES),
        remap_weight.reshape(rows, LANES),
        latlon_cell.reshape(slots // LANES, LANES),
    )


def solution(mesh):
    field = P("lev", "px", "py")
    entries = P(("px", "py"))
    sizes = (mesh.shape["px"], mesh.shape["py"], mesh.shape["lev"])
    return jax.shard_map(
        functools.partial(per_device, sizes),
        mesh=mesh,
        in_specs=(field,) * 5 + (P(), entries, entries, P(("px", "py"), None), entries),
        out_specs=(field, P(None, "lev", ("px", "py"))),
        check_vma=False,
    )
```

```python
import functools

import jax
import jax.numpy as jnp
from jax import lax
from jax.experimental import pallas as pl
from jax.experimental.pallas import tpu as pltpu
from jax.sharding import PartitionSpec as P

SUBSTEPS = 4
A = 0.45
B = 0.3
LANES = 128
BLOCK = 256
EARLY = 2
MESH = pl.DeviceIdType.MESH


def iota(shape, dim):
    return lax.broadcasted_iota(jnp.int32, shape, dim)


def parts2(x):
    high = x.astype(jnp.bfloat16)
    return high, (x - high.astype(jnp.float32)).astype(jnp.bfloat16)


def dot_nt(a, b):
    return lax.dot_general(a, b, (((1,), (1,)), ((), ())), preferred_element_type=jnp.float32)


def opposite(s):
    return (s + 2) & 3


SHIFT = ((-1, 0), (0, -1), (1, 0), (0, 1))
DIAGONAL = ((0, 1), (0, 3), (2, 1), (2, 3))


def whole_kernel(
    sizes,
    edges_in,
    p_in,
    we_in,
    wn_in,
    wu_in,
    st_in,
    owner_in,
    source_in,
    weight_in,
    cell_in,
    p,
    latlon,
    edges,
    we,
    wn,
    wu,
    st,
    owner,
    source,
    weight,
    cell,
    table,
    near_send,
    near_recv,
    diag_send,
    diag_recv,
    far_send,
    far_recv,
    own_relay,
    level_send,
    level_recv,
    plane_send,
    plane_recv,
    wu_below,
    flipped_cols,
    ghost_rows,
    p_strips,
    w_strips,
    st_strips,
    rim_change,
    slot_source,
    slot_weight,
    pick_hot,
    pick_mask,
    land_hot,
    split,
    picked_early,
    picked_first,
    picked_second,
    picked_third,
    payload_early,
    payload_first,
    payload_top,
    payload_second,
    payload_third,
    arrived_early,
    arrived_first,
    arrived_top,
    arrived_second,
    arrived_third,
    total,
    in_sems,
    near_sems,
    diag_sems,
    far_sems,
    level_sems,
    plane_sems,
    wub_sems,
    give_sem,
    take_sem,
):
    n_px, n_py, n_lev = sizes
    levels, tile, _ = p.shape
    last = tile - 1
    ix, iy, iz = lax.axis_index("px"), lax.axis_index("py"), lax.axis_index("lev")
    has_above, has_below = iz < n_lev - 1, iz > 0
    payload = (payload_early, payload_first, payload_top, payload_second, payload_third)
    arrived = (arrived_early, arrived_first, arrived_top, arrived_second, arrived_third)

    def place(dx, dy):
        return lax.rem(ix + dx + 2 * n_px, n_px), lax.rem(iy + dy + 2 * n_py, n_py)

    def at(dx, dy):
        x, y = place(dx, dy)
        return {"px": x, "py": y}

    others = {(d, 0) for d in range(1, n_px)}
    for dx, dy in ((0, 1), (0, -1), (0, 2), (0, -2), (1, 1), (1, -1), (-1, 1), (-1, -1)):
        others.add((dx % n_px, dy % n_py))
    beside = sorted(o for o in others if o[1])

    barrier = pltpu.get_barrier_semaphore()
    for dx, dy in beside:
        pl.semaphore_signal(barrier, inc=1, device_id=at(dx, dy), device_id_type=MESH)

    def greet(d, carry):
        pl.semaphore_signal(barrier, inc=1, device_id={"px": lax.rem(ix + d, n_px)}, device_id_type=MESH)
        return carry

    lax.fori_loop(1, n_px, greet, 0)

    @pl.when(has_above)
    def _():
        pl.semaphore_signal(barrier, inc=1, device_id={"lev": iz + 1}, device_id_type=MESH)

    @pl.when(has_below)
    def _():
        pl.semaphore_signal(barrier, inc=1, device_id={"lev": iz - 1}, device_id_type=MESH)

    loads = [
        pltpu.make_async_copy(src, dst, in_sems.at[k])
        for k, (src, dst) in enumerate(
            (
                (edges_in, edges),
                (p_in, p),
                (we_in, we),
                (wn_in, wn),
                (st_in, st),
                (wu_in, wu),
                (owner_in, owner),
                (source_in, source),
                (weight_in, weight),
                (cell_in, cell),
            )
        )
    ]
    for load in loads:
        load.start()
    def remote(src, dst, sems, index, device):
        return pltpu.make_async_remote_copy(
            src_ref=src,
            dst_ref=dst,
            send_sem=sems.at[(0,) + index],
            recv_sem=sems.at[(1,) + index],
            device_id=device,
            device_id_type=MESH,
        )

    def near_copy(t, s):
        dx, dy = SHIFT[s]
        return remote(near_send.at[t, s], near_recv.at[t, s], near_sems, (t, s), at(-dx, -dy))

    def diag_copy(t, k):
        (ax, ay), (bx, by) = SHIFT[DIAGONAL[k][0]], SHIFT[DIAGONAL[k][1]]
        return remote(diag_send.at[t, k], diag_recv.at[t, k], diag_sems, (t, k), at(-ax - bx, -ay - by))

    def far_copy(t, s):
        dx, dy = SHIFT[s]
        return remote(far_send.at[t, s], far_recv.at[t, s], far_sems, (t, s), at(-2 * dx, -2 * dy))

    def level_copy(t, up):
        return remote(
            level_send.at[t, up],
            level_recv.at[t, up],
            level_sems,
            (t, up),
            {"lev": iz + 1 if up else iz - 1},
        )

    def plane_copy(t, up, first=False):
        src = p_in.at[levels - 1 if up else 0] if first else plane_send.at[t, up]
        return remote(src, plane_recv.at[t, up], plane_sems, (t, up), {"lev": iz + 1 if up else iz - 1})

    def wub_copy():
        return remote(wu_in.at[levels - 1], wu_below, wub_sems, (0,), {"lev": iz + 1})

    row, lane = iota((tile, tile), 0), iota((tile, tile), 1)
    strip_row, strip_lane = iota((2 * levels, tile), 0), iota((2 * levels, tile), 1)
    outer = strip_row < levels

    def d_rows(f):
        return jnp.where(row == last, 0.0, pltpu.roll(f, last, 0)) - jnp.where(
            row == 0, 0.0, pltpu.roll(f, 1, 0)
        )

    def d_lanes(f):
        return jnp.where(lane == last, 0.0, pltpu.roll(f, last, 1)) - jnp.where(
            lane == 0, 0.0, pltpu.roll(f, 1, 1)
        )

    def columns(deep, shallow):
        packed = jnp.zeros((tile, tile), jnp.float32)
        for j, f in enumerate(deep):
            packed = jnp.where((lane >> 2) == j, pltpu.roll(f, 4 * j + 2, 1), packed)
        base = 4 * len(deep)
        for j, f in enumerate(shallow):
            packed = jnp.where((lane >> 1) == base // 2 + j, pltpu.roll(f, base + 2 * j + 1, 1), packed)
        flipped_cols[...] = packed.T

    def column(k):
        return flipped_cols[pl.ds(k, levels, stride=4), :]

    def rim_column(k):
        return flipped_cols[pl.ds(4 * levels + k, levels, stride=2), :]

    def take_strips():
        columns([p[j] for j in range(levels)], [wn[j] for j in range(levels)])
        for s, (a, b) in ((0, (0, 1)), (2, (last, last - 1))):
            p_strips[s, :levels] = p[:, a, :]
            p_strips[s, levels:] = p[:, b, :]
            w_strips[s, :levels] = we[:, a, :]
        for s, (a, b, c) in ((1, (2, 3, 1)), (3, (1, 0, 0))):
            p_strips[s, :levels] = column(a)
            p_strips[s, levels:] = column(b)
            w_strips[s, :levels] = rim_column(c)

    def code(x, y, s):
        c = edges[x, y, s]
        return c & 3, c >> 2

    def wanted(s, turn):
        return (s + 2 + turn) & 3

    def sign(s, turn):
        plus = ((turn + 1) & 3) < 2 if s % 2 == 0 else turn < 2
        return jnp.where(plus, 1.0, -1.0) * (1.0 if s < 2 else -1.0)

    def rim_sign(w):
        return jnp.where(w < 2, 1.0, -1.0) if not isinstance(w, int) else (1.0 if w < 2 else -1.0)

    loads[0].wait()
    near_plan = []
    for s in range(4):
        dx, dy = SHIFT[s]
        turn, flip = code(*place(-dx, -dy), s)
        near_plan.append((flip * 4 + wanted(s, turn), sign(s, turn)))

    def relay_plan(s, w, ax, ay):
        turn_a, flip_a = code(*place(ax, ay), s)
        turn_b, flip_b = code(*place(ax + SHIFT[s][0], ay + SHIFT[s][1]), w)
        return (flip_a ^ flip_b) * 4 + wanted(w, turn_b), sign(s, turn_a) * rim_sign(w)

    def relay_to(s, w):
        return relay_plan(s, w, -SHIFT[s][0] - SHIFT[w][0], -SHIFT[s][1] - SHIFT[w][1])

    diag_plan = [(relay_to(a, b), relay_to(b, a)) for a, b in DIAGONAL]
    far_plan = [relay_to(s, s) for s in range(4)]
    own_plan = [relay_to(s, opposite(s)) for s in range(4)]
    mine = [wanted(s, code(ix, iy, s)[0]) for s in range(4)]

    def relayed(t, s):
        found = own_relay[s]
        for k, (a, b) in enumerate(DIAGONAL):
            if s == a:
                found = jnp.where(mine[s] == b, diag_recv[t, k, :levels], found)
            if s == b:
                found = jnp.where(mine[s] == a, diag_recv[t, k, levels:], found)
        return jnp.where(mine[s] == s, far_recv[t, s], found)

    def send_rims(t):
        strips = [p_strips[s] for s in range(4)]
        rims = []
        for s in range(4):
            turned = A * pltpu.roll(strips[s], levels, 0)
            rims.append(jnp.where(outer, w_strips[s] - rim_sign(s) * turned, turned))
        for s in range(4):
            table[s] = rims[s]
            table[4 + s] = jnp.take_along_axis(rims[s], last - strip_lane, axis=1)
        for s in range(4):
            k, sgn = near_plan[s]
            rim = table[k]
            near_send[t, s] = jnp.where(outer, sgn * rim, rim)
            near_copy(t, s).start()
        for k in range(4):
            for half in range(2):
                which, sgn = diag_plan[k][half]
                diag_send[t, k, half * levels : (half + 1) * levels] = sgn * table[which, levels:]
            diag_copy(t, k).start()
        for s in range(4):
            k, sgn = far_plan[s]
            far_send[t, s] = sgn * table[k, levels:]
            far_copy(t, s).start()
        for s in range(4):
            k, sgn = own_plan[s]
            own_relay[s] = sgn * table[k, levels:]
            for up, level in ((1, levels - 1), (0, 0)):
                level_send[t, up, 2 * s : 2 * s + 2] = p_strips[s, pl.ds(level, 2, stride=levels), :]

        @pl.when(has_above)
        def _():
            level_copy(t, 1).start()

        @pl.when(has_below)
        def _():
            level_copy(t, 0).start()

    def corners(s, low, high):
        found = jnp.zeros((2 * levels, tile), jnp.float32)
        for depth in range(2):
            start = depth if s < 2 else last - depth
            for e in range(2):
                for pair, end in ((low, e), (high, last - e)):
                    moved = pltpu.roll(pair[depth ^ e], (end - start) % tile, 1) if end != start else pair[depth ^ e]
                    here = (strip_lane == end) & (outer if depth == 0 else jnp.logical_not(outer))
                    found = jnp.where(here, moved, found)
        return found

    def next_strips(t):
        for s in range(4):
            near_copy(t, s).wait_recv()
        for k in range(4):
            diag_copy(t, k).wait_recv()
        for s in range(4):
            far_copy(t, s).wait_recv()

        @pl.when(has_above)
        def _():
            level_copy(t, 0).wait_recv()

        @pl.when(has_below)
        def _():
            level_copy(t, 1).wait_recv()

        zero = jnp.zeros((levels, tile), jnp.float32)
        ghosts = []
        for s in range(4):
            ghosts.append(near_recv[t, s] + jnp.concatenate([relayed(t, s), zero], axis=0))
        pairs = [(g, pltpu.roll(g, levels, 0)) for g in ghosts]
        for s in range(2):
            rim_change[s] = jnp.where(outer, pairs[s][1], -ghosts[s + 2])
        for s in range(4):
            low, high = (pairs[1], pairs[3]) if s % 2 == 0 else (pairs[0], pairs[2])
            across = jnp.zeros((2 * levels, tile), jnp.float32)
            for depth in range(2):
                below, above = level_recv[t, 1], level_recv[t, 0]
                k = 2 * s + depth
                across = jnp.where(strip_row == depth * levels, below[k : k + 1], across)
                across = across + jnp.where(strip_row == (depth + 1) * levels - 1, above[k : k + 1], 0.0)
            p_strips[s] = p_strips[s] + st_strips[s] * (
                A * (ghosts[s] + corners(s, low, high)) + (B * B) * across
            )
            w_strips[s] = jnp.where(outer, w_strips[s] + rim_sign(s) * pairs[s][1], 0.0)

    def give_copy(c, o):
        return pltpu.make_async_remote_copy(
            src_ref=payload[c].at[o],
            dst_ref=arrived[c].at[ix],
            send_sem=give_sem.at[c, o],
            recv_sem=take_sem.at[c, ix],
            device_id={"px": o},
            device_id_type=MESH,
        )

    def got(c, o):
        return pltpu.make_async_remote_copy(
            src_ref=payload[c].at[o],
            dst_ref=arrived[c].at[o],
            send_sem=give_sem.at[c, o],
            recv_sem=take_sem.at[c, o],
            device_id={"px": o},
            device_id_type=MESH,
        )

    w_strips[...] = jnp.zeros(w_strips.shape, jnp.float32)
    ghost_rows[...] = jnp.zeros((tile, tile), jnp.float32)

    @pl.when(jnp.logical_not(has_below))
    def _():
        wu_below[...] = jnp.zeros((tile, tile), jnp.float32)
        level_recv[:, 1] = jnp.zeros((SUBSTEPS, 8, tile), jnp.float32)

    @pl.when(jnp.logical_not(has_above))
    def _():
        level_recv[:, 0] = jnp.zeros((SUBSTEPS, 8, tile), jnp.float32)

    for load in loads[1:4]:
        load.wait()
    take_strips()
    pl.semaphore_wait(
        barrier, n_px - 1 + len(beside) + has_above.astype(jnp.int32) + has_below.astype(jnp.int32)
    )
    send_rims(0)

    @pl.when(has_above)
    def _():
        wub_copy().start()
        plane_copy(0, 1, True).start()

    @pl.when(has_below)
    def _():
        plane_copy(0, 0, True).start()

    for load in loads[4:]:
        load.wait()
    columns([st[j] for j in range(levels)], [])
    for s, (a, b) in ((0, (0, 1)), (2, (last, last - 1))):
        st_strips[s, :levels] = st[:, a, :]
        st_strips[s, levels:] = st[:, b, :]
    for s, (a, b) in ((1, (2, 3)), (3, (1, 0))):
        st_strips[s, :levels] = column(a)
        st_strips[s, levels:] = column(b)
    slot_count = payload_first.shape[2]
    top = levels - 1
    every = tuple(range(levels))
    stages = (
        (picked_early, ((0, 0, top),), [(wu, l) for l in every[:top]]),
        (picked_first, ((1, 0, levels),), [(we, l) for l in every]),
        (picked_second, ((3, 0, levels), (2, levels, levels + 1)), [(wn, l) for l in every] + [(wu, top)]),
        (picked_third, ((4, 0, levels),), [(p, l) for l in every]),
    )
    capacity = pick_hot.shape[1]
    packed = capacity < n_px * slot_count
    find_slots(n_px, slot_count, packed, owner, source, weight, slot_source, slot_weight)
    steps = (capacity // LANES - 1).bit_length()
    if packed:
        filled = [
            jnp.sum(jnp.sum((owner[...] == o).astype(jnp.int32), axis=0, keepdims=True), axis=1, keepdims=True)
            for o in range(n_px)
        ]

    def part_of(o, found, low, high):
        if not packed:
            return found[low:high, pl.ds(pl.multiple_of(o * slot_count, LANES), slot_count)]
        start, count = jnp.zeros((1, 1), jnp.int32), jnp.zeros((1, 1), jnp.int32)
        for k, n in enumerate(filled):
            start = start + jnp.where(k < o, (n + (LANES - 1)) >> 7, 0)
            count = count + jnp.where(k == o, n, 0)
        part = found[low:high, :]
        for k in reversed(range(steps)):
            width = slot_count + ((1 << k) - 1) * LANES
            part = jnp.where(
                ((start >> k) & 1) == 1, part[:, LANES << k : (LANES << k) + width], part[:, :width]
            )
        return jnp.where(iota(part.shape, 1) < count, part, 0.0)

    def ahead(d):
        return lax.rem(ix + d + 1, n_px)

    def choose(k):
        found, _, planes = stages[k]
        first = sum(len(stage[2]) for stage in stages[:k])
        for n, (field, l) in enumerate(planes):
            split_plane(split, field[l], first + n)
        pick(first, split, pick_hot, pick_mask, found)

    def add_rims(k):
        found = stages[k][0]

        def step(b, carry):
            at = pl.ds(pl.multiple_of(b * LANES, LANES), LANES)
            src = jnp.broadcast_to(slot_source[pl.ds(b, 1), :], (2 * levels, LANES))
            across, along = (src >> 7, src & last) if k == 1 else (src & last, src >> 7)
            change = jnp.take_along_axis(rim_change[k - 1], along, axis=1) * slot_weight[pl.ds(b, 1), :]
            change = jnp.where(across == jnp.where(outer, 0, last), change, 0.0)
            found[:, at] = found[:, at] + (change[:levels] + change[levels:])
            return carry

        lax.fori_loop(0, capacity // LANES, step, 0, unroll=4)

    def hand_over(k):
        found, parts, planes = stages[k]

        def lay_out(o):
            whole = part_of(o, found, 0, len(planes))
            for c, low, high in parts:
                payload[c][o] = whole[low:high]

        def send(d, carry):
            lay_out(ahead(d))
            for c, _, _ in parts:
                give_copy(c, ahead(d)).start()
            return carry

        lax.fori_loop(0, n_px - 1, send, 0)
        lay_out(ix)

    def substep(t, carry):
        for j in range(levels):
            we[j] = we[j] - A * d_rows(p[j])
            wn[j] = wn[j] - A * d_lanes(p[j])
        for j in range(levels - 1):
            wu[j] = wu[j] - B * (p[j + 1] - p[j])

        @pl.when(has_above)
        def _():
            wu[levels - 1] = wu[levels - 1] + B * p[levels - 1]

        @pl.when(jnp.logical_not(has_above))
        def _():
            wu[levels - 1] = jnp.zeros((tile, tile), jnp.float32)

        for j in range(1, levels):
            p[j] = p[j] - st[j] * (A * (d_rows(we[j]) + d_lanes(wn[j])) + B * (wu[j] - wu[j - 1]))

        @pl.when(has_below & (t == 0))
        def _():
            wub_copy().wait_recv()

        @pl.when(has_below)
        def _():
            wu_below[...] = wu_below[...] - B * p[0]

        p[0] = p[0] - st[0] * (A * (d_rows(we[0]) + d_lanes(wn[0])) + B * (wu[0] - wu_below[...]))
        take_strips()

        @pl.when(t == 1)
        def _():
            pick_tables(slot_source, slot_weight, pick_hot, pick_mask)
            if packed:
                for found, _, planes in stages:
                    found[:, capacity:] = jnp.zeros((len(planes), found.shape[1] - capacity), jnp.float32)

        @pl.when(t == 2)
        def _():
            land_tables(cell, land_hot)
            total[...] = jnp.zeros(total.shape, jnp.float32)

        @pl.when(t == SUBSTEPS - 1)
        def _():
            choose(0)
            hand_over(0)
            for k in range(1, EARLY):
                choose(k)

        next_strips(t)

        @pl.when(t == SUBSTEPS - 1)
        def _():
            for k in range(1, EARLY):
                add_rims(k)
                hand_over(k)

        @pl.when(t < SUBSTEPS - 1)
        def _():
            send_rims(t + 1)

        @pl.when(has_above)
        def _():
            plane_copy(t, 0).wait_recv()
            wu[levels - 1] = wu[levels - 1] - B * plane_recv[t, 0]
            p[levels - 1] = p[levels - 1] + (B * B) * (st[levels - 1] * plane_recv[t, 0])

        @pl.when(has_below)
        def _():
            plane_copy(t, 1).wait_recv()
            wu_below[...] = wu_below[...] + B * plane_recv[t, 1]
            p[0] = p[0] + (B * B) * (st[0] * plane_recv[t, 1])

        for s, (a, b) in ((0, (0, 1)), (2, (last, last - 1))):
            p[:, a, :] = p_strips[s, :levels]
            p[:, b, :] = p_strips[s, levels:]
            we[:, a, :] = w_strips[s, :levels]
        for k, (s, half) in enumerate(((3, 1), (3, 0), (1, 0), (1, 1))):
            ghost_rows[pl.ds(k, levels, stride=4), :] = p_strips[s, half * levels : (half + 1) * levels]
        for k, s in enumerate((3, 1)):
            ghost_rows[pl.ds(4 * levels + k, levels, stride=2), :] = w_strips[s, :levels]
        turned = ghost_rows[...].T
        rim = (lane == 0) | (lane == last)
        band = (lane <= 1) | (lane >= last - 1)

        def put_sides(j):
            p[j] = jnp.where(band, pltpu.roll(turned, (tile - 4 * j - 2) % tile, 1), p[j])

        put_sides(levels - 1)

        @pl.when((t < SUBSTEPS - 1) & has_above)
        def _():
            plane_send[t + 1, 1] = p[levels - 1]
            plane_copy(t + 1, 1).start()

        put_sides(0)

        @pl.when((t < SUBSTEPS - 1) & has_below)
        def _():
            plane_send[t + 1, 0] = p[0]
            plane_copy(t + 1, 0).start()

        for j in range(1, levels - 1):
            put_sides(j)
        for j in range(levels):
            wn[j] = jnp.where(rim, pltpu.roll(turned, (tile - 4 * levels - 2 * j - 1) % tile, 1), wn[j])

        return carry

    lax.fori_loop(0, SUBSTEPS, substep, 0)

    for k in range(EARLY, len(stages)):
        choose(k)
        hand_over(k)

    groups = latlon.shape[2] // BLOCK
    sums = (((1, 2), (1, 3)), ((3, 0), (0, 2, 4)))

    for n, (_, parts) in enumerate(sums):
        land(n, [payload[c][ix] for c in parts], cell, land_hot, ix, total)

    for n, (names, parts) in enumerate(sums):

        def bring_in(d, carry):
            o = lax.rem(ix + n_px - d - 1, n_px)
            for c in parts:
                got(c, o).wait_recv()
            land(n, [arrived[c][o] for c in parts], cell, land_hot, o, total)
            return carry

        lax.fori_loop(0, n_px - 1, bring_in, 0)
        for g in range(groups):
            rows = len(names) * levels
            high, low = g * rows, (groups + g) * rows
            both = total[n, high : high + rows] + total[n, low : low + rows]
            for k, q in enumerate(names):
                latlon[q, :, g * BLOCK : (g + 1) * BLOCK] = both[k * levels : (k + 1) * levels]

    def drain(t, carry):
        for s in range(4):
            near_copy(t, s).wait_send()
            diag_copy(t, s).wait_send()
            far_copy(t, s).wait_send()

        @pl.when(has_above)
        def _():
            level_copy(t, 1).wait_send()
            plane_copy(t, 1).wait_send()

        @pl.when(has_below)
        def _():
            level_copy(t, 0).wait_send()
            plane_copy(t, 0).wait_send()

        return carry

    lax.fori_loop(0, SUBSTEPS, drain, 0)

    @pl.when(has_above)
    def _():
        wub_copy().wait_send()

    def sent(d, carry):
        for c in range(len(payload)):
            give_copy(c, ahead(d)).wait_send()
        return carry

    lax.fori_loop(0, n_px - 1, sent, 0)


def find_slots(owner_count, slot_count, packed, owner, source, weight, slot_source, slot_weight):
    rows = owner.shape[0]
    slot_rows = slot_source.shape[0]
    names = owner[...]
    up_to = (iota((LANES, LANES), 0) <= iota((LANES, LANES), 1)).astype(jnp.bfloat16)
    ones = jnp.ones((LANES, LANES), jnp.bfloat16)
    before = (iota((rows, rows), 0) > iota((rows, rows), 1)).astype(jnp.bfloat16)

    def count(o, carry):
        place, start = carry
        named = names == o
        hot = named.astype(jnp.float32).astype(jnp.bfloat16)
        within = jnp.dot(hot, up_to, preferred_element_type=jnp.float32)
        total = jnp.dot(hot, ones, preferred_element_type=jnp.float32)
        earlier = jnp.dot(before, total.astype(jnp.bfloat16), preferred_element_type=jnp.float32)
        place = jnp.where(named, within + earlier - 1.0 + start, place)
        if packed:
            filled = jnp.sum(total, axis=0, keepdims=True)
            start = start + jnp.floor((filled + (LANES - 1.0)) / LANES) * LANES
        else:
            start = start + float(slot_count)
        return place, start

    zero = jnp.zeros(names.shape, jnp.float32)
    place, _ = lax.fori_loop(0, owner_count, count, (zero, jnp.zeros((1, LANES), jnp.float32)))
    slot = place.astype(jnp.int32)
    slot_high, slot_low = slot >> 7, slot & (LANES - 1)
    src = source[...]
    w = weight[...]
    w1 = w.astype(jnp.bfloat16).astype(jnp.float32)
    w2 = (w - w1).astype(jnp.bfloat16).astype(jnp.float32)
    w3 = w - w1 - w2
    pieces = [(src >> 7).astype(jnp.float32), (src & (LANES - 1)).astype(jnp.float32), w1, w2, w3]
    high_place, low_place = iota((slot_rows, LANES), 0), iota((LANES, LANES), 0)
    total = jnp.zeros((len(pieces) * slot_rows, LANES), jnp.float32)
    for r in range(rows):
        here = high_place == slot_high[r : r + 1]
        left = jnp.concatenate([jnp.where(here, piece[r : r + 1], 0.0) for piece in pieces], axis=0)
        right = jnp.where(low_place == slot_low[r : r + 1], 1.0, 0.0)
        total += dot_nt(left.astype(jnp.bfloat16), right.astype(jnp.bfloat16))
    part = [total[k * slot_rows : (k + 1) * slot_rows] for k in range(len(pieces))]
    slot_source[...] = (part[0] * LANES + part[1]).astype(jnp.int32)
    slot_weight[...] = part[2] + part[3] + part[4]


def split_plane(split, plane, r):
    tile = plane.shape[0]
    half = tile // 2
    h, d = parts2(plane.T)
    for k, part in enumerate((h[:half], h[half:], d[:half], d[half:])):
        split[r * half : (r + 1) * half, k * tile : (k + 1) * tile] = part


def joined(ref, row, pieces):
    return jnp.concatenate([ref[pl.ds(row + k, 1), :] for k in range(pieces)], axis=1)


def pick_tables(slot_source, slot_weight, pick_hot, pick_mask):
    lines, capacity = pick_hot.shape
    tile, half = lines // 2, pick_mask.shape[0]
    pieces = BLOCK // LANES

    def step(b, carry):
        at = pl.ds(pl.multiple_of(b * BLOCK, BLOCK), BLOCK)
        src, w = joined(slot_source, b * pieces, pieces), joined(slot_weight, b * pieces, pieces)
        x, y = src >> 7, src & (tile - 1)
        line = x + jnp.where(y >= half, tile, 0)
        pick_hot[:, at] = jnp.where(iota((lines, BLOCK), 0) == line, 1.0, 0.0).astype(jnp.bfloat16)
        pick_mask[:, at] = jnp.where(iota((half, BLOCK), 0) == (y & (half - 1)), w, 0.0)
        return carry

    lax.fori_loop(0, capacity // BLOCK, step, 0)


def pick(first, split, pick_hot, pick_mask, found):
    rows = found.shape[0]
    half, capacity = pick_mask.shape
    lines = slice(first * half, (first + rows) * half)
    width = 2 * BLOCK if capacity % (2 * BLOCK) == 0 else BLOCK
    steps = capacity // width

    def step(b, carry):
        at = pl.ds(pl.multiple_of(b * width, width), width)
        hot = pick_hot[:, at]
        line = jnp.dot(
            split[lines, :], jnp.concatenate([hot, hot], axis=0), preferred_element_type=jnp.float32
        )
        found[:, at] = jnp.sum(line.reshape(rows, half, width) * pick_mask[:, at][None], axis=1)
        return carry

    lax.fori_loop(0, steps, step, 0, unroll=steps if steps < 12 else 4)


def land_tables(cell, land_hot):
    owner_count, _, slot_count = land_hot.shape
    pieces = slot_count // LANES

    def step(o, carry):
        c = joined(cell, o * pieces, pieces)
        hot = jnp.where(iota((BLOCK, slot_count), 0) == (c & (BLOCK - 1)), 1.0, 0.0)
        land_hot[o] = hot.astype(jnp.bfloat16)
        return carry

    lax.fori_loop(0, owner_count, step, 0)


def land(q, parts, cell, land_hot, o, total):
    values = parts[0] if len(parts) == 1 else jnp.concatenate(parts, axis=0)
    rows, slot_count = values.shape
    groups = total.shape[1] // (2 * rows)
    pieces = slot_count // LANES
    group = joined(cell, o * pieces, pieces) >> 8
    h = values.astype(jnp.bfloat16).astype(jnp.float32)
    spread = [jnp.where(group == g, h, 0.0) for g in range(groups)]
    spread += [jnp.where(group == g, values - h, 0.0) for g in range(groups)]
    total[q] += dot_nt(jnp.concatenate(spread, axis=0).astype(jnp.bfloat16), land_hot[o])


def per_device(
    sizes,
    pressure,
    wind_east,
    wind_north,
    wind_up,
    stiffness,
    edge_table,
    remap_source,
    remap_weight,
    remap_owner,
    latlon_cell,
):
    levels, tile, _ = pressure.shape
    owner_count = sizes[0]
    slots = latlon_cell.shape[0]
    slot_count = slots // owner_count
    cell_count = tile * tile // 8
    count = 4 * levels
    entries = remap_source.shape[0]
    rows = entries // LANES
    capacity = -(-(entries + (owner_count - 1) * (LANES - 1)) // BLOCK) * BLOCK
    capacity = min(capacity, slots)
    room = capacity
    if capacity < slots:
        room = slot_count + ((2 << (capacity // LANES - 1).bit_length() - 1) - 1) * LANES + LANES
        room = max(room, capacity)
    slot_rows = -(-capacity // (8 * LANES)) * 8
    part_rows = (levels - 1, levels, 1, levels, levels)
    f32, i32 = jnp.float32, jnp.int32
    n = SUBSTEPS
    field = pltpu.VMEM(pressure.shape, f32)
    plane = pltpu.VMEM((tile, tile), f32)
    dma = pltpu.SemaphoreType.DMA
    in_vmem = pl.BlockSpec(memory_space=pltpu.VMEM)
    results = pl.pallas_call(
        functools.partial(whole_kernel, sizes),
        out_shape=[
            pltpu.VMEM(pressure.shape, f32),
            pltpu.VMEM((4, levels, cell_count), f32),
        ],
        in_specs=[pl.BlockSpec(memory_space=pl.ANY)] * 10,
        out_specs=[in_vmem] * 2,
        scratch_shapes=[
            pltpu.SMEM(edge_table.shape, i32),
            field,
            field,
            field,
            field,
            pltpu.VMEM((rows, LANES), i32),
            pltpu.VMEM((rows, LANES), i32),
            pltpu.VMEM((rows, LANES), f32),
            pltpu.VMEM((slots // LANES, LANES), i32),
            pltpu.VMEM((8, 2 * levels, tile), f32),
            pltpu.VMEM((n, 4, 2 * levels, tile), f32),
            pltpu.VMEM((n, 4, 2 * levels, tile), f32),
            pltpu.VMEM((n, 4, 2 * levels, tile), f32),
            pltpu.VMEM((n, 4, 2 * levels, tile), f32),
            pltpu.VMEM((n, 4, levels, tile), f32),
            pltpu.VMEM((n, 4, levels, tile), f32),
            pltpu.VMEM((4, levels, tile), f32),
            pltpu.VMEM((n, 2, 8, tile), f32),
            pltpu.VMEM((n, 2, 8, tile), f32),
            pltpu.VMEM((n, 2, tile, tile), f32),
            pltpu.VMEM((n, 2, tile, tile), f32),
            plane,
            plane,
            plane,
            pltpu.VMEM((4, 2 * levels, tile), f32),
            pltpu.VMEM((4, 2 * levels, tile), f32),
            pltpu.VMEM((4, 2 * levels, tile), f32),
            pltpu.VMEM((2, 2 * levels, tile), f32),
            pltpu.VMEM((slot_rows, LANES), i32),
            pltpu.VMEM((slot_rows, LANES), f32),
            pltpu.VMEM((2 * tile, capacity), jnp.bfloat16),
            pltpu.VMEM((tile // 2, capacity), f32),
            pltpu.VMEM((owner_count, BLOCK, slot_count), jnp.bfloat16),
            pltpu.VMEM((count * tile // 2, 4 * tile), jnp.bfloat16),
            *(pltpu.VMEM((n_rows, room), f32) for n_rows in (levels - 1, levels, levels + 1, levels)),
            *(pltpu.VMEM((owner_count, n_rows, slot_count), f32) for n_rows in part_rows),
            *(pltpu.VMEM((owner_count, n_rows, slot_count), f32) for n_rows in part_rows),
            pltpu.VMEM((2, 4 * levels * (cell_count // BLOCK), BLOCK), f32),
            dma((10,)),
            dma((2, n, 4)),
            dma((2, n, 4)),
            dma((2, n, 4)),
            dma((2, n, 2)),
            dma((2, n, 2)),
            dma((2, 1)),
            dma((len(part_rows), owner_count)),
            dma((len(part_rows), owner_count)),
        ],
        compiler_params=pltpu.CompilerParams(
            collective_id=0, has_side_effects=True, vmem_limit_bytes=60 * 2**20
        ),
    )(
        edge_table,
        pressure,
        wind_east,
        wind_north,
        wind_up,
        stiffness,
        remap_owner.reshape(rows, LANES),
        remap_source.reshape(rows, LANES),
        remap_weight.reshape(rows, LANES),
        latlon_cell.reshape(slots // LANES, LANES),
    )
    anywhere = pl.BlockSpec(memory_space=pl.ANY)
    return pl.pallas_call(
        pass_on,
        out_shape=[jax.ShapeDtypeStruct(r.shape, f32) for r in results],
        in_specs=[in_vmem] * 2,
        out_specs=[anywhere] * 2,
        scratch_shapes=[dma((2,))],
    )(*(pltpu.with_memory_space_constraint(r, pltpu.VMEM) for r in results))


def pass_on(p, latlon, p_out, latlon_out, sems):
    copies = [
        pltpu.make_async_copy(src, dst, sems.at[k]) for k, (src, dst) in enumerate(((p, p_out), (latlon, latlon_out)))
    ]
    for copy in copies:
        copy.start()
    for copy in copies:
        copy.wait()


def solution(mesh):
    field = P("lev", "px", "py")
    entries = P(("px", "py"))
    sizes = (mesh.shape["px"], mesh.shape["py"], mesh.shape["lev"])
    return jax.shard_map(
        functools.partial(per_device, sizes),
        mesh=mesh,
        in_specs=(field,) * 5 + (P(), entries, entries, P(("px", "py"), None), entries),
        out_specs=(field, P(None, "lev", ("px", "py"))),
        check_vma=False,
    )
```

```python
import functools

import jax
import jax.numpy as jnp
from jax import lax
from jax.experimental import pallas as pl
from jax.experimental.pallas import tpu as pltpu
from jax.sharding import PartitionSpec as P

SUBSTEPS = 4
A = 0.45
B = 0.3
LANES = 128
BLOCK = 256
EARLY = 2
MESH = pl.DeviceIdType.MESH


def iota(shape, dim):
    return lax.broadcasted_iota(jnp.int32, shape, dim)


def parts2(x):
    high = x.astype(jnp.bfloat16)
    return high, (x - high.astype(jnp.float32)).astype(jnp.bfloat16)


def dot_nt(a, b):
    return lax.dot_general(a, b, (((1,), (1,)), ((), ())), preferred_element_type=jnp.float32)


def opposite(s):
    return (s + 2) & 3


SHIFT = ((-1, 0), (0, -1), (1, 0), (0, 1))
DIAGONAL = ((0, 1), (0, 3), (2, 1), (2, 3))


def whole_kernel(
    sizes,
    edges_in,
    p_in,
    we_in,
    wn_in,
    wu_in,
    st_in,
    owner_in,
    source_in,
    weight_in,
    cell_in,
    p,
    latlon,
    edges,
    we,
    wn,
    wu,
    st,
    owner,
    source,
    weight,
    cell,
    table,
    near_send,
    near_recv,
    diag_send,
    diag_recv,
    far_send,
    far_recv,
    own_relay,
    level_send,
    level_recv,
    plane_send,
    plane_recv,
    wu_below,
    flipped_cols,
    ghost_rows,
    p_strips,
    w_strips,
    st_strips,
    wu_rims,
    rim_change,
    slot_source,
    slot_weight,
    pick_hot,
    pick_mask,
    land_hot,
    split,
    picked_early,
    picked_first,
    picked_second,
    picked_third,
    payload_early,
    payload_first,
    payload_top,
    payload_second,
    payload_third,
    arrived_early,
    arrived_first,
    arrived_top,
    arrived_second,
    arrived_third,
    total,
    in_sems,
    near_sems,
    diag_sems,
    far_sems,
    level_sems,
    plane_sems,
    give_sem,
    take_sem,
):
    n_px, n_py, n_lev = sizes
    levels, tile, _ = p.shape
    last = tile - 1
    ix, iy, iz = lax.axis_index("px"), lax.axis_index("py"), lax.axis_index("lev")
    has_above, has_below = iz < n_lev - 1, iz > 0
    payload = (payload_early, payload_first, payload_top, payload_second, payload_third)
    arrived = (arrived_early, arrived_first, arrived_top, arrived_second, arrived_third)

    def place(dx, dy):
        return lax.rem(ix + dx + 2 * n_px, n_px), lax.rem(iy + dy + 2 * n_py, n_py)

    def at(dx, dy):
        x, y = place(dx, dy)
        return {"px": x, "py": y}

    others = {(d, 0) for d in range(1, n_px)}
    for dx, dy in ((0, 1), (0, -1), (0, 2), (0, -2), (1, 1), (1, -1), (-1, 1), (-1, -1)):
        others.add((dx % n_px, dy % n_py))
    beside = sorted(o for o in others if o[1])

    barrier = pltpu.get_barrier_semaphore()
    for dx, dy in beside:
        pl.semaphore_signal(barrier, inc=1, device_id=at(dx, dy), device_id_type=MESH)

    def greet(d, carry):
        pl.semaphore_signal(barrier, inc=1, device_id={"px": lax.rem(ix + d, n_px)}, device_id_type=MESH)
        return carry

    lax.fori_loop(1, n_px, greet, 0)

    @pl.when(has_above)
    def _():
        pl.semaphore_signal(barrier, inc=1, device_id={"lev": iz + 1}, device_id_type=MESH)

    @pl.when(has_below)
    def _():
        pl.semaphore_signal(barrier, inc=1, device_id={"lev": iz - 1}, device_id_type=MESH)

    loads = [
        pltpu.make_async_copy(src, dst, in_sems.at[k])
        for k, (src, dst) in enumerate(
            (
                (edges_in, edges),
                (p_in, p),
                (we_in, we),
                (wn_in, wn),
                (wu_in, wu),
                (st_in, st),
                (owner_in, owner),
                (source_in, source),
                (weight_in, weight),
                (cell_in, cell),
            )
        )
    ]
    for load in loads:
        load.start()
    def remote(src, dst, sems, index, device):
        return pltpu.make_async_remote_copy(
            src_ref=src,
            dst_ref=dst,
            send_sem=sems.at[(0,) + index],
            recv_sem=sems.at[(1,) + index],
            device_id=device,
            device_id_type=MESH,
        )

    def near_copy(t, s):
        dx, dy = SHIFT[s]
        return remote(near_send.at[t, s], near_recv.at[t, s], near_sems, (t, s), at(-dx, -dy))

    def diag_copy(t, k):
        (ax, ay), (bx, by) = SHIFT[DIAGONAL[k][0]], SHIFT[DIAGONAL[k][1]]
        return remote(diag_send.at[t, k], diag_recv.at[t, k], diag_sems, (t, k), at(-ax - bx, -ay - by))

    def far_copy(t, s):
        dx, dy = SHIFT[s]
        return remote(far_send.at[t, s], far_recv.at[t, s], far_sems, (t, s), at(-2 * dx, -2 * dy))

    def level_copy(t, up):
        return remote(
            level_send.at[t, up],
            level_recv.at[t, up],
            level_sems,
            (t, up),
            {"lev": iz + 1 if up else iz - 1},
        )

    def plane_copy(t, up):
        return remote(plane_send.at[t, up], plane_recv.at[t, up], plane_sems, (t, up), {"lev": iz + 1 if up else iz - 1})

    row, lane = iota((tile, tile), 0), iota((tile, tile), 1)
    strip_row, strip_lane = iota((2 * levels, tile), 0), iota((2 * levels, tile), 1)
    outer = strip_row < levels

    def d_rows(f):
        return jnp.where(row == last, 0.0, pltpu.roll(f, last, 0)) - jnp.where(
            row == 0, 0.0, pltpu.roll(f, 1, 0)
        )

    def d_lanes(f):
        return jnp.where(lane == last, 0.0, pltpu.roll(f, last, 1)) - jnp.where(
            lane == 0, 0.0, pltpu.roll(f, 1, 1)
        )

    def columns(deep, shallow):
        packed = jnp.zeros((tile, tile), jnp.float32)
        for j, f in enumerate(deep):
            packed = jnp.where((lane >> 2) == j, pltpu.roll(f, 4 * j + 2, 1), packed)
        base = 4 * len(deep)
        for j, f in enumerate(shallow):
            packed = jnp.where((lane >> 1) == base // 2 + j, pltpu.roll(f, base + 2 * j + 1, 1), packed)
        flipped_cols[...] = packed.T

    def column(k):
        return flipped_cols[pl.ds(k, levels, stride=4), :]

    def rim_column(k):
        return flipped_cols[pl.ds(4 * levels + k, levels, stride=2), :]

    def take_strips():
        columns([p[j] for j in range(levels)], [wn[j] for j in range(levels)])
        for s, (a, b) in ((0, (0, 1)), (2, (last, last - 1))):
            p_strips[s, :levels] = p[:, a, :]
            p_strips[s, levels:] = p[:, b, :]
            w_strips[s, :levels] = we[:, a, :]
        for s, (a, b, c) in ((1, (2, 3, 1)), (3, (1, 0, 0))):
            p_strips[s, :levels] = column(a)
            p_strips[s, levels:] = column(b)
            w_strips[s, :levels] = rim_column(c)

    def code(x, y, s):
        c = edges[x, y, s]
        return c & 3, c >> 2

    def wanted(s, turn):
        return (s + 2 + turn) & 3

    def sign(s, turn):
        plus = ((turn + 1) & 3) < 2 if s % 2 == 0 else turn < 2
        return jnp.where(plus, 1.0, -1.0) * (1.0 if s < 2 else -1.0)

    def rim_sign(w):
        return jnp.where(w < 2, 1.0, -1.0) if not isinstance(w, int) else (1.0 if w < 2 else -1.0)

    loads[0].wait()
    near_plan = []
    for s in range(4):
        dx, dy = SHIFT[s]
        turn, flip = code(*place(-dx, -dy), s)
        near_plan.append((flip * 4 + wanted(s, turn), sign(s, turn)))

    def relay_plan(s, w, ax, ay):
        turn_a, flip_a = code(*place(ax, ay), s)
        turn_b, flip_b = code(*place(ax + SHIFT[s][0], ay + SHIFT[s][1]), w)
        return (flip_a ^ flip_b) * 4 + wanted(w, turn_b), sign(s, turn_a) * rim_sign(w)

    def relay_to(s, w):
        return relay_plan(s, w, -SHIFT[s][0] - SHIFT[w][0], -SHIFT[s][1] - SHIFT[w][1])

    diag_plan = [(relay_to(a, b), relay_to(b, a)) for a, b in DIAGONAL]
    far_plan = [relay_to(s, s) for s in range(4)]
    own_plan = [relay_to(s, opposite(s)) for s in range(4)]
    mine = [wanted(s, code(ix, iy, s)[0]) for s in range(4)]

    def relayed(t, s):
        found = own_relay[s]
        for k, (a, b) in enumerate(DIAGONAL):
            if s == a:
                found = jnp.where(mine[s] == b, diag_recv[t, k, :levels], found)
            if s == b:
                found = jnp.where(mine[s] == a, diag_recv[t, k, levels:], found)
        return jnp.where(mine[s] == s, far_recv[t, s], found)

    def send_rims(t, first=False):
        strips = [p_strips[s] for s in range(4)]
        rims = []
        for s in range(4):
            turned = A * pltpu.roll(strips[s], levels, 0)
            rims.append(jnp.where(outer, w_strips[s] - rim_sign(s) * turned, turned))
        for s in range(4):
            table[s] = rims[s]
            table[4 + s] = jnp.take_along_axis(rims[s], last - strip_lane, axis=1)
        for k in range(4):
            for half in range(2):
                which, sgn = diag_plan[k][half]
                diag_send[t, k, half * levels : (half + 1) * levels] = sgn * table[which, levels:]
            diag_copy(t, k).start()
        for s in range(4):
            k, sgn = near_plan[s]
            rim = table[k]
            near_send[t, s] = jnp.where(outer, sgn * rim, rim)
            near_copy(t, s).start()
        for s in range(4):
            k, sgn = far_plan[s]
            far_send[t, s] = sgn * table[k, levels:]
            far_copy(t, s).start()
        for s in range(4):
            k, sgn = own_plan[s]
            own_relay[s] = sgn * table[k, levels:]
            for up, level in ((1, levels - 1), (0, 0)):
                level_send[t, up, 2 * s : 2 * s + 2] = p_strips[s, pl.ds(level, 2, stride=levels), :]
        if first:
            level_send[t, 1] = level_send[t, 1] + wu_rims[...] * (1.0 / B)

        @pl.when(has_above)
        def _():
            level_copy(t, 1).start()

        @pl.when(has_below)
        def _():
            level_copy(t, 0).start()

    def corners(s, low, high):
        found = jnp.zeros((2 * levels, tile), jnp.float32)
        for depth in range(2):
            start = depth if s < 2 else last - depth
            for e in range(2):
                for pair, end in ((low, e), (high, last - e)):
                    moved = pltpu.roll(pair[depth ^ e], (end - start) % tile, 1) if end != start else pair[depth ^ e]
                    here = (strip_lane == end) & (outer if depth == 0 else jnp.logical_not(outer))
                    found = jnp.where(here, moved, found)
        return found

    def next_strips(t):
        for s in range(4):
            near_copy(t, s).wait_recv()
        for k in range(4):
            diag_copy(t, k).wait_recv()
        for s in range(4):
            far_copy(t, s).wait_recv()

        @pl.when(has_above)
        def _():
            level_copy(t, 0).wait_recv()

        @pl.when(has_below)
        def _():
            level_copy(t, 1).wait_recv()

        zero = jnp.zeros((levels, tile), jnp.float32)
        ghosts = []
        for s in range(4):
            ghosts.append(near_recv[t, s] + jnp.concatenate([relayed(t, s), zero], axis=0))
        pairs = [(g, pltpu.roll(g, levels, 0)) for g in ghosts]
        for s in range(2):
            rim_change[s] = jnp.where(outer, pairs[s][1], -ghosts[s + 2])
        for s in range(4):
            low, high = (pairs[1], pairs[3]) if s % 2 == 0 else (pairs[0], pairs[2])
            across = jnp.zeros((2 * levels, tile), jnp.float32)
            for depth in range(2):
                below, above = level_recv[t, 1], level_recv[t, 0]
                k = 2 * s + depth
                across = jnp.where(strip_row == depth * levels, below[k : k + 1], across)
                across = across + jnp.where(strip_row == (depth + 1) * levels - 1, above[k : k + 1], 0.0)
            p_strips[s] = p_strips[s] + st_strips[s] * (
                A * (ghosts[s] + corners(s, low, high)) + (B * B) * across
            )
            w_strips[s] = jnp.where(outer, w_strips[s] + rim_sign(s) * pairs[s][1], 0.0)

    def give_copy(c, o):
        return pltpu.make_async_remote_copy(
            src_ref=payload[c].at[o],
            dst_ref=arrived[c].at[ix],
            send_sem=give_sem.at[c, o],
            recv_sem=take_sem.at[c, ix],
            device_id={"px": o},
            device_id_type=MESH,
        )

    def got(c, o):
        return pltpu.make_async_remote_copy(
            src_ref=payload[c].at[o],
            dst_ref=arrived[c].at[o],
            send_sem=give_sem.at[c, o],
            recv_sem=take_sem.at[c, o],
            device_id={"px": o},
            device_id_type=MESH,
        )

    w_strips[...] = jnp.zeros(w_strips.shape, jnp.float32)
    ghost_rows[...] = jnp.zeros((tile, tile), jnp.float32)

    wu_below[...] = jnp.zeros((tile, tile), jnp.float32)

    @pl.when(jnp.logical_not(has_below))
    def _():
        level_recv[:, 1] = jnp.zeros((SUBSTEPS, 8, tile), jnp.float32)

    @pl.when(jnp.logical_not(has_above))
    def _():
        level_recv[:, 0] = jnp.zeros((SUBSTEPS, 8, tile), jnp.float32)

    for load in loads[1:5]:
        load.wait()
    columns([wu[levels - 1]], [])
    for k, place_of in enumerate((0, 1, None, None, last, last - 1)):
        if place_of is not None:
            wu_rims[k : k + 1] = wu[levels - 1, place_of : place_of + 1, :]
    for k, place_of in ((2, 2), (3, 3), (6, 1), (7, 0)):
        wu_rims[k : k + 1] = flipped_cols[place_of : place_of + 1, :]
    take_strips()
    plane_send[0, 1] = p[levels - 1] + wu[levels - 1] * (1.0 / B)
    plane_send[0, 0] = p[0]
    pl.semaphore_wait(
        barrier, n_px - 1 + len(beside) + has_above.astype(jnp.int32) + has_below.astype(jnp.int32)
    )
    send_rims(0, True)

    @pl.when(has_above)
    def _():
        plane_copy(0, 1).start()

    @pl.when(has_below)
    def _():
        plane_copy(0, 0).start()

    for load in loads[5:]:
        load.wait()
    columns([st[j] for j in range(levels)], [])
    for s, (a, b) in ((0, (0, 1)), (2, (last, last - 1))):
        st_strips[s, :levels] = st[:, a, :]
        st_strips[s, levels:] = st[:, b, :]
    for s, (a, b) in ((1, (2, 3)), (3, (1, 0))):
        st_strips[s, :levels] = column(a)
        st_strips[s, levels:] = column(b)
    slot_count = payload_first.shape[2]
    top = levels - 1
    every = tuple(range(levels))
    stages = (
        (picked_early, ((0, 0, top),), [(wu, l) for l in every[:top]]),
        (picked_first, ((1, 0, levels),), [(we, l) for l in every]),
        (picked_second, ((3, 0, levels), (2, levels, levels + 1)), [(wn, l) for l in every] + [(wu, top)]),
        (picked_third, ((4, 0, levels),), [(p, l) for l in every]),
    )
    capacity = pick_hot.shape[1]
    packed = capacity < n_px * slot_count
    find_slots(n_px, slot_count, packed, owner, source, weight, slot_source, slot_weight)
    steps = (capacity // LANES - 1).bit_length()
    if packed:
        filled = [
            jnp.sum(jnp.sum((owner[...] == o).astype(jnp.int32), axis=0, keepdims=True), axis=1, keepdims=True)
            for o in range(n_px)
        ]

    def part_of(o, found, low, high):
        if not packed:
            return found[low:high, pl.ds(pl.multiple_of(o * slot_count, LANES), slot_count)]
        start, count = jnp.zeros((1, 1), jnp.int32), jnp.zeros((1, 1), jnp.int32)
        for k, n in enumerate(filled):
            start = start + jnp.where(k < o, (n + (LANES - 1)) >> 7, 0)
            count = count + jnp.where(k == o, n, 0)
        part = found[low:high, :]
        for k in reversed(range(steps)):
            width = slot_count + ((1 << k) - 1) * LANES
            part = jnp.where(
                ((start >> k) & 1) == 1, part[:, LANES << k : (LANES << k) + width], part[:, :width]
            )
        return jnp.where(iota(part.shape, 1) < count, part, 0.0)

    def ahead(d):
        return lax.rem(ix + d + 1, n_px)

    def choose(k):
        found, _, planes = stages[k]
        first = sum(len(stage[2]) for stage in stages[:k])
        for n, (field, l) in enumerate(planes):
            split_plane(split, field[l], first + n)
        pick(first, split, pick_hot, pick_mask, found)

    def add_rims(k):
        found = stages[k][0]

        def step(b, carry):
            at = pl.ds(pl.multiple_of(b * LANES, LANES), LANES)
            src = jnp.broadcast_to(slot_source[pl.ds(b, 1), :], (2 * levels, LANES))
            across, along = (src >> 7, src & last) if k == 1 else (src & last, src >> 7)
            change = jnp.take_along_axis(rim_change[k - 1], along, axis=1) * slot_weight[pl.ds(b, 1), :]
            change = jnp.where(across == jnp.where(outer, 0, last), change, 0.0)
            found[:, at] = found[:, at] + (change[:levels] + change[levels:])
            return carry

        lax.fori_loop(0, capacity // LANES, step, 0, unroll=4)

    def hand_over(k):
        found, parts, planes = stages[k]

        def lay_out(o):
            whole = part_of(o, found, 0, len(planes))
            for c, low, high in parts:
                payload[c][o] = whole[low:high]

        def send(d, carry):
            lay_out(ahead(d))
            for c, _, _ in parts:
                give_copy(c, ahead(d)).start()
            return carry

        lax.fori_loop(0, n_px - 1, send, 0)
        lay_out(ix)

    def substep(t, carry):
        for j in range(levels):
            we[j] = we[j] - A * d_rows(p[j])
            wn[j] = wn[j] - A * d_lanes(p[j])
        for j in range(levels - 1):
            wu[j] = wu[j] - B * (p[j + 1] - p[j])

        @pl.when(has_above)
        def _():
            wu[levels - 1] = wu[levels - 1] + B * p[levels - 1]

        @pl.when(jnp.logical_not(has_above))
        def _():
            wu[levels - 1] = jnp.zeros((tile, tile), jnp.float32)

        for j in range(1, levels):
            p[j] = p[j] - st[j] * (A * (d_rows(we[j]) + d_lanes(wn[j])) + B * (wu[j] - wu[j - 1]))

        @pl.when(has_below)
        def _():
            wu_below[...] = wu_below[...] - B * p[0]

        p[0] = p[0] - st[0] * (A * (d_rows(we[0]) + d_lanes(wn[0])) + B * (wu[0] - wu_below[...]))
        take_strips()

        @pl.when(t == 1)
        def _():
            pick_tables(slot_source, slot_weight, pick_hot, pick_mask)
            if packed:
                for found, _, planes in stages:
                    found[:, capacity:] = jnp.zeros((len(planes), found.shape[1] - capacity), jnp.float32)

        @pl.when(t == 2)
        def _():
            land_tables(cell, land_hot)
            total[...] = jnp.zeros(total.shape, jnp.float32)

        @pl.when(t == SUBSTEPS - 1)
        def _():
            choose(0)
            hand_over(0)
            for k in range(1, EARLY):
                choose(k)

        next_strips(t)

        @pl.when(t == SUBSTEPS - 1)
        def _():
            for k in range(1, EARLY):
                add_rims(k)
                hand_over(k)

        @pl.when(t < SUBSTEPS - 1)
        def _():
            send_rims(t + 1)

        @pl.when(has_above)
        def _():
            plane_copy(t, 0).wait_recv()
            wu[levels - 1] = wu[levels - 1] - B * plane_recv[t, 0]
            p[levels - 1] = p[levels - 1] + (B * B) * (st[levels - 1] * plane_recv[t, 0])

        @pl.when(has_below)
        def _():
            plane_copy(t, 1).wait_recv()
            wu_below[...] = wu_below[...] + B * plane_recv[t, 1]
            p[0] = p[0] + (B * B) * (st[0] * plane_recv[t, 1])

        for s, (a, b) in ((0, (0, 1)), (2, (last, last - 1))):
            p[:, a, :] = p_strips[s, :levels]
            p[:, b, :] = p_strips[s, levels:]
            we[:, a, :] = w_strips[s, :levels]
        for k, (s, half) in enumerate(((3, 1), (3, 0), (1, 0), (1, 1))):
            ghost_rows[pl.ds(k, levels, stride=4), :] = p_strips[s, half * levels : (half + 1) * levels]
        for k, s in enumerate((3, 1)):
            ghost_rows[pl.ds(4 * levels + k, levels, stride=2), :] = w_strips[s, :levels]
        turned = ghost_rows[...].T
        rim = (lane == 0) | (lane == last)
        band = (lane <= 1) | (lane >= last - 1)

        def put_sides(j):
            p[j] = jnp.where(band, pltpu.roll(turned, (tile - 4 * j - 2) % tile, 1), p[j])

        put_sides(levels - 1)

        @pl.when((t < SUBSTEPS - 1) & has_above)
        def _():
            plane_send[t + 1, 1] = p[levels - 1]
            plane_copy(t + 1, 1).start()

        put_sides(0)

        @pl.when((t < SUBSTEPS - 1) & has_below)
        def _():
            plane_send[t + 1, 0] = p[0]
            plane_copy(t + 1, 0).start()

        for j in range(1, levels - 1):
            put_sides(j)
        for j in range(levels):
            wn[j] = jnp.where(rim, pltpu.roll(turned, (tile - 4 * levels - 2 * j - 1) % tile, 1), wn[j])

        return carry

    lax.fori_loop(0, SUBSTEPS, substep, 0)

    for k in range(EARLY, len(stages)):
        choose(k)
        hand_over(k)

    groups = latlon.shape[2] // BLOCK
    sums = (((1, 2), (1, 3)), ((3, 0), (0, 2, 4)))

    for n, (_, parts) in enumerate(sums):
        land(n, [payload[c][ix] for c in parts], cell, land_hot, ix, total)

    for n, (names, parts) in enumerate(sums):

        def bring_in(d, carry):
            o = lax.rem(ix + n_px - d - 1, n_px)
            for c in parts:
                got(c, o).wait_recv()
            land(n, [arrived[c][o] for c in parts], cell, land_hot, o, total)
            return carry

        lax.fori_loop(0, n_px - 1, bring_in, 0)
        for g in range(groups):
            rows = len(names) * levels
            high, low = g * rows, (groups + g) * rows
            both = total[n, high : high + rows] + total[n, low : low + rows]
            for k, q in enumerate(names):
                latlon[q, :, g * BLOCK : (g + 1) * BLOCK] = both[k * levels : (k + 1) * levels]

    def drain(t, carry):
        for s in range(4):
            near_copy(t, s).wait_send()
            diag_copy(t, s).wait_send()
            far_copy(t, s).wait_send()

        @pl.when(has_above)
        def _():
            level_copy(t, 1).wait_send()
            plane_copy(t, 1).wait_send()

        @pl.when(has_below)
        def _():
            level_copy(t, 0).wait_send()
            plane_copy(t, 0).wait_send()

        return carry

    lax.fori_loop(0, SUBSTEPS, drain, 0)

    def sent(d, carry):
        for c in range(len(payload)):
            give_copy(c, ahead(d)).wait_send()
        return carry

    lax.fori_loop(0, n_px - 1, sent, 0)


def find_slots(owner_count, slot_count, packed, owner, source, weight, slot_source, slot_weight):
    rows = owner.shape[0]
    slot_rows = slot_source.shape[0]
    names = owner[...]
    up_to = (iota((LANES, LANES), 0) <= iota((LANES, LANES), 1)).astype(jnp.bfloat16)
    ones = jnp.ones((LANES, LANES), jnp.bfloat16)
    before = (iota((rows, rows), 0) > iota((rows, rows), 1)).astype(jnp.bfloat16)

    def count(o, carry):
        place, start = carry
        named = names == o
        hot = named.astype(jnp.float32).astype(jnp.bfloat16)
        within = jnp.dot(hot, up_to, preferred_element_type=jnp.float32)
        total = jnp.dot(hot, ones, preferred_element_type=jnp.float32)
        earlier = jnp.dot(before, total.astype(jnp.bfloat16), preferred_element_type=jnp.float32)
        place = jnp.where(named, within + earlier - 1.0 + start, place)
        if packed:
            filled = jnp.sum(total, axis=0, keepdims=True)
            start = start + jnp.floor((filled + (LANES - 1.0)) / LANES) * LANES
        else:
            start = start + float(slot_count)
        return place, start

    zero = jnp.zeros(names.shape, jnp.float32)
    place, _ = lax.fori_loop(0, owner_count, count, (zero, jnp.zeros((1, LANES), jnp.float32)))
    slot = place.astype(jnp.int32)
    slot_high, slot_low = slot >> 7, slot & (LANES - 1)
    src = source[...]
    w = weight[...]
    w1 = w.astype(jnp.bfloat16).astype(jnp.float32)
    w2 = (w - w1).astype(jnp.bfloat16).astype(jnp.float32)
    w3 = w - w1 - w2
    pieces = [(src >> 7).astype(jnp.float32), (src & (LANES - 1)).astype(jnp.float32), w1, w2, w3]
    high_place, low_place = iota((slot_rows, LANES), 0), iota((LANES, LANES), 0)
    total = jnp.zeros((len(pieces) * slot_rows, LANES), jnp.float32)
    for r in range(rows):
        here = high_place == slot_high[r : r + 1]
        left = jnp.concatenate([jnp.where(here, piece[r : r + 1], 0.0) for piece in pieces], axis=0)
        right = jnp.where(low_place == slot_low[r : r + 1], 1.0, 0.0)
        total += dot_nt(left.astype(jnp.bfloat16), right.astype(jnp.bfloat16))
    part = [total[k * slot_rows : (k + 1) * slot_rows] for k in range(len(pieces))]
    slot_source[...] = (part[0] * LANES + part[1]).astype(jnp.int32)
    slot_weight[...] = part[2] + part[3] + part[4]


def split_plane(split, plane, r):
    tile = plane.shape[0]
    half = tile // 2
    h, d = parts2(plane.T)
    for k, part in enumerate((h[:half], h[half:], d[:half], d[half:])):
        split[r * half : (r + 1) * half, k * tile : (k + 1) * tile] = part


def joined(ref, row, pieces):
    return jnp.concatenate([ref[pl.ds(row + k, 1), :] for k in range(pieces)], axis=1)


def pick_tables(slot_source, slot_weight, pick_hot, pick_mask):
    lines, capacity = pick_hot.shape
    tile, half = lines // 2, pick_mask.shape[0]
    pieces = BLOCK // LANES

    def step(b, carry):
        at = pl.ds(pl.multiple_of(b * BLOCK, BLOCK), BLOCK)
        src, w = joined(slot_source, b * pieces, pieces), joined(slot_weight, b * pieces, pieces)
        x, y = src >> 7, src & (tile - 1)
        line = x + jnp.where(y >= half, tile, 0)
        pick_hot[:, at] = jnp.where(iota((lines, BLOCK), 0) == line, 1.0, 0.0).astype(jnp.bfloat16)
        pick_mask[:, at] = jnp.where(iota((half, BLOCK), 0) == (y & (half - 1)), w, 0.0)
        return carry

    lax.fori_loop(0, capacity // BLOCK, step, 0)


def pick(first, split, pick_hot, pick_mask, found):
    rows = found.shape[0]
    half, capacity = pick_mask.shape
    lines = slice(first * half, (first + rows) * half)
    width = 2 * BLOCK if capacity % (2 * BLOCK) == 0 else BLOCK
    steps = capacity // width

    def step(b, carry):
        at = pl.ds(pl.multiple_of(b * width, width), width)
        hot = pick_hot[:, at]
        line = jnp.dot(
            split[lines, :], jnp.concatenate([hot, hot], axis=0), preferred_element_type=jnp.float32
        )
        found[:, at] = jnp.sum(line.reshape(rows, half, width) * pick_mask[:, at][None], axis=1)
        return carry

    lax.fori_loop(0, steps, step, 0, unroll=steps if steps < 12 else 4)


def land_tables(cell, land_hot):
    owner_count, _, slot_count = land_hot.shape
    pieces = slot_count // LANES

    def step(o, carry):
        c = joined(cell, o * pieces, pieces)
        hot = jnp.where(iota((BLOCK, slot_count), 0) == (c & (BLOCK - 1)), 1.0, 0.0)
        land_hot[o] = hot.astype(jnp.bfloat16)
        return carry

    lax.fori_loop(0, owner_count, step, 0)


def land(q, parts, cell, land_hot, o, total):
    values = parts[0] if len(parts) == 1 else jnp.concatenate(parts, axis=0)
    rows, slot_count = values.shape
    groups = total.shape[1] // (2 * rows)
    pieces = slot_count // LANES
    group = joined(cell, o * pieces, pieces) >> 8
    h = values.astype(jnp.bfloat16).astype(jnp.float32)
    spread = [jnp.where(group == g, h, 0.0) for g in range(groups)]
    spread += [jnp.where(group == g, values - h, 0.0) for g in range(groups)]
    total[q] += dot_nt(jnp.concatenate(spread, axis=0).astype(jnp.bfloat16), land_hot[o])


def per_device(
    sizes,
    pressure,
    wind_east,
    wind_north,
    wind_up,
    stiffness,
    edge_table,
    remap_source,
    remap_weight,
    remap_owner,
    latlon_cell,
):
    levels, tile, _ = pressure.shape
    owner_count = sizes[0]
    slots = latlon_cell.shape[0]
    slot_count = slots // owner_count
    cell_count = tile * tile // 8
    count = 4 * levels
    entries = remap_source.shape[0]
    rows = entries // LANES
    capacity = -(-(entries + (owner_count - 1) * (LANES - 1)) // BLOCK) * BLOCK
    capacity = min(capacity, slots)
    room = capacity
    if capacity < slots:
        room = slot_count + ((2 << (capacity // LANES - 1).bit_length() - 1) - 1) * LANES + LANES
        room = max(room, capacity)
    slot_rows = -(-capacity // (8 * LANES)) * 8
    part_rows = (levels - 1, levels, 1, levels, levels)
    f32, i32 = jnp.float32, jnp.int32
    n = SUBSTEPS
    field = pltpu.VMEM(pressure.shape, f32)
    plane = pltpu.VMEM((tile, tile), f32)
    dma = pltpu.SemaphoreType.DMA
    in_vmem = pl.BlockSpec(memory_space=pltpu.VMEM)
    results = pl.pallas_call(
        functools.partial(whole_kernel, sizes),
        out_shape=[
            pltpu.VMEM(pressure.shape, f32),
            pltpu.VMEM((4, levels, cell_count), f32),
        ],
        in_specs=[pl.BlockSpec(memory_space=pl.ANY)] * 10,
        out_specs=[in_vmem] * 2,
        scratch_shapes=[
            pltpu.SMEM(edge_table.shape, i32),
            field,
            field,
            field,
            field,
            pltpu.VMEM((rows, LANES), i32),
            pltpu.VMEM((rows, LANES), i32),
            pltpu.VMEM((rows, LANES), f32),
            pltpu.VMEM((slots // LANES, LANES), i32),
            pltpu.VMEM((8, 2 * levels, tile), f32),
            pltpu.VMEM((n, 4, 2 * levels, tile), f32),
            pltpu.VMEM((n, 4, 2 * levels, tile), f32),
            pltpu.VMEM((n, 4, 2 * levels, tile), f32),
            pltpu.VMEM((n, 4, 2 * levels, tile), f32),
            pltpu.VMEM((n, 4, levels, tile), f32),
            pltpu.VMEM((n, 4, levels, tile), f32),
            pltpu.VMEM((4, levels, tile), f32),
            pltpu.VMEM((n, 2, 8, tile), f32),
            pltpu.VMEM((n, 2, 8, tile), f32),
            pltpu.VMEM((n, 2, tile, tile), f32),
            pltpu.VMEM((n, 2, tile, tile), f32),
            plane,
            plane,
            plane,
            pltpu.VMEM((4, 2 * levels, tile), f32),
            pltpu.VMEM((4, 2 * levels, tile), f32),
            pltpu.VMEM((4, 2 * levels, tile), f32),
            pltpu.VMEM((8, tile), f32),
            pltpu.VMEM((2, 2 * levels, tile), f32),
            pltpu.VMEM((slot_rows, LANES), i32),
            pltpu.VMEM((slot_rows, LANES), f32),
            pltpu.VMEM((2 * tile, capacity), jnp.bfloat16),
            pltpu.VMEM((tile // 2, capacity), f32),
            pltpu.VMEM((owner_count, BLOCK, slot_count), jnp.bfloat16),
            pltpu.VMEM((count * tile // 2, 4 * tile), jnp.bfloat16),
            *(pltpu.VMEM((n_rows, room), f32) for n_rows in (levels - 1, levels, levels + 1, levels)),
            *(pltpu.VMEM((owner_count, n_rows, slot_count), f32) for n_rows in part_rows),
            *(pltpu.VMEM((owner_count, n_rows, slot_count), f32) for n_rows in part_rows),
            pltpu.VMEM((2, 4 * levels * (cell_count // BLOCK), BLOCK), f32),
            dma((10,)),
            dma((2, n, 4)),
            dma((2, n, 4)),
            dma((2, n, 4)),
            dma((2, n, 2)),
            dma((2, n, 2)),
            dma((len(part_rows), owner_count)),
            dma((len(part_rows), owner_count)),
        ],
        compiler_params=pltpu.CompilerParams(
            collective_id=0, has_side_effects=True, vmem_limit_bytes=60 * 2**20
        ),
    )(
        edge_table,
        pressure,
        wind_east,
        wind_north,
        wind_up,
        stiffness,
        remap_owner.reshape(rows, LANES),
        remap_source.reshape(rows, LANES),
        remap_weight.reshape(rows, LANES),
        latlon_cell.reshape(slots // LANES, LANES),
    )
    anywhere = pl.BlockSpec(memory_space=pl.ANY)
    return pl.pallas_call(
        pass_on,
        out_shape=[jax.ShapeDtypeStruct(r.shape, f32) for r in results],
        in_specs=[in_vmem] * 2,
        out_specs=[anywhere] * 2,
        scratch_shapes=[dma((2,))],
    )(*(pltpu.with_memory_space_constraint(r, pltpu.VMEM) for r in results))


def pass_on(p, latlon, p_out, latlon_out, sems):
    copies = [
        pltpu.make_async_copy(src, dst, sems.at[k]) for k, (src, dst) in enumerate(((p, p_out), (latlon, latlon_out)))
    ]
    for copy in copies:
        copy.start()
    for copy in copies:
        copy.wait()


def solution(mesh):
    field = P("lev", "px", "py")
    entries = P(("px", "py"))
    sizes = (mesh.shape["px"], mesh.shape["py"], mesh.shape["lev"])
    return jax.shard_map(
        functools.partial(per_device, sizes),
        mesh=mesh,
        in_specs=(field,) * 5 + (P(), entries, entries, P(("px", "py"), None), entries),
        out_specs=(field, P(None, "lev", ("px", "py"))),
        check_vma=False,
    )
```

```python
import functools

import jax
import jax.numpy as jnp
from jax import lax
from jax.experimental import pallas as pl
from jax.experimental.pallas import tpu as pltpu
from jax.sharding import PartitionSpec as P

SUBSTEPS = 4
A = 0.45
B = 0.3
LANES = 128
BLOCK = 256
EARLY = 2
MESH = pl.DeviceIdType.MESH


def iota(shape, dim):
    return lax.broadcasted_iota(jnp.int32, shape, dim)


def parts2(x):
    high = x.astype(jnp.bfloat16)
    return high, (x - high.astype(jnp.float32)).astype(jnp.bfloat16)


def dot_nt(a, b):
    return lax.dot_general(a, b, (((1,), (1,)), ((), ())), preferred_element_type=jnp.float32)


def opposite(s):
    return (s + 2) & 3


SHIFT = ((-1, 0), (0, -1), (1, 0), (0, 1))
DIAGONAL = ((0, 1), (0, 3), (2, 1), (2, 3))


def whole_kernel(
    sizes,
    edges_in,
    p_in,
    we_in,
    wn_in,
    wu_in,
    st_in,
    owner_in,
    source_in,
    weight_in,
    cell_in,
    p,
    latlon,
    edges,
    we,
    wn,
    wu,
    st,
    owner,
    source,
    weight,
    cell,
    table,
    near_send,
    near_recv,
    diag_send,
    diag_recv,
    far_send,
    far_recv,
    own_relay,
    level_send,
    level_recv,
    plane_send,
    plane_recv,
    wu_below,
    flipped_cols,
    ghost_rows,
    p_strips,
    w_strips,
    st_strips,
    wu_rims,
    rim_change,
    slot_source,
    slot_weight,
    pick_hot,
    pick_mask,
    land_hot,
    split,
    picked_early,
    picked_first,
    picked_second,
    picked_third,
    payload_early,
    payload_first,
    payload_top,
    payload_second,
    payload_third,
    arrived_early,
    arrived_first,
    arrived_top,
    arrived_second,
    arrived_third,
    total,
    in_sems,
    near_sems,
    diag_sems,
    far_sems,
    level_sems,
    plane_sems,
    give_sem,
    take_sem,
):
    n_px, n_py, n_lev = sizes
    levels, tile, _ = p.shape
    last = tile - 1
    ix, iy, iz = lax.axis_index("px"), lax.axis_index("py"), lax.axis_index("lev")
    has_above, has_below = iz < n_lev - 1, iz > 0
    payload = (payload_early, payload_first, payload_top, payload_second, payload_third)
    arrived = (arrived_early, arrived_first, arrived_top, arrived_second, arrived_third)

    def place(dx, dy):
        return lax.rem(ix + dx + 2 * n_px, n_px), lax.rem(iy + dy + 2 * n_py, n_py)

    def at(dx, dy):
        x, y = place(dx, dy)
        return {"px": x, "py": y}

    others = {(d, 0) for d in range(1, n_px)}
    for dx, dy in ((0, 1), (0, -1), (0, 2), (0, -2), (1, 1), (1, -1), (-1, 1), (-1, -1)):
        others.add((dx % n_px, dy % n_py))
    beside = sorted(o for o in others if o[1])

    barrier = pltpu.get_barrier_semaphore()
    for dx, dy in beside:
        pl.semaphore_signal(barrier, inc=1, device_id=at(dx, dy), device_id_type=MESH)

    def greet(d, carry):
        pl.semaphore_signal(barrier, inc=1, device_id={"px": lax.rem(ix + d, n_px)}, device_id_type=MESH)
        return carry

    lax.fori_loop(1, n_px, greet, 0)

    @pl.when(has_above)
    def _():
        pl.semaphore_signal(barrier, inc=1, device_id={"lev": iz + 1}, device_id_type=MESH)

    @pl.when(has_below)
    def _():
        pl.semaphore_signal(barrier, inc=1, device_id={"lev": iz - 1}, device_id_type=MESH)

    loads = [
        pltpu.make_async_copy(src, dst, in_sems.at[k])
        for k, (src, dst) in enumerate(
            (
                (edges_in, edges),
                (p_in, p),
                (we_in, we),
                (wn_in, wn),
                (wu_in, wu),
                (st_in, st),
                (owner_in, owner),
                (source_in, source),
                (weight_in, weight),
                (cell_in, cell),
            )
        )
    ]
    for load in loads:
        load.start()
    def remote(src, dst, sems, index, device):
        return pltpu.make_async_remote_copy(
            src_ref=src,
            dst_ref=dst,
            send_sem=sems.at[(0,) + index],
            recv_sem=sems.at[(1,) + index],
            device_id=device,
            device_id_type=MESH,
        )

    def near_copy(t, s):
        dx, dy = SHIFT[s]
        return remote(near_send.at[t, s], near_recv.at[t, s], near_sems, (t, s), at(-dx, -dy))

    def diag_copy(t, k):
        (ax, ay), (bx, by) = SHIFT[DIAGONAL[k][0]], SHIFT[DIAGONAL[k][1]]
        return remote(diag_send.at[t, k], diag_recv.at[t, k], diag_sems, (t, k), at(-ax - bx, -ay - by))

    def far_copy(t, s):
        dx, dy = SHIFT[s]
        return remote(far_send.at[t, s], far_recv.at[t, s], far_sems, (t, s), at(-2 * dx, -2 * dy))

    def level_copy(t, up):
        return remote(
            level_send.at[t, up],
            level_recv.at[t, up],
            level_sems,
            (t, up),
            {"lev": iz + 1 if up else iz - 1},
        )

    def plane_copy(t, up):
        return remote(plane_send.at[t, up], plane_recv.at[t, up], plane_sems, (t, up), {"lev": iz + 1 if up else iz - 1})

    row, lane = iota((tile, tile), 0), iota((tile, tile), 1)
    strip_row, strip_lane = iota((2 * levels, tile), 0), iota((2 * levels, tile), 1)
    outer = strip_row < levels

    def d_rows(f):
        return jnp.where(row == last, 0.0, pltpu.roll(f, last, 0)) - jnp.where(
            row == 0, 0.0, pltpu.roll(f, 1, 0)
        )

    def d_lanes(f):
        return jnp.where(lane == last, 0.0, pltpu.roll(f, last, 1)) - jnp.where(
            lane == 0, 0.0, pltpu.roll(f, 1, 1)
        )

    def columns(deep, shallow):
        packed = jnp.zeros((tile, tile), jnp.float32)
        for j, f in enumerate(deep):
            packed = jnp.where((lane >> 2) == j, pltpu.roll(f, 4 * j + 2, 1), packed)
        base = 4 * len(deep)
        for j, f in enumerate(shallow):
            packed = jnp.where((lane >> 1) == base // 2 + j, pltpu.roll(f, base + 2 * j + 1, 1), packed)
        flipped_cols[...] = packed.T

    def column(k):
        return flipped_cols[pl.ds(k, levels, stride=4), :]

    def rim_column(k):
        return flipped_cols[pl.ds(4 * levels + k, levels, stride=2), :]

    def take_strips():
        columns([p[j] for j in range(levels)], [wn[j] for j in range(levels)])
        for s, (a, b) in ((0, (0, 1)), (2, (last, last - 1))):
            p_strips[s, :levels] = p[:, a, :]
            p_strips[s, levels:] = p[:, b, :]
            w_strips[s, :levels] = we[:, a, :]
        for s, (a, b, c) in ((1, (2, 3, 1)), (3, (1, 0, 0))):
            p_strips[s, :levels] = column(a)
            p_strips[s, levels:] = column(b)
            w_strips[s, :levels] = rim_column(c)

    def code(x, y, s):
        c = edges[x, y, s]
        return c & 3, c >> 2

    def wanted(s, turn):
        return (s + 2 + turn) & 3

    def sign(s, turn):
        plus = ((turn + 1) & 3) < 2 if s % 2 == 0 else turn < 2
        return jnp.where(plus, 1.0, -1.0) * (1.0 if s < 2 else -1.0)

    def rim_sign(w):
        return jnp.where(w < 2, 1.0, -1.0) if not isinstance(w, int) else (1.0 if w < 2 else -1.0)

    loads[0].wait()
    near_plan = []
    for s in range(4):
        dx, dy = SHIFT[s]
        turn, flip = code(*place(-dx, -dy), s)
        near_plan.append((flip * 4 + wanted(s, turn), sign(s, turn)))

    def relay_plan(s, w, ax, ay):
        turn_a, flip_a = code(*place(ax, ay), s)
        turn_b, flip_b = code(*place(ax + SHIFT[s][0], ay + SHIFT[s][1]), w)
        return (flip_a ^ flip_b) * 4 + wanted(w, turn_b), sign(s, turn_a) * rim_sign(w)

    def relay_to(s, w):
        return relay_plan(s, w, -SHIFT[s][0] - SHIFT[w][0], -SHIFT[s][1] - SHIFT[w][1])

    diag_plan = [(relay_to(a, b), relay_to(b, a)) for a, b in DIAGONAL]
    far_plan = [relay_to(s, s) for s in range(4)]
    own_plan = [relay_to(s, opposite(s)) for s in range(4)]
    mine = [wanted(s, code(ix, iy, s)[0]) for s in range(4)]

    def relayed(t, s):
        found = own_relay[s]
        for k, (a, b) in enumerate(DIAGONAL):
            if s == a:
                found = jnp.where(mine[s] == b, diag_recv[t, k, :levels], found)
            if s == b:
                found = jnp.where(mine[s] == a, diag_recv[t, k, levels:], found)
        return jnp.where(mine[s] == s, far_recv[t, s], found)

    def send_rims(t, first=False):
        strips = [p_strips[s] for s in range(4)]
        rims = []
        for s in range(4):
            turned = A * pltpu.roll(strips[s], levels, 0)
            rims.append(jnp.where(outer, w_strips[s] - rim_sign(s) * turned, turned))
        for s in range(4):
            table[s] = rims[s]
            table[4 + s] = jnp.take_along_axis(rims[s], last - strip_lane, axis=1)
        for k in range(4):
            for half in range(2):
                which, sgn = diag_plan[k][half]
                diag_send[t, k, half * levels : (half + 1) * levels] = sgn * table[which, levels:]
            diag_copy(t, k).start()
        for s in range(4):
            k, sgn = near_plan[s]
            rim = table[k]
            near_send[t, s] = jnp.where(outer, sgn * rim, rim)
            near_copy(t, s).start()
        for s in range(4):
            k, sgn = far_plan[s]
            far_send[t, s] = sgn * table[k, levels:]
            far_copy(t, s).start()
        for s in range(4):
            k, sgn = own_plan[s]
            own_relay[s] = sgn * table[k, levels:]
            for up, level in ((1, levels - 1), (0, 0)):
                level_send[t, up, 2 * s : 2 * s + 2] = p_strips[s, pl.ds(level, 2, stride=levels), :]
        if first:
            level_send[t, 1] = level_send[t, 1] + wu_rims[...] * (1.0 / B)

        @pl.when(has_above)
        def _():
            level_copy(t, 1).start()

        @pl.when(has_below)
        def _():
            level_copy(t, 0).start()

    def corners(s, low, high):
        found = jnp.zeros((2 * levels, tile), jnp.float32)
        for depth in range(2):
            start = depth if s < 2 else last - depth
            for e in range(2):
                for pair, end in ((low, e), (high, last - e)):
                    moved = pltpu.roll(pair[depth ^ e], (end - start) % tile, 1) if end != start else pair[depth ^ e]
                    here = (strip_lane == end) & (outer if depth == 0 else jnp.logical_not(outer))
                    found = jnp.where(here, moved, found)
        return found

    def next_strips(t):
        for s in range(4):
            near_copy(t, s).wait_recv()
        for k in range(4):
            diag_copy(t, k).wait_recv()
        for s in range(4):
            far_copy(t, s).wait_recv()

        @pl.when(has_above)
        def _():
            level_copy(t, 0).wait_recv()

        @pl.when(has_below)
        def _():
            level_copy(t, 1).wait_recv()

        zero = jnp.zeros((levels, tile), jnp.float32)
        ghosts = []
        for s in range(4):
            ghosts.append(near_recv[t, s] + jnp.concatenate([relayed(t, s), zero], axis=0))
        pairs = [(g, pltpu.roll(g, levels, 0)) for g in ghosts]
        for s in range(2):
            rim_change[s] = jnp.where(outer, pairs[s][1], -ghosts[s + 2])
        for s in range(4):
            low, high = (pairs[1], pairs[3]) if s % 2 == 0 else (pairs[0], pairs[2])
            across = jnp.zeros((2 * levels, tile), jnp.float32)
            for depth in range(2):
                below, above = level_recv[t, 1], level_recv[t, 0]
                k = 2 * s + depth
                across = jnp.where(strip_row == depth * levels, below[k : k + 1], across)
                across = across + jnp.where(strip_row == (depth + 1) * levels - 1, above[k : k + 1], 0.0)
            p_strips[s] = p_strips[s] + st_strips[s] * (
                A * (ghosts[s] + corners(s, low, high)) + (B * B) * across
            )
            w_strips[s] = jnp.where(outer, w_strips[s] + rim_sign(s) * pairs[s][1], 0.0)

    def give_copy(c, o):
        return pltpu.make_async_remote_copy(
            src_ref=payload[c].at[o],
            dst_ref=arrived[c].at[ix],
            send_sem=give_sem.at[c, o],
            recv_sem=take_sem.at[c, ix],
            device_id={"px": o},
            device_id_type=MESH,
        )

    def got(c, o):
        return pltpu.make_async_remote_copy(
            src_ref=payload[c].at[o],
            dst_ref=arrived[c].at[o],
            send_sem=give_sem.at[c, o],
            recv_sem=take_sem.at[c, o],
            device_id={"px": o},
            device_id_type=MESH,
        )

    w_strips[...] = jnp.zeros(w_strips.shape, jnp.float32)
    ghost_rows[...] = jnp.zeros((tile, tile), jnp.float32)

    wu_below[...] = jnp.zeros((tile, tile), jnp.float32)

    @pl.when(jnp.logical_not(has_below))
    def _():
        level_recv[:, 1] = jnp.zeros((SUBSTEPS, 8, tile), jnp.float32)

    @pl.when(jnp.logical_not(has_above))
    def _():
        level_recv[:, 0] = jnp.zeros((SUBSTEPS, 8, tile), jnp.float32)

    for load in loads[1:5]:
        load.wait()
    columns([wu[levels - 1]], [])
    for k, place_of in enumerate((0, 1, None, None, last, last - 1)):
        if place_of is not None:
            wu_rims[k : k + 1] = wu[levels - 1, place_of : place_of + 1, :]
    for k, place_of in ((2, 2), (3, 3), (6, 1), (7, 0)):
        wu_rims[k : k + 1] = flipped_cols[place_of : place_of + 1, :]
    take_strips()
    plane_send[0, 1] = p[levels - 1] + wu[levels - 1] * (1.0 / B)
    plane_send[0, 0] = p[0]
    pl.semaphore_wait(
        barrier, n_px - 1 + len(beside) + has_above.astype(jnp.int32) + has_below.astype(jnp.int32)
    )
    send_rims(0, True)

    @pl.when(has_above)
    def _():
        plane_copy(0, 1).start()

    @pl.when(has_below)
    def _():
        plane_copy(0, 0).start()

    for load in loads[5:]:
        load.wait()
    columns([st[j] for j in range(levels)], [])
    for s, (a, b) in ((0, (0, 1)), (2, (last, last - 1))):
        st_strips[s, :levels] = st[:, a, :]
        st_strips[s, levels:] = st[:, b, :]
    for s, (a, b) in ((1, (2, 3)), (3, (1, 0))):
        st_strips[s, :levels] = column(a)
        st_strips[s, levels:] = column(b)
    slot_count = payload_first.shape[2]
    top = levels - 1
    every = tuple(range(levels))
    stages = (
        (picked_early, ((0, 0, top),), [(wu, l) for l in every[:top]]),
        (picked_first, ((1, 0, levels),), [(we, l) for l in every]),
        (picked_second, ((3, 0, levels), (2, levels, levels + 1)), [(wn, l) for l in every] + [(wu, top)]),
        (picked_third, ((4, 0, levels),), [(p, l) for l in every]),
    )
    capacity = pick_hot.shape[1]
    packed = capacity < n_px * slot_count
    find_slots(n_px, slot_count, packed, owner, source, weight, slot_source, slot_weight)
    steps = (capacity // LANES - 1).bit_length()
    if packed:
        filled = [
            jnp.sum(jnp.sum((owner[...] == o).astype(jnp.int32), axis=0, keepdims=True), axis=1, keepdims=True)
            for o in range(n_px)
        ]

    def part_of(o, found, low, high):
        if not packed:
            return found[low:high, pl.ds(pl.multiple_of(o * slot_count, LANES), slot_count)]
        start, count = jnp.zeros((1, 1), jnp.int32), jnp.zeros((1, 1), jnp.int32)
        for k, n in enumerate(filled):
            start = start + jnp.where(k < o, (n + (LANES - 1)) >> 7, 0)
            count = count + jnp.where(k == o, n, 0)
        part = found[low:high, :]
        for k in reversed(range(steps)):
            width = slot_count + ((1 << k) - 1) * LANES
            part = jnp.where(
                ((start >> k) & 1) == 1, part[:, LANES << k : (LANES << k) + width], part[:, :width]
            )
        return jnp.where(iota(part.shape, 1) < count, part, 0.0)

    def ahead(d):
        return lax.rem(ix + d + 1, n_px)

    def choose(k):
        found, _, planes = stages[k]
        first = sum(len(stage[2]) for stage in stages[:k])
        for n, (field, l) in enumerate(planes):
            split_plane(split, field[l], first + n)
        pick(first, split, pick_hot, pick_mask, found)

    def add_rims(k):
        found = stages[k][0]

        def step(b, carry):
            at = pl.ds(pl.multiple_of(b * LANES, LANES), LANES)
            src = jnp.broadcast_to(slot_source[pl.ds(b, 1), :], (2 * levels, LANES))
            across, along = (src >> 7, src & last) if k == 1 else (src & last, src >> 7)
            change = jnp.take_along_axis(rim_change[k - 1], along, axis=1) * slot_weight[pl.ds(b, 1), :]
            change = jnp.where(across == jnp.where(outer, 0, last), change, 0.0)
            found[:, at] = found[:, at] + (change[:levels] + change[levels:])
            return carry

        lax.fori_loop(0, capacity // LANES, step, 0, unroll=4)

    def hand_over(k):
        found, parts, planes = stages[k]

        def lay_out(o):
            whole = part_of(o, found, 0, len(planes))
            for c, low, high in parts:
                payload[c][o] = whole[low:high]

        def send(d, carry):
            lay_out(ahead(d))
            for c, _, _ in parts:
                give_copy(c, ahead(d)).start()
            return carry

        lax.fori_loop(0, n_px - 1, send, 0)
        lay_out(ix)

    def substep(t, carry):
        for j in range(levels - 1):
            wu[j] = wu[j] - B * (p[j + 1] - p[j])

        @pl.when(t == SUBSTEPS - 1)
        def _():
            choose(0)
            hand_over(0)

        for j in range(levels):
            we[j] = we[j] - A * d_rows(p[j])
            wn[j] = wn[j] - A * d_lanes(p[j])

        @pl.when(has_above)
        def _():
            wu[levels - 1] = wu[levels - 1] + B * p[levels - 1]

        @pl.when(jnp.logical_not(has_above))
        def _():
            wu[levels - 1] = jnp.zeros((tile, tile), jnp.float32)

        for j in range(1, levels):
            p[j] = p[j] - st[j] * (A * (d_rows(we[j]) + d_lanes(wn[j])) + B * (wu[j] - wu[j - 1]))

        @pl.when(has_below)
        def _():
            wu_below[...] = wu_below[...] - B * p[0]

        p[0] = p[0] - st[0] * (A * (d_rows(we[0]) + d_lanes(wn[0])) + B * (wu[0] - wu_below[...]))
        take_strips()

        @pl.when(t == 1)
        def _():
            pick_tables(slot_source, slot_weight, pick_hot, pick_mask)
            if packed:
                for found, _, planes in stages:
                    found[:, capacity:] = jnp.zeros((len(planes), found.shape[1] - capacity), jnp.float32)

        @pl.when(t == 2)
        def _():
            land_tables(cell, land_hot)
            total[...] = jnp.zeros(total.shape, jnp.float32)

        @pl.when(t == SUBSTEPS - 1)
        def _():
            for k in range(1, EARLY):
                choose(k)

        next_strips(t)

        @pl.when(t == SUBSTEPS - 1)
        def _():
            for k in range(1, EARLY):
                add_rims(k)
                hand_over(k)

        @pl.when(t < SUBSTEPS - 1)
        def _():
            send_rims(t + 1)

        @pl.when(has_above)
        def _():
            plane_copy(t, 0).wait_recv()
            wu[levels - 1] = wu[levels - 1] - B * plane_recv[t, 0]
            p[levels - 1] = p[levels - 1] + (B * B) * (st[levels - 1] * plane_recv[t, 0])

        @pl.when(has_below)
        def _():
            plane_copy(t, 1).wait_recv()
            wu_below[...] = wu_below[...] + B * plane_recv[t, 1]
            p[0] = p[0] + (B * B) * (st[0] * plane_recv[t, 1])

        for s, (a, b) in ((0, (0, 1)), (2, (last, last - 1))):
            p[:, a, :] = p_strips[s, :levels]
            p[:, b, :] = p_strips[s, levels:]
            we[:, a, :] = w_strips[s, :levels]
        for k, (s, half) in enumerate(((3, 1), (3, 0), (1, 0), (1, 1))):
            ghost_rows[pl.ds(k, levels, stride=4), :] = p_strips[s, half * levels : (half + 1) * levels]
        for k, s in enumerate((3, 1)):
            ghost_rows[pl.ds(4 * levels + k, levels, stride=2), :] = w_strips[s, :levels]
        turned = ghost_rows[...].T
        rim = (lane == 0) | (lane == last)
        band = (lane <= 1) | (lane >= last - 1)

        def put_sides(j):
            p[j] = jnp.where(band, pltpu.roll(turned, (tile - 4 * j - 2) % tile, 1), p[j])

        put_sides(levels - 1)

        @pl.when((t < SUBSTEPS - 1) & has_above)
        def _():
            plane_send[t + 1, 1] = p[levels - 1]
            plane_copy(t + 1, 1).start()

        put_sides(0)

        @pl.when((t < SUBSTEPS - 1) & has_below)
        def _():
            plane_send[t + 1, 0] = p[0]
            plane_copy(t + 1, 0).start()

        for j in range(1, levels - 1):
            put_sides(j)
        for j in range(levels):
            wn[j] = jnp.where(rim, pltpu.roll(turned, (tile - 4 * levels - 2 * j - 1) % tile, 1), wn[j])

        return carry

    lax.fori_loop(0, SUBSTEPS, substep, 0)

    for k in range(EARLY, len(stages)):
        choose(k)
        hand_over(k)

    groups = latlon.shape[2] // BLOCK
    sums = (((1, 2), (1, 3)), ((3, 0), (0, 2, 4)))

    for n, (_, parts) in enumerate(sums):
        land(n, [payload[c][ix] for c in parts], cell, land_hot, ix, total)

    for n, (names, parts) in enumerate(sums):

        def bring_in(d, carry):
            o = lax.rem(ix + n_px - d - 1, n_px)
            for c in parts:
                got(c, o).wait_recv()
            land(n, [arrived[c][o] for c in parts], cell, land_hot, o, total)
            return carry

        lax.fori_loop(0, n_px - 1, bring_in, 0)
        for g in range(groups):
            rows = len(names) * levels
            high, low = g * rows, (groups + g) * rows
            both = total[n, high : high + rows] + total[n, low : low + rows]
            for k, q in enumerate(names):
                latlon[q, :, g * BLOCK : (g + 1) * BLOCK] = both[k * levels : (k + 1) * levels]

    def drain(t, carry):
        for s in range(4):
            near_copy(t, s).wait_send()
            diag_copy(t, s).wait_send()
            far_copy(t, s).wait_send()

        @pl.when(has_above)
        def _():
            level_copy(t, 1).wait_send()
            plane_copy(t, 1).wait_send()

        @pl.when(has_below)
        def _():
            level_copy(t, 0).wait_send()
            plane_copy(t, 0).wait_send()

        return carry

    lax.fori_loop(0, SUBSTEPS, drain, 0)

    def sent(d, carry):
        for c in range(len(payload)):
            give_copy(c, ahead(d)).wait_send()
        return carry

    lax.fori_loop(0, n_px - 1, sent, 0)


def find_slots(owner_count, slot_count, packed, owner, source, weight, slot_source, slot_weight):
    rows = owner.shape[0]
    slot_rows = slot_source.shape[0]
    names = owner[...]
    up_to = (iota((LANES, LANES), 0) <= iota((LANES, LANES), 1)).astype(jnp.bfloat16)
    ones = jnp.ones((LANES, LANES), jnp.bfloat16)
    before = (iota((rows, rows), 0) > iota((rows, rows), 1)).astype(jnp.bfloat16)

    def count(o, carry):
        place, start = carry
        named = names == o
        hot = named.astype(jnp.float32).astype(jnp.bfloat16)
        within = jnp.dot(hot, up_to, preferred_element_type=jnp.float32)
        total = jnp.dot(hot, ones, preferred_element_type=jnp.float32)
        earlier = jnp.dot(before, total.astype(jnp.bfloat16), preferred_element_type=jnp.float32)
        place = jnp.where(named, within + earlier - 1.0 + start, place)
        if packed:
            filled = jnp.sum(total, axis=0, keepdims=True)
            start = start + jnp.floor((filled + (LANES - 1.0)) / LANES) * LANES
        else:
            start = start + float(slot_count)
        return place, start

    zero = jnp.zeros(names.shape, jnp.float32)
    place, _ = lax.fori_loop(0, owner_count, count, (zero, jnp.zeros((1, LANES), jnp.float32)))
    slot = place.astype(jnp.int32)
    slot_high, slot_low = slot >> 7, slot & (LANES - 1)
    src = source[...]
    w = weight[...]
    w1 = w.astype(jnp.bfloat16).astype(jnp.float32)
    w2 = (w - w1).astype(jnp.bfloat16).astype(jnp.float32)
    w3 = w - w1 - w2
    pieces = [(src >> 7).astype(jnp.float32), (src & (LANES - 1)).astype(jnp.float32), w1, w2, w3]
    high_place, low_place = iota((slot_rows, LANES), 0), iota((LANES, LANES), 0)
    total = jnp.zeros((len(pieces) * slot_rows, LANES), jnp.float32)
    for r in range(rows):
        here = high_place == slot_high[r : r + 1]
        left = jnp.concatenate([jnp.where(here, piece[r : r + 1], 0.0) for piece in pieces], axis=0)
        right = jnp.where(low_place == slot_low[r : r + 1], 1.0, 0.0)
        total += dot_nt(left.astype(jnp.bfloat16), right.astype(jnp.bfloat16))
    part = [total[k * slot_rows : (k + 1) * slot_rows] for k in range(len(pieces))]
    slot_source[...] = (part[0] * LANES + part[1]).astype(jnp.int32)
    slot_weight[...] = part[2] + part[3] + part[4]


def split_plane(split, plane, r):
    tile = plane.shape[0]
    half = tile // 2
    h, d = parts2(plane.T)
    for k, part in enumerate((h[:half], h[half:], d[:half], d[half:])):
        split[r * half : (r + 1) * half, k * tile : (k + 1) * tile] = part


def joined(ref, row, pieces):
    return jnp.concatenate([ref[pl.ds(row + k, 1), :] for k in range(pieces)], axis=1)


def pick_tables(slot_source, slot_weight, pick_hot, pick_mask):
    lines, capacity = pick_hot.shape
    tile, half = lines // 2, pick_mask.shape[0]
    pieces = BLOCK // LANES

    def step(b, carry):
        at = pl.ds(pl.multiple_of(b * BLOCK, BLOCK), BLOCK)
        src, w = joined(slot_source, b * pieces, pieces), joined(slot_weight, b * pieces, pieces)
        x, y = src >> 7, src & (tile - 1)
        line = x + jnp.where(y >= half, tile, 0)
        pick_hot[:, at] = jnp.where(iota((lines, BLOCK), 0) == line, 1.0, 0.0).astype(jnp.bfloat16)
        pick_mask[:, at] = jnp.where(iota((half, BLOCK), 0) == (y & (half - 1)), w, 0.0)
        return carry

    lax.fori_loop(0, capacity // BLOCK, step, 0)


def pick(first, split, pick_hot, pick_mask, found):
    rows = found.shape[0]
    half, capacity = pick_mask.shape
    lines = slice(first * half, (first + rows) * half)
    width = 2 * BLOCK if capacity % (2 * BLOCK) == 0 else BLOCK
    steps = capacity // width

    def step(b, carry):
        at = pl.ds(pl.multiple_of(b * width, width), width)
        hot = pick_hot[:, at]
        line = jnp.dot(
            split[lines, :], jnp.concatenate([hot, hot], axis=0), preferred_element_type=jnp.float32
        )
        found[:, at] = jnp.sum(line.reshape(rows, half, width) * pick_mask[:, at][None], axis=1)
        return carry

    lax.fori_loop(0, steps, step, 0, unroll=steps if steps < 12 else 4)


def land_tables(cell, land_hot):
    owner_count, _, slot_count = land_hot.shape
    pieces = slot_count // LANES

    def step(o, carry):
        c = joined(cell, o * pieces, pieces)
        hot = jnp.where(iota((BLOCK, slot_count), 0) == (c & (BLOCK - 1)), 1.0, 0.0)
        land_hot[o] = hot.astype(jnp.bfloat16)
        return carry

    lax.fori_loop(0, owner_count, step, 0)


def land(q, parts, cell, land_hot, o, total):
    values = parts[0] if len(parts) == 1 else jnp.concatenate(parts, axis=0)
    rows, slot_count = values.shape
    groups = total.shape[1] // (2 * rows)
    pieces = slot_count // LANES
    group = joined(cell, o * pieces, pieces) >> 8
    h = values.astype(jnp.bfloat16).astype(jnp.float32)
    spread = [jnp.where(group == g, h, 0.0) for g in range(groups)]
    spread += [jnp.where(group == g, values - h, 0.0) for g in range(groups)]
    total[q] += dot_nt(jnp.concatenate(spread, axis=0).astype(jnp.bfloat16), land_hot[o])


def per_device(
    sizes,
    pressure,
    wind_east,
    wind_north,
    wind_up,
    stiffness,
    edge_table,
    remap_source,
    remap_weight,
    remap_owner,
    latlon_cell,
):
    levels, tile, _ = pressure.shape
    owner_count = sizes[0]
    slots = latlon_cell.shape[0]
    slot_count = slots // owner_count
    cell_count = tile * tile // 8
    count = 4 * levels
    entries = remap_source.shape[0]
    rows = entries // LANES
    capacity = -(-(entries + (owner_count - 1) * (LANES - 1)) // BLOCK) * BLOCK
    capacity = min(capacity, slots)
    room = capacity
    if capacity < slots:
        room = slot_count + ((2 << (capacity // LANES - 1).bit_length() - 1) - 1) * LANES + LANES
        room = max(room, capacity)
    slot_rows = -(-capacity // (8 * LANES)) * 8
    part_rows = (levels - 1, levels, 1, levels, levels)
    f32, i32 = jnp.float32, jnp.int32
    n = SUBSTEPS
    field = pltpu.VMEM(pressure.shape, f32)
    plane = pltpu.VMEM((tile, tile), f32)
    dma = pltpu.SemaphoreType.DMA
    in_vmem = pl.BlockSpec(memory_space=pltpu.VMEM)
    results = pl.pallas_call(
        functools.partial(whole_kernel, sizes),
        out_shape=[
            pltpu.VMEM(pressure.shape, f32),
            pltpu.VMEM((4, levels, cell_count), f32),
        ],
        in_specs=[pl.BlockSpec(memory_space=pl.ANY)] * 10,
        out_specs=[in_vmem] * 2,
        scratch_shapes=[
            pltpu.SMEM(edge_table.shape, i32),
            field,
            field,
            field,
            field,
            pltpu.VMEM((rows, LANES), i32),
            pltpu.VMEM((rows, LANES), i32),
            pltpu.VMEM((rows, LANES), f32),
            pltpu.VMEM((slots // LANES, LANES), i32),
            pltpu.VMEM((8, 2 * levels, tile), f32),
            pltpu.VMEM((n, 4, 2 * levels, tile), f32),
            pltpu.VMEM((n, 4, 2 * levels, tile), f32),
            pltpu.VMEM((n, 4, 2 * levels, tile), f32),
            pltpu.VMEM((n, 4, 2 * levels, tile), f32),
            pltpu.VMEM((n, 4, levels, tile), f32),
            pltpu.VMEM((n, 4, levels, tile), f32),
            pltpu.VMEM((4, levels, tile), f32),
            pltpu.VMEM((n, 2, 8, tile), f32),
            pltpu.VMEM((n, 2, 8, tile), f32),
            pltpu.VMEM((n, 2, tile, tile), f32),
            pltpu.VMEM((n, 2, tile, tile), f32),
            plane,
            plane,
            plane,
            pltpu.VMEM((4, 2 * levels, tile), f32),
            pltpu.VMEM((4, 2 * levels, tile), f32),
            pltpu.VMEM((4, 2 * levels, tile), f32),
            pltpu.VMEM((8, tile), f32),
            pltpu.VMEM((2, 2 * levels, tile), f32),
            pltpu.VMEM((slot_rows, LANES), i32),
            pltpu.VMEM((slot_rows, LANES), f32),
            pltpu.VMEM((2 * tile, capacity), jnp.bfloat16),
            pltpu.VMEM((tile // 2, capacity), f32),
            pltpu.VMEM((owner_count, BLOCK, slot_count), jnp.bfloat16),
            pltpu.VMEM((count * tile // 2, 4 * tile), jnp.bfloat16),
            *(pltpu.VMEM((n_rows, room), f32) for n_rows in (levels - 1, levels, levels + 1, levels)),
            *(pltpu.VMEM((owner_count, n_rows, slot_count), f32) for n_rows in part_rows),
            *(pltpu.VMEM((owner_count, n_rows, slot_count), f32) for n_rows in part_rows),
            pltpu.VMEM((2, 4 * levels * (cell_count // BLOCK), BLOCK), f32),
            dma((10,)),
            dma((2, n, 4)),
            dma((2, n, 4)),
            dma((2, n, 4)),
            dma((2, n, 2)),
            dma((2, n, 2)),
            dma((len(part_rows), owner_count)),
            dma((len(part_rows), owner_count)),
        ],
        compiler_params=pltpu.CompilerParams(
            collective_id=0, has_side_effects=True, vmem_limit_bytes=60 * 2**20
        ),
    )(
        edge_table,
        pressure,
        wind_east,
        wind_north,
        wind_up,
        stiffness,
        remap_owner.reshape(rows, LANES),
        remap_source.reshape(rows, LANES),
        remap_weight.reshape(rows, LANES),
        latlon_cell.reshape(slots // LANES, LANES),
    )
    anywhere = pl.BlockSpec(memory_space=pl.ANY)
    return pl.pallas_call(
        pass_on,
        out_shape=[jax.ShapeDtypeStruct(r.shape, f32) for r in results],
        in_specs=[in_vmem] * 2,
        out_specs=[anywhere] * 2,
        scratch_shapes=[dma((2,))],
    )(*(pltpu.with_memory_space_constraint(r, pltpu.VMEM) for r in results))


def pass_on(p, latlon, p_out, latlon_out, sems):
    copies = [
        pltpu.make_async_copy(src, dst, sems.at[k]) for k, (src, dst) in enumerate(((p, p_out), (latlon, latlon_out)))
    ]
    for copy in copies:
        copy.start()
    for copy in copies:
        copy.wait()


def solution(mesh):
    field = P("lev", "px", "py")
    entries = P(("px", "py"))
    sizes = (mesh.shape["px"], mesh.shape["py"], mesh.shape["lev"])
    return jax.shard_map(
        functools.partial(per_device, sizes),
        mesh=mesh,
        in_specs=(field,) * 5 + (P(), entries, entries, P(("px", "py"), None), entries),
        out_specs=(field, P(None, "lev", ("px", "py"))),
        check_vma=False,
    )
```

```python
import functools

import jax
import jax.numpy as jnp
from jax import lax
from jax.experimental import pallas as pl
from jax.experimental.pallas import tpu as pltpu
from jax.sharding import PartitionSpec as P

SUBSTEPS = 4
A = 0.45
B = 0.3
LANES = 128
BLOCK = 256
EARLY = 2
MESH = pl.DeviceIdType.MESH


def iota(shape, dim):
    return lax.broadcasted_iota(jnp.int32, shape, dim)


def parts2(x):
    high = x.astype(jnp.bfloat16)
    return high, (x - high.astype(jnp.float32)).astype(jnp.bfloat16)


def dot_nt(a, b):
    return lax.dot_general(a, b, (((1,), (1,)), ((), ())), preferred_element_type=jnp.float32)


def opposite(s):
    return (s + 2) & 3


SHIFT = ((-1, 0), (0, -1), (1, 0), (0, 1))
DIAGONAL = ((0, 1), (0, 3), (2, 1), (2, 3))


def whole_kernel(
    sizes,
    edges_in,
    p_in,
    we_in,
    wn_in,
    wu_in,
    st_in,
    owner_in,
    source_in,
    weight_in,
    cell_in,
    p,
    latlon,
    edges,
    we,
    wn,
    wu,
    st,
    owner,
    source,
    weight,
    cell,
    table,
    near_send,
    near_recv,
    diag_send,
    diag_recv,
    far_send,
    far_recv,
    own_relay,
    level_send,
    level_recv,
    plane_send,
    plane_recv,
    wu_below,
    flipped_cols,
    ghost_rows,
    p_strips,
    w_strips,
    st_strips,
    wu_rims,
    rim_change,
    slot_source,
    slot_weight,
    pick_hot,
    pick_mask,
    land_hot,
    split,
    picked_early,
    picked_first,
    picked_second,
    picked_third,
    payload_early,
    payload_first,
    payload_top,
    payload_second,
    payload_third,
    arrived_early,
    arrived_first,
    arrived_top,
    arrived_second,
    arrived_third,
    total,
    in_sems,
    near_sems,
    diag_sems,
    far_sems,
    level_sems,
    plane_sems,
    give_sem,
    take_sem,
):
    n_px, n_py, n_lev = sizes
    levels, tile, _ = p.shape
    last = tile - 1
    ix, iy, iz = lax.axis_index("px"), lax.axis_index("py"), lax.axis_index("lev")
    has_above, has_below = iz < n_lev - 1, iz > 0
    payload = (payload_early, payload_first, payload_top, payload_second, payload_third)
    arrived = (arrived_early, arrived_first, arrived_top, arrived_second, arrived_third)

    def place(dx, dy):
        return lax.rem(ix + dx + 2 * n_px, n_px), lax.rem(iy + dy + 2 * n_py, n_py)

    def at(dx, dy):
        x, y = place(dx, dy)
        return {"px": x, "py": y}

    others = {(d, 0) for d in range(1, n_px)}
    for dx, dy in ((0, 1), (0, -1), (0, 2), (0, -2), (1, 1), (1, -1), (-1, 1), (-1, -1)):
        others.add((dx % n_px, dy % n_py))
    beside = sorted(o for o in others if o[1])

    barrier = pltpu.get_barrier_semaphore()
    for dx, dy in beside:
        pl.semaphore_signal(barrier, inc=1, device_id=at(dx, dy), device_id_type=MESH)

    def greet(d, carry):
        pl.semaphore_signal(barrier, inc=1, device_id={"px": lax.rem(ix + d, n_px)}, device_id_type=MESH)
        return carry

    lax.fori_loop(1, n_px, greet, 0)

    @pl.when(has_above)
    def _():
        pl.semaphore_signal(barrier, inc=1, device_id={"lev": iz + 1}, device_id_type=MESH)

    @pl.when(has_below)
    def _():
        pl.semaphore_signal(barrier, inc=1, device_id={"lev": iz - 1}, device_id_type=MESH)

    loads = [
        pltpu.make_async_copy(src, dst, in_sems.at[k])
        for k, (src, dst) in enumerate(
            (
                (edges_in, edges),
                (p_in, p),
                (we_in, we),
                (wn_in, wn),
                (wu_in, wu),
                (st_in, st),
                (owner_in, owner),
                (source_in, source),
                (weight_in, weight),
                (cell_in, cell),
            )
        )
    ]
    for load in loads:
        load.start()
    def remote(src, dst, sems, index, device):
        return pltpu.make_async_remote_copy(
            src_ref=src,
            dst_ref=dst,
            send_sem=sems.at[(0,) + index],
            recv_sem=sems.at[(1,) + index],
            device_id=device,
            device_id_type=MESH,
        )

    def near_copy(t, s):
        dx, dy = SHIFT[s]
        return remote(near_send.at[t, s], near_recv.at[t, s], near_sems, (t, s), at(-dx, -dy))

    def diag_copy(t, k):
        (ax, ay), (bx, by) = SHIFT[DIAGONAL[k][0]], SHIFT[DIAGONAL[k][1]]
        return remote(diag_send.at[t, k], diag_recv.at[t, k], diag_sems, (t, k), at(-ax - bx, -ay - by))

    def far_copy(t, s):
        dx, dy = SHIFT[s]
        return remote(far_send.at[t, s], far_recv.at[t, s], far_sems, (t, s), at(-2 * dx, -2 * dy))

    def level_copy(t, up):
        return remote(
            level_send.at[t, up],
            level_recv.at[t, up],
            level_sems,
            (t, up),
            {"lev": iz + 1 if up else iz - 1},
        )

    def plane_copy(t, up):
        return remote(plane_send.at[t, up], plane_recv.at[t, up], plane_sems, (t, up), {"lev": iz + 1 if up else iz - 1})

    row, lane = iota((tile, tile), 0), iota((tile, tile), 1)
    strip_row, strip_lane = iota((2 * levels, tile), 0), iota((2 * levels, tile), 1)
    outer = strip_row < levels

    def d_rows(f):
        return jnp.where(row == last, 0.0, pltpu.roll(f, last, 0)) - jnp.where(
            row == 0, 0.0, pltpu.roll(f, 1, 0)
        )

    def d_lanes(f):
        return jnp.where(lane == last, 0.0, pltpu.roll(f, last, 1)) - jnp.where(
            lane == 0, 0.0, pltpu.roll(f, 1, 1)
        )

    def columns(deep, shallow):
        packed = jnp.zeros((tile, tile), jnp.float32)
        for j, f in enumerate(deep):
            packed = jnp.where((lane >> 2) == j, pltpu.roll(f, 4 * j + 2, 1), packed)
        base = 4 * len(deep)
        for j, f in enumerate(shallow):
            packed = jnp.where((lane >> 1) == base // 2 + j, pltpu.roll(f, base + 2 * j + 1, 1), packed)
        flipped_cols[...] = packed.T

    def column(k):
        return flipped_cols[pl.ds(k, levels, stride=4), :]

    def rim_column(k):
        return flipped_cols[pl.ds(4 * levels + k, levels, stride=2), :]

    def take_strips():
        columns([p[j] for j in range(levels)], [wn[j] for j in range(levels)])
        for s, (a, b) in ((0, (0, 1)), (2, (last, last - 1))):
            p_strips[s, :levels] = p[:, a, :]
            p_strips[s, levels:] = p[:, b, :]
            w_strips[s, :levels] = we[:, a, :]
        for s, (a, b, c) in ((1, (2, 3, 1)), (3, (1, 0, 0))):
            p_strips[s, :levels] = column(a)
            p_strips[s, levels:] = column(b)
            w_strips[s, :levels] = rim_column(c)

    def code(x, y, s):
        c = edges[x, y, s]
        return c & 3, c >> 2

    def wanted(s, turn):
        return (s + 2 + turn) & 3

    def sign(s, turn):
        plus = ((turn + 1) & 3) < 2 if s % 2 == 0 else turn < 2
        return jnp.where(plus, 1.0, -1.0) * (1.0 if s < 2 else -1.0)

    def rim_sign(w):
        return jnp.where(w < 2, 1.0, -1.0) if not isinstance(w, int) else (1.0 if w < 2 else -1.0)

    loads[0].wait()
    near_plan = []
    for s in range(4):
        dx, dy = SHIFT[s]
        turn, flip = code(*place(-dx, -dy), s)
        near_plan.append((flip * 4 + wanted(s, turn), sign(s, turn)))

    def relay_plan(s, w, ax, ay):
        turn_a, flip_a = code(*place(ax, ay), s)
        turn_b, flip_b = code(*place(ax + SHIFT[s][0], ay + SHIFT[s][1]), w)
        return (flip_a ^ flip_b) * 4 + wanted(w, turn_b), sign(s, turn_a) * rim_sign(w)

    def relay_to(s, w):
        return relay_plan(s, w, -SHIFT[s][0] - SHIFT[w][0], -SHIFT[s][1] - SHIFT[w][1])

    diag_plan = [(relay_to(a, b), relay_to(b, a)) for a, b in DIAGONAL]
    far_plan = [relay_to(s, s) for s in range(4)]
    own_plan = [relay_to(s, opposite(s)) for s in range(4)]
    mine = [wanted(s, code(ix, iy, s)[0]) for s in range(4)]

    def relayed(t, s):
        found = own_relay[s]
        for k, (a, b) in enumerate(DIAGONAL):
            if s == a:
                found = jnp.where(mine[s] == b, diag_recv[t, k, :levels], found)
            if s == b:
                found = jnp.where(mine[s] == a, diag_recv[t, k, levels:], found)
        return jnp.where(mine[s] == s, far_recv[t, s], found)

    def send_rims(t, first=False):
        for s in range(4):
            for up, level in ((1, levels - 1), (0, 0)):
                level_send[t, up, 2 * s : 2 * s + 2] = p_strips[s, pl.ds(level, 2, stride=levels), :]
        if first:
            level_send[t, 1] = level_send[t, 1] + wu_rims[...] * (1.0 / B)

        @pl.when(has_above)
        def _():
            level_copy(t, 1).start()

        @pl.when(has_below)
        def _():
            level_copy(t, 0).start()

        strips = [p_strips[s] for s in range(4)]
        rims = []
        for s in range(4):
            turned = A * pltpu.roll(strips[s], levels, 0)
            rims.append(jnp.where(outer, w_strips[s] - rim_sign(s) * turned, turned))
        for s in range(4):
            table[s] = rims[s]
            table[4 + s] = jnp.take_along_axis(rims[s], last - strip_lane, axis=1)
        for k in range(4):
            for half in range(2):
                which, sgn = diag_plan[k][half]
                diag_send[t, k, half * levels : (half + 1) * levels] = sgn * table[which, levels:]
            diag_copy(t, k).start()
        for s in range(4):
            k, sgn = near_plan[s]
            rim = table[k]
            near_send[t, s] = jnp.where(outer, sgn * rim, rim)
            near_copy(t, s).start()
        for s in range(4):
            k, sgn = far_plan[s]
            far_send[t, s] = sgn * table[k, levels:]
            far_copy(t, s).start()
        for s in range(4):
            k, sgn = own_plan[s]
            own_relay[s] = sgn * table[k, levels:]

    def corners(s, low, high):
        found = jnp.zeros((2 * levels, tile), jnp.float32)
        for depth in range(2):
            start = depth if s < 2 else last - depth
            for e in range(2):
                for pair, end in ((low, e), (high, last - e)):
                    moved = pltpu.roll(pair[depth ^ e], (end - start) % tile, 1) if end != start else pair[depth ^ e]
                    here = (strip_lane == end) & (outer if depth == 0 else jnp.logical_not(outer))
                    found = jnp.where(here, moved, found)
        return found

    def next_strips(t):
        for s in range(4):
            near_copy(t, s).wait_recv()
        for k in range(4):
            diag_copy(t, k).wait_recv()
        for s in range(4):
            far_copy(t, s).wait_recv()

        @pl.when(has_above)
        def _():
            level_copy(t, 0).wait_recv()

        @pl.when(has_below)
        def _():
            level_copy(t, 1).wait_recv()

        zero = jnp.zeros((levels, tile), jnp.float32)
        ghosts = []
        for s in range(4):
            ghosts.append(near_recv[t, s] + jnp.concatenate([relayed(t, s), zero], axis=0))
        pairs = [(g, pltpu.roll(g, levels, 0)) for g in ghosts]
        for s in range(2):
            rim_change[s] = jnp.where(outer, pairs[s][1], -ghosts[s + 2])
        for s in range(4):
            low, high = (pairs[1], pairs[3]) if s % 2 == 0 else (pairs[0], pairs[2])
            across = jnp.zeros((2 * levels, tile), jnp.float32)
            for depth in range(2):
                below, above = level_recv[t, 1], level_recv[t, 0]
                k = 2 * s + depth
                across = jnp.where(strip_row == depth * levels, below[k : k + 1], across)
                across = across + jnp.where(strip_row == (depth + 1) * levels - 1, above[k : k + 1], 0.0)
            p_strips[s] = p_strips[s] + st_strips[s] * (
                A * (ghosts[s] + corners(s, low, high)) + (B * B) * across
            )
            w_strips[s] = jnp.where(outer, w_strips[s] + rim_sign(s) * pairs[s][1], 0.0)

    def give_copy(c, o):
        return pltpu.make_async_remote_copy(
            src_ref=payload[c].at[o],
            dst_ref=arrived[c].at[ix],
            send_sem=give_sem.at[c, o],
            recv_sem=take_sem.at[c, ix],
            device_id={"px": o},
            device_id_type=MESH,
        )

    def got(c, o):
        return pltpu.make_async_remote_copy(
            src_ref=payload[c].at[o],
            dst_ref=arrived[c].at[o],
            send_sem=give_sem.at[c, o],
            recv_sem=take_sem.at[c, o],
            device_id={"px": o},
            device_id_type=MESH,
        )

    w_strips[...] = jnp.zeros(w_strips.shape, jnp.float32)
    ghost_rows[...] = jnp.zeros((tile, tile), jnp.float32)

    wu_below[...] = jnp.zeros((tile, tile), jnp.float32)

    @pl.when(jnp.logical_not(has_below))
    def _():
        level_recv[:, 1] = jnp.zeros((SUBSTEPS, 8, tile), jnp.float32)

    @pl.when(jnp.logical_not(has_above))
    def _():
        level_recv[:, 0] = jnp.zeros((SUBSTEPS, 8, tile), jnp.float32)

    for load in loads[1:5]:
        load.wait()
    columns([wu[levels - 1]], [])
    for k, place_of in enumerate((0, 1, None, None, last, last - 1)):
        if place_of is not None:
            wu_rims[k : k + 1] = wu[levels - 1, place_of : place_of + 1, :]
    for k, place_of in ((2, 2), (3, 3), (6, 1), (7, 0)):
        wu_rims[k : k + 1] = flipped_cols[place_of : place_of + 1, :]
    take_strips()
    plane_send[0, 1] = p[levels - 1] + wu[levels - 1] * (1.0 / B)
    plane_send[0, 0] = p[0]
    pl.semaphore_wait(
        barrier, n_px - 1 + len(beside) + has_above.astype(jnp.int32) + has_below.astype(jnp.int32)
    )
    send_rims(0, True)

    @pl.when(has_above)
    def _():
        plane_copy(0, 1).start()

    @pl.when(has_below)
    def _():
        plane_copy(0, 0).start()

    for load in loads[5:]:
        load.wait()
    columns([st[j] for j in range(levels)], [])
    for s, (a, b) in ((0, (0, 1)), (2, (last, last - 1))):
        st_strips[s, :levels] = st[:, a, :]
        st_strips[s, levels:] = st[:, b, :]
    for s, (a, b) in ((1, (2, 3)), (3, (1, 0))):
        st_strips[s, :levels] = column(a)
        st_strips[s, levels:] = column(b)
    slot_count = payload_first.shape[2]
    top = levels - 1
    every = tuple(range(levels))
    stages = (
        (picked_early, ((0, 0, top),), [(wu, l) for l in every[:top]]),
        (picked_first, ((1, 0, levels),), [(we, l) for l in every]),
        (picked_second, ((3, 0, levels), (2, levels, levels + 1)), [(wn, l) for l in every] + [(wu, top)]),
        (picked_third, ((4, 0, levels),), [(p, l) for l in every]),
    )
    capacity = pick_hot.shape[1]
    packed = capacity < n_px * slot_count
    find_slots(n_px, slot_count, packed, owner, source, weight, slot_source, slot_weight)
    steps = (capacity // LANES - 1).bit_length()
    if packed:
        filled = [
            jnp.sum(jnp.sum((owner[...] == o).astype(jnp.int32), axis=0, keepdims=True), axis=1, keepdims=True)
            for o in range(n_px)
        ]

    def part_of(o, found, low, high):
        if not packed:
            return found[low:high, pl.ds(pl.multiple_of(o * slot_count, LANES), slot_count)]
        start, count = jnp.zeros((1, 1), jnp.int32), jnp.zeros((1, 1), jnp.int32)
        for k, n in enumerate(filled):
            start = start + jnp.where(k < o, (n + (LANES - 1)) >> 7, 0)
            count = count + jnp.where(k == o, n, 0)
        part = found[low:high, :]
        for k in reversed(range(steps)):
            width = slot_count + ((1 << k) - 1) * LANES
            part = jnp.where(
                ((start >> k) & 1) == 1, part[:, LANES << k : (LANES << k) + width], part[:, :width]
            )
        return jnp.where(iota(part.shape, 1) < count, part, 0.0)

    def ahead(d):
        return lax.rem(ix + d + 1, n_px)

    def choose(k):
        found, _, planes = stages[k]
        first = sum(len(stage[2]) for stage in stages[:k])
        for n, (field, l) in enumerate(planes):
            split_plane(split, field[l], first + n)
        pick(first, split, pick_hot, pick_mask, found)

    def add_rims(k):
        found = stages[k][0]

        def step(b, carry):
            at = pl.ds(pl.multiple_of(b * LANES, LANES), LANES)
            src = jnp.broadcast_to(slot_source[pl.ds(b, 1), :], (2 * levels, LANES))
            across, along = (src >> 7, src & last) if k == 1 else (src & last, src >> 7)
            change = jnp.take_along_axis(rim_change[k - 1], along, axis=1) * slot_weight[pl.ds(b, 1), :]
            change = jnp.where(across == jnp.where(outer, 0, last), change, 0.0)
            found[:, at] = found[:, at] + (change[:levels] + change[levels:])
            return carry

        lax.fori_loop(0, capacity // LANES, step, 0, unroll=4)

    def hand_over(k):
        found, parts, planes = stages[k]

        def lay_out(o):
            whole = part_of(o, found, 0, len(planes))
            for c, low, high in parts:
                payload[c][o] = whole[low:high]

        def send(d, carry):
            lay_out(ahead(d))
            for c, _, _ in parts:
                give_copy(c, ahead(d)).start()
            return carry

        lax.fori_loop(0, n_px - 1, send, 0)
        lay_out(ix)

    def substep(t, carry):
        for j in range(levels - 1):
            wu[j] = wu[j] - B * (p[j + 1] - p[j])

        @pl.when(t == SUBSTEPS - 1)
        def _():
            choose(0)
            hand_over(0)

        for j in range(levels):
            we[j] = we[j] - A * d_rows(p[j])
            wn[j] = wn[j] - A * d_lanes(p[j])

        @pl.when(has_above)
        def _():
            wu[levels - 1] = wu[levels - 1] + B * p[levels - 1]

        @pl.when(jnp.logical_not(has_above))
        def _():
            wu[levels - 1] = jnp.zeros((tile, tile), jnp.float32)

        for j in range(1, levels):
            p[j] = p[j] - st[j] * (A * (d_rows(we[j]) + d_lanes(wn[j])) + B * (wu[j] - wu[j - 1]))

        @pl.when(has_below)
        def _():
            wu_below[...] = wu_below[...] - B * p[0]

        p[0] = p[0] - st[0] * (A * (d_rows(we[0]) + d_lanes(wn[0])) + B * (wu[0] - wu_below[...]))
        take_strips()

        @pl.when(t == 1)
        def _():
            pick_tables(slot_source, slot_weight, pick_hot, pick_mask)
            if packed:
                for found, _, planes in stages:
                    found[:, capacity:] = jnp.zeros((len(planes), found.shape[1] - capacity), jnp.float32)

        @pl.when(t == 2)
        def _():
            land_tables(cell, land_hot)
            total[...] = jnp.zeros(total.shape, jnp.float32)

        @pl.when(t == SUBSTEPS - 1)
        def _():
            for k in range(1, EARLY):
                choose(k)

        next_strips(t)

        @pl.when(t == SUBSTEPS - 1)
        def _():
            for k in range(1, EARLY):
                add_rims(k)
                hand_over(k)

        @pl.when(t < SUBSTEPS - 1)
        def _():
            send_rims(t + 1)

        @pl.when(has_above)
        def _():
            plane_copy(t, 0).wait_recv()
            wu[levels - 1] = wu[levels - 1] - B * plane_recv[t, 0]
            p[levels - 1] = p[levels - 1] + (B * B) * (st[levels - 1] * plane_recv[t, 0])

        @pl.when(has_below)
        def _():
            plane_copy(t, 1).wait_recv()
            wu_below[...] = wu_below[...] + B * plane_recv[t, 1]
            p[0] = p[0] + (B * B) * (st[0] * plane_recv[t, 1])

        for s, (a, b) in ((0, (0, 1)), (2, (last, last - 1))):
            p[:, a, :] = p_strips[s, :levels]
            p[:, b, :] = p_strips[s, levels:]
            we[:, a, :] = w_strips[s, :levels]
        for k, (s, half) in enumerate(((3, 1), (3, 0), (1, 0), (1, 1))):
            ghost_rows[pl.ds(k, levels, stride=4), :] = p_strips[s, half * levels : (half + 1) * levels]
        for k, s in enumerate((3, 1)):
            ghost_rows[pl.ds(4 * levels + k, levels, stride=2), :] = w_strips[s, :levels]
        turned = ghost_rows[...].T
        rim = (lane == 0) | (lane == last)
        band = (lane <= 1) | (lane >= last - 1)

        def put_sides(j):
            p[j] = jnp.where(band, pltpu.roll(turned, (tile - 4 * j - 2) % tile, 1), p[j])

        put_sides(levels - 1)

        @pl.when((t < SUBSTEPS - 1) & has_above)
        def _():
            plane_send[t + 1, 1] = p[levels - 1]
            plane_copy(t + 1, 1).start()

        put_sides(0)

        @pl.when((t < SUBSTEPS - 1) & has_below)
        def _():
            plane_send[t + 1, 0] = p[0]
            plane_copy(t + 1, 0).start()

        for j in range(1, levels - 1):
            put_sides(j)
        for j in range(levels):
            wn[j] = jnp.where(rim, pltpu.roll(turned, (tile - 4 * levels - 2 * j - 1) % tile, 1), wn[j])

        return carry

    lax.fori_loop(0, SUBSTEPS, substep, 0)

    for k in range(EARLY, len(stages)):
        choose(k)
        hand_over(k)

    groups = latlon.shape[2] // BLOCK
    sums = (((1, 2), (1, 3)), ((3, 0), (0, 2, 4)))

    for n, (_, parts) in enumerate(sums):
        land(n, [payload[c][ix] for c in parts], cell, land_hot, ix, total)

    for n, (names, parts) in enumerate(sums):

        def bring_in(d, carry):
            o = lax.rem(ix + n_px - d - 1, n_px)
            for c in parts:
                got(c, o).wait_recv()
            land(n, [arrived[c][o] for c in parts], cell, land_hot, o, total)
            return carry

        lax.fori_loop(0, n_px - 1, bring_in, 0)
        for g in range(groups):
            rows = len(names) * levels
            high, low = g * rows, (groups + g) * rows
            both = total[n, high : high + rows] + total[n, low : low + rows]
            for k, q in enumerate(names):
                latlon[q, :, g * BLOCK : (g + 1) * BLOCK] = both[k * levels : (k + 1) * levels]

    def drain(t, carry):
        for s in range(4):
            near_copy(t, s).wait_send()
            diag_copy(t, s).wait_send()
            far_copy(t, s).wait_send()

        @pl.when(has_above)
        def _():
            level_copy(t, 1).wait_send()
            plane_copy(t, 1).wait_send()

        @pl.when(has_below)
        def _():
            level_copy(t, 0).wait_send()
            plane_copy(t, 0).wait_send()

        return carry

    lax.fori_loop(0, SUBSTEPS, drain, 0)

    def sent(d, carry):
        for c in range(len(payload)):
            give_copy(c, ahead(d)).wait_send()
        return carry

    lax.fori_loop(0, n_px - 1, sent, 0)


def find_slots(owner_count, slot_count, packed, owner, source, weight, slot_source, slot_weight):
    rows = owner.shape[0]
    slot_rows = slot_source.shape[0]
    names = owner[...]
    up_to = (iota((LANES, LANES), 0) <= iota((LANES, LANES), 1)).astype(jnp.bfloat16)
    ones = jnp.ones((LANES, LANES), jnp.bfloat16)
    before = (iota((rows, rows), 0) > iota((rows, rows), 1)).astype(jnp.bfloat16)

    def count(o, carry):
        place, start = carry
        named = names == o
        hot = named.astype(jnp.float32).astype(jnp.bfloat16)
        within = jnp.dot(hot, up_to, preferred_element_type=jnp.float32)
        total = jnp.dot(hot, ones, preferred_element_type=jnp.float32)
        earlier = jnp.dot(before, total.astype(jnp.bfloat16), preferred_element_type=jnp.float32)
        place = jnp.where(named, within + earlier - 1.0 + start, place)
        if packed:
            filled = jnp.sum(total, axis=0, keepdims=True)
            start = start + jnp.floor((filled + (LANES - 1.0)) / LANES) * LANES
        else:
            start = start + float(slot_count)
        return place, start

    zero = jnp.zeros(names.shape, jnp.float32)
    place, _ = lax.fori_loop(0, owner_count, count, (zero, jnp.zeros((1, LANES), jnp.float32)))
    slot = place.astype(jnp.int32)
    slot_high, slot_low = slot >> 7, slot & (LANES - 1)
    src = source[...]
    w = weight[...]
    w1 = w.astype(jnp.bfloat16).astype(jnp.float32)
    w2 = (w - w1).astype(jnp.bfloat16).astype(jnp.float32)
    w3 = w - w1 - w2
    pieces = [(src >> 7).astype(jnp.float32), (src & (LANES - 1)).astype(jnp.float32), w1, w2, w3]
    high_place, low_place = iota((slot_rows, LANES), 0), iota((LANES, LANES), 0)
    total = jnp.zeros((len(pieces) * slot_rows, LANES), jnp.float32)
    for r in range(rows):
        here = high_place == slot_high[r : r + 1]
        left = jnp.concatenate([jnp.where(here, piece[r : r + 1], 0.0) for piece in pieces], axis=0)
        right = jnp.where(low_place == slot_low[r : r + 1], 1.0, 0.0)
        total += dot_nt(left.astype(jnp.bfloat16), right.astype(jnp.bfloat16))
    part = [total[k * slot_rows : (k + 1) * slot_rows] for k in range(len(pieces))]
    slot_source[...] = (part[0] * LANES + part[1]).astype(jnp.int32)
    slot_weight[...] = part[2] + part[3] + part[4]


def split_plane(split, plane, r):
    tile = plane.shape[0]
    half = tile // 2
    h, d = parts2(plane.T)
    for k, part in enumerate((h[:half], h[half:], d[:half], d[half:])):
        split[r * half : (r + 1) * half, k * tile : (k + 1) * tile] = part


def joined(ref, row, pieces):
    return jnp.concatenate([ref[pl.ds(row + k, 1), :] for k in range(pieces)], axis=1)


def pick_tables(slot_source, slot_weight, pick_hot, pick_mask):
    lines, capacity = pick_hot.shape
    tile, half = lines // 2, pick_mask.shape[0]
    pieces = BLOCK // LANES

    def step(b, carry):
        at = pl.ds(pl.multiple_of(b * BLOCK, BLOCK), BLOCK)
        src, w = joined(slot_source, b * pieces, pieces), joined(slot_weight, b * pieces, pieces)
        x, y = src >> 7, src & (tile - 1)
        line = x + jnp.where(y >= half, tile, 0)
        pick_hot[:, at] = jnp.where(iota((lines, BLOCK), 0) == line, 1.0, 0.0).astype(jnp.bfloat16)
        pick_mask[:, at] = jnp.where(iota((half, BLOCK), 0) == (y & (half - 1)), w, 0.0)
        return carry

    lax.fori_loop(0, capacity // BLOCK, step, 0)


def pick(first, split, pick_hot, pick_mask, found):
    rows = found.shape[0]
    half, capacity = pick_mask.shape
    lines = slice(first * half, (first + rows) * half)
    width = 2 * BLOCK if capacity % (2 * BLOCK) == 0 else BLOCK
    steps = capacity // width

    def step(b, carry):
        at = pl.ds(pl.multiple_of(b * width, width), width)
        hot = pick_hot[:, at]
        line = jnp.dot(
            split[lines, :], jnp.concatenate([hot, hot], axis=0), preferred_element_type=jnp.float32
        )
        found[:, at] = jnp.sum(line.reshape(rows, half, width) * pick_mask[:, at][None], axis=1)
        return carry

    lax.fori_loop(0, steps, step, 0, unroll=steps if steps < 12 else 4)


def land_tables(cell, land_hot):
    owner_count, _, slot_count = land_hot.shape
    pieces = slot_count // LANES

    def step(o, carry):
        c = joined(cell, o * pieces, pieces)
        hot = jnp.where(iota((BLOCK, slot_count), 0) == (c & (BLOCK - 1)), 1.0, 0.0)
        land_hot[o] = hot.astype(jnp.bfloat16)
        return carry

    lax.fori_loop(0, owner_count, step, 0)


def land(q, parts, cell, land_hot, o, total):
    values = parts[0] if len(parts) == 1 else jnp.concatenate(parts, axis=0)
    rows, slot_count = values.shape
    groups = total.shape[1] // (2 * rows)
    pieces = slot_count // LANES
    group = joined(cell, o * pieces, pieces) >> 8
    h = values.astype(jnp.bfloat16).astype(jnp.float32)
    spread = [jnp.where(group == g, h, 0.0) for g in range(groups)]
    spread += [jnp.where(group == g, values - h, 0.0) for g in range(groups)]
    total[q] += dot_nt(jnp.concatenate(spread, axis=0).astype(jnp.bfloat16), land_hot[o])


def per_device(
    sizes,
    pressure,
    wind_east,
    wind_north,
    wind_up,
    stiffness,
    edge_table,
    remap_source,
    remap_weight,
    remap_owner,
    latlon_cell,
):
    levels, tile, _ = pressure.shape
    owner_count = sizes[0]
    slots = latlon_cell.shape[0]
    slot_count = slots // owner_count
    cell_count = tile * tile // 8
    count = 4 * levels
    entries = remap_source.shape[0]
    rows = entries // LANES
    capacity = -(-(entries + (owner_count - 1) * (LANES - 1)) // BLOCK) * BLOCK
    capacity = min(capacity, slots)
    room = capacity
    if capacity < slots:
        room = slot_count + ((2 << (capacity // LANES - 1).bit_length() - 1) - 1) * LANES + LANES
        room = max(room, capacity)
    slot_rows = -(-capacity // (8 * LANES)) * 8
    part_rows = (levels - 1, levels, 1, levels, levels)
    f32, i32 = jnp.float32, jnp.int32
    n = SUBSTEPS
    field = pltpu.VMEM(pressure.shape, f32)
    plane = pltpu.VMEM((tile, tile), f32)
    dma = pltpu.SemaphoreType.DMA
    in_vmem = pl.BlockSpec(memory_space=pltpu.VMEM)
    results = pl.pallas_call(
        functools.partial(whole_kernel, sizes),
        out_shape=[
            pltpu.VMEM(pressure.shape, f32),
            pltpu.VMEM((4, levels, cell_count), f32),
        ],
        in_specs=[pl.BlockSpec(memory_space=pl.ANY)] * 10,
        out_specs=[in_vmem] * 2,
        scratch_shapes=[
            pltpu.SMEM(edge_table.shape, i32),
            field,
            field,
            field,
            field,
            pltpu.VMEM((rows, LANES), i32),
            pltpu.VMEM((rows, LANES), i32),
            pltpu.VMEM((rows, LANES), f32),
            pltpu.VMEM((slots // LANES, LANES), i32),
            pltpu.VMEM((8, 2 * levels, tile), f32),
            pltpu.VMEM((n, 4, 2 * levels, tile), f32),
            pltpu.VMEM((n, 4, 2 * levels, tile), f32),
            pltpu.VMEM((n, 4, 2 * levels, tile), f32),
            pltpu.VMEM((n, 4, 2 * levels, tile), f32),
            pltpu.VMEM((n, 4, levels, tile), f32),
            pltpu.VMEM((n, 4, levels, tile), f32),
            pltpu.VMEM((4, levels, tile), f32),
            pltpu.VMEM((n, 2, 8, tile), f32),
            pltpu.VMEM((n, 2, 8, tile), f32),
            pltpu.VMEM((n, 2, tile, tile), f32),
            pltpu.VMEM((n, 2, tile, tile), f32),
            plane,
            plane,
            plane,
            pltpu.VMEM((4, 2 * levels, tile), f32),
            pltpu.VMEM((4, 2 * levels, tile), f32),
            pltpu.VMEM((4, 2 * levels, tile), f32),
            pltpu.VMEM((8, tile), f32),
            pltpu.VMEM((2, 2 * levels, tile), f32),
            pltpu.VMEM((slot_rows, LANES), i32),
            pltpu.VMEM((slot_rows, LANES), f32),
            pltpu.VMEM((2 * tile, capacity), jnp.bfloat16),
            pltpu.VMEM((tile // 2, capacity), f32),
            pltpu.VMEM((owner_count, BLOCK, slot_count), jnp.bfloat16),
            pltpu.VMEM((count * tile // 2, 4 * tile), jnp.bfloat16),
            *(pltpu.VMEM((n_rows, room), f32) for n_rows in (levels - 1, levels, levels + 1, levels)),
            *(pltpu.VMEM((owner_count, n_rows, slot_count), f32) for n_rows in part_rows),
            *(pltpu.VMEM((owner_count, n_rows, slot_count), f32) for n_rows in part_rows),
            pltpu.VMEM((2, 4 * levels * (cell_count // BLOCK), BLOCK), f32),
            dma((10,)),
            dma((2, n, 4)),
            dma((2, n, 4)),
            dma((2, n, 4)),
            dma((2, n, 2)),
            dma((2, n, 2)),
            dma((len(part_rows), owner_count)),
            dma((len(part_rows), owner_count)),
        ],
        compiler_params=pltpu.CompilerParams(
            collective_id=0, has_side_effects=True, vmem_limit_bytes=60 * 2**20
        ),
    )(
        edge_table,
        pressure,
        wind_east,
        wind_north,
        wind_up,
        stiffness,
        remap_owner.reshape(rows, LANES),
        remap_source.reshape(rows, LANES),
        remap_weight.reshape(rows, LANES),
        latlon_cell.reshape(slots // LANES, LANES),
    )
    anywhere = pl.BlockSpec(memory_space=pl.ANY)
    return pl.pallas_call(
        pass_on,
        out_shape=[jax.ShapeDtypeStruct(r.shape, f32) for r in results],
        in_specs=[in_vmem] * 2,
        out_specs=[anywhere] * 2,
        scratch_shapes=[dma((2,))],
    )(*(pltpu.with_memory_space_constraint(r, pltpu.VMEM) for r in results))


def pass_on(p, latlon, p_out, latlon_out, sems):
    copies = [
        pltpu.make_async_copy(src, dst, sems.at[k]) for k, (src, dst) in enumerate(((p, p_out), (latlon, latlon_out)))
    ]
    for copy in copies:
        copy.start()
    for copy in copies:
        copy.wait()


def solution(mesh):
    field = P("lev", "px", "py")
    entries = P(("px", "py"))
    sizes = (mesh.shape["px"], mesh.shape["py"], mesh.shape["lev"])
    return jax.shard_map(
        functools.partial(per_device, sizes),
        mesh=mesh,
        in_specs=(field,) * 5 + (P(), entries, entries, P(("px", "py"), None), entries),
        out_specs=(field, P(None, "lev", ("px", "py"))),
        check_vma=False,
    )
```
